128 devices in a mesh: section: 2 (over y_lo), dp: 4 (over y_hi, core), expert: 16 (over z, x).
Axes of the slice: x: 4, y: 4 (y_hi: 2, y_lo: 2; y = y_hi * 2 + y_lo), z: 4, core: 2. Of those that a mesh axis runs over, the one named last changes fastest.
Arguments:
- inputs: bfloat16 [2, 8192, 1024], P(None, ('dp', 'expert')), may hold values from -6 to 6
- cotangent: bfloat16 [2, 8192, 1024], P(None, ('dp', 'expert')), may hold values from -6 to 6
- offsets: int32 [2, 8192], P(None, ('dp', 'expert')), may hold values from 0 to 2047, as said below
- routes: int32 [2, 2, 8192, 8], P('section', None, ('dp', 'expert')), may hold values from 0 to 31, all different within a row; in each aligned block of 128 rows (0 to 127, 128 to 255, ..., all dimensions but the last counted through in order) at most 33 rows name the same one
- w_query: bfloat16 [2, 1024, 1024], P('section'), may hold values from -0.1875 to 0.1875
- w_key: bfloat16 [2, 1024, 512], P('section'), may hold values from -0.1875 to 0.1875
- w_value: bfloat16 [2, 1024, 512], P('section'), may hold values from -0.1875 to 0.1875
- w_out: bfloat16 [2, 1024, 1024], P('section'), may hold values from -1 to 1
- norm_attn: bfloat16 [2, 1024], P('section'), may hold values from 0.5 to 1.5
- norm_moe: bfloat16 [2, 1024], P('section'), may hold values from 0.5 to 1.5
- w_router: bfloat16 [2, 1024, 32], P('section'), may hold values from -0.09375 to 0.09375
- w_gate: bfloat16 [2, 32, 1024, 512], P('section', 'expert', 'dp'), may hold values from -0.1875 to 0.1875
- w_up: bfloat16 [2, 32, 1024, 512], P('section', 'expert', 'dp'), may hold values from -0.1875 to 0.1875
- w_down: bfloat16 [2, 32, 1024, 512], P('section', 'expert', 'dp'), may hold values from -0.75 to 0.75
Outputs:
- acts: bfloat16 [2, 2, 8192, 1024], P('section', None, ('dp', 'expert'))
- in_grads: bfloat16 [2, 2, 8192, 1024], P('section', None, ('dp', 'expert'))
- grad_query: float32 [2, 1024, 1024], P('section')
- grad_key: float32 [2, 1024, 512], P('section')
- grad_value: float32 [2, 1024, 512], P('section')
- grad_out: float32 [2, 1024, 1024], P('section')
- grad_norm_attn: float32 [2, 1024], P('section')
- grad_norm_moe: float32 [2, 1024], P('section')
- grad_router: float32 [2, 1024, 32], P('section')
- grad_gate: float32 [2, 32, 1024, 512], P('section', 'expert', 'dp')
- grad_up: float32 [2, 32, 1024, 512], P('section', 'expert', 'dp')
- grad_down: float32 [2, 32, 1024, 512], P('section', 'expert', 'dp')
The draws below stay inside these ranges and needn't reach their ends.
Inputs may be any that keep to these rules, and one draw needn't show every extreme that they name: `offsets`: A token's value equals the previous token's or its own index within its group of 2048 consecutive tokens, and the first token of a group has 0; every group holds a sequence that begins within its first 128 tokens and ends within its last 128. `routes`: in each aligned block of 128 rows (one device's tokens of one layer and micro-batch), no expert is named by more than 33 rows.
All inputs are finite; a program needn't handle non-finite values.
Results may differ from the reference program's by a relative error of at most 0.025.
Values may be sent and summed in bfloat16 or wider, within the bound.
A program may use at most 320 MiB of HBM per device.

```python
import math
import jax
import jax.numpy as jnp
import numpy as np
from jax import lax

D = 1024
HEADS = 16
KV_HEADS = 8
HEAD = 64
FFE = 512
EXPERTS = 32
TOP = 8
MICRO = 2
LAYERS = 2
TOK_DEV = 128
GROUP = 2048
TOKENS = 8192
CAP = 33
N_DP = 4


def draw_offsets(key, part):
    key = jax.random.fold_in(key, 11)
    groups = TOKENS // GROUP
    keys = jax.random.split(key, 4)
    shape = (MICRO, groups, 1)
    start = jax.random.randint(keys[0], shape, 1, TOK_DEV)
    finish = jax.random.randint(keys[1], shape, GROUP - TOK_DEV + 1, GROUP)
    before = jax.random.randint(keys[2], shape, 0, start)
    after = jax.random.randint(keys[3], shape, finish, GROUP)
    group_ids = jnp.arange(groups, dtype=jnp.int32)[None, :, None]
    after = jnp.where(group_ids == 0, GROUP - 1, after)
    index = jnp.arange(GROUP, dtype=jnp.int32)[None, None, :]
    later = jnp.where(index < after, finish, after)
    middle = jnp.where(index < finish, start, later)
    early = jnp.where(index < start, before, middle)
    values = jnp.where(index < before, 0, early)
    return values.reshape(MICRO, TOKENS).astype(jnp.int32)


def shard_levels(key, dims, shards, smallest, largest):
    def one(dim, parts):
        steps = jax.random.uniform(jax.random.fold_in(jax.random.fold_in(key, 6), dim), (parts,), jnp.float32, smallest / len(shards), largest / len(shards))
        return jnp.repeat(jnp.exp(steps), dims[dim] // parts).reshape((-1,) + (1,) * (len(dims) - dim - 1))

    factor_of = one(*shards[0])
    for cut in shards[1:]:
        factor_of = factor_of * one(*cut)
    return factor_of


def assign_block(key, own, number, rows, amount, top, reach, skew):
    ranking = jax.random.permutation(key, amount)
    crowded, common = shares(amount, rows * top, reach, skew, True), shares(amount, rows * top, reach, skew, False)
    places = jnp.arange(amount)

    def named(sizes, offset_by):
        used = int((sizes > 0).sum())
        fixed = max(1, used // 4)
        passed = fixed + (places - fixed + offset_by * (used - fixed)) % max(1, amount - fixed)
        return jnp.zeros((amount,), jnp.int32).at[ranking[jnp.where(places < fixed, places, passed)]].set(jnp.asarray(sizes, jnp.int32))

    sizes = jnp.where(number % 4 == 0, named(crowded, number // 4), named(common, number - number // 4 - 1))
    mixed = jax.random.permutation(jax.random.fold_in(own, 3), amount)
    giver, receiver = mixed[0:amount // 2 * 2:2], mixed[1:amount // 2 * 2:2]
    margin = jnp.minimum(sizes[giver] - 1, reach - sizes[receiver]) // 2
    margin = jnp.where((giver == ranking[0]) | (receiver == ranking[0]) | (sizes[receiver] == 0), 0, jnp.maximum(margin, 0))
    passed = jax.random.randint(jax.random.fold_in(own, 4), (amount // 2,), 0, 1 << 20) % (margin + 1)
    sizes = sizes.at[giver].add(-passed).at[receiver].add(passed)
    labels = jnp.searchsorted(jnp.cumsum(sizes), jnp.arange(rows * top), side="right").astype(jnp.int32)
    grid = labels.reshape(top, rows).T
    grid = grid[jax.random.permutation(jax.random.fold_in(own, 1), rows)]
    offset_by = jax.random.randint(jax.random.fold_in(own, 2), (rows, 1), 0, top)
    return jnp.take_along_axis(grid, (jnp.arange(top)[None, :] + offset_by) % top, axis=1)


def shares(number_of, total, limit, lean, full):
    weights = [(1 << 20) // math.isqrt(rank ** lean) + 1 for rank in range(1, number_of + 1)]
    largest = limit if full else min(limit, max(-(-total // number_of), total * weights[0] // sum(weights)))
    least = 1 if total - largest >= number_of - 1 else 0
    given, surplus = [largest] + [least] * (number_of - 1), total - largest - least * (number_of - 1)
    while surplus > 0:
        free = [i for i in range(1, number_of) if given[i] < largest] or [i for i in range(1, number_of) if given[i] < limit]
        pool, left = sum([weights[i] for i in free]), surplus
        for i in free:
            more = min(limit - given[i], max(1, left * weights[i] // pool), surplus)
            given[i] = given[i] + more
            surplus = surplus - more
    return np.array(given)


def normal_values(stream_key, dims, spread, most, shards=(), kind=jnp.bfloat16):
    loudness = shard_levels(stream_key, dims, shards, -0.22, 0.18) if shards else 1.0
    drawn = jax.random.normal(stream_key, dims, jnp.float32) * spread * loudness
    return jnp.minimum(jnp.maximum(drawn, -most), most).astype(kind)


def setup_inputs(seed: int = 0) -> dict:
    seeds = jax.random.split(jax.random.key(seed), 15)
    inputs = normal_values(seeds[0], (MICRO, TOKENS, D), 1.0, 6.0, ((1, 64),))
    cotangent = normal_values(seeds[1], (MICRO, TOKENS, D), 1.0, 6.0, ((1, 64),))
    offsets = draw_offsets(jax.random.fold_in(seeds[14], 71), 0)
    routes_keys = jax.random.split(jax.random.fold_in(seeds[3], 1), LAYERS * MICRO * TOKENS // TOK_DEV)
    routes_turns = jax.random.permutation(jax.random.fold_in(seeds[3], 3), LAYERS * MICRO * TOKENS // TOK_DEV)
    routes = jax.vmap(lambda own, number: assign_block(jax.random.fold_in(seeds[3], 2), own, number, TOK_DEV, EXPERTS, TOP, CAP, 0))(routes_keys, routes_turns).reshape((LAYERS, MICRO, TOKENS, TOP))
    w_query = normal_values(seeds[4], (LAYERS, D, HEADS * HEAD), D ** -0.5, 0.1875, ((0, 2),))
    w_key = normal_values(seeds[5], (LAYERS, D, KV_HEADS * HEAD), D ** -0.5, 0.1875, ((0, 2),))
    w_value = normal_values(seeds[6], (LAYERS, D, KV_HEADS * HEAD), D ** -0.5, 0.1875, ((0, 2),))
    w_out = normal_values(seeds[7], (LAYERS, HEADS * HEAD, D), (D // 32) ** -0.5, 1.0, ((0, 2),))
    norm_attn = jnp.clip(1.0 + 0.1 * jax.random.normal(seeds[8], (LAYERS, D), jnp.float32), 0.5, 1.5).astype(jnp.bfloat16)
    norm_moe = jnp.clip(1.0 + 0.1 * jax.random.normal(seeds[9], (LAYERS, D), jnp.float32), 0.5, 1.5).astype(jnp.bfloat16)
    w_router = normal_values(seeds[10], (LAYERS, D, EXPERTS), (4 * D) ** -0.5, 0.09375, ((0, 2),))
    w_gate = normal_values(seeds[11], (LAYERS, EXPERTS, D, FFE), D ** -0.5, 0.1875, ((0, 2), (1, 16), (2, 4)))
    w_up = normal_values(seeds[12], (LAYERS, EXPERTS, D, FFE), D ** -0.5, 0.1875, ((0, 2), (1, 16), (2, 4)))
    w_down = normal_values(seeds[13], (LAYERS, EXPERTS, D, FFE), (FFE // 8) ** -0.5, 0.75, ((0, 2), (1, 16), (2, 4)))
    return dict(inputs=inputs, cotangent=cotangent, offsets=offsets, routes=routes, w_query=w_query, w_key=w_key, w_value=w_value, w_out=w_out, norm_attn=norm_attn, norm_moe=norm_moe, w_router=w_router, w_gate=w_gate, w_up=w_up, w_down=w_down)


norm_eps = 1e-06
masked_score = -1e+30
rope_base = 10000.0
highest = lax.Precision.HIGHEST

@jax.custom_vjp
def low(v):
    return lax.optimization_barrier(v.astype(jnp.bfloat16)).astype(jnp.float32)

@jax.custom_vjp
def low_back(v):
    return v

def low_keep(v):
    return (low(v), None)

def low_pass(kept, grad):
    return (grad,)

def back_keep(v):
    return (v, None)

def back_low(kept, grad):
    return (low(grad),)
low.defvjp(low_keep, low_pass)
low_back.defvjp(back_keep, back_low)

def matmul(left, right):
    return jnp.dot(left, right, precision=highest, preferred_element_type=jnp.float32)

def rms_scaled(values, gain):
    return values * lax.rsqrt(lax.optimization_barrier(jnp.mean(values * values, axis=-1, keepdims=True)) + norm_eps) * gain

def rotate_half(values):
    middle = values.shape[-1] // 2
    return jnp.concatenate([-values[..., middle:], values[..., :middle]], axis=-1)

def rotate(values, positions):
    steps_half = jnp.arange(HEAD // 2, dtype=jnp.float32) * 2.0 / HEAD
    frequency = rope_base ** (-steps_half)
    angles = positions.astype(jnp.float32)[:, None] * frequency[None, :]
    angles = jnp.concatenate([angles, angles], axis=-1)
    return values * jnp.cos(angles)[:, None, :] + rotate_half(values) * jnp.sin(angles)[:, None, :]

def attend(items):
    queries, keys, values, seq_offsets = items
    scores = low_back(jnp.einsum('tkgd,skd->kgts', queries, keys, precision=highest) * 0.125)
    index = jnp.arange(GROUP, dtype=jnp.int32)
    visible = (index[None, :] <= index[:, None]) & (index[None, :] >= seq_offsets[:, None])
    scores = jnp.where(visible, scores, masked_score)
    probs = low(jax.nn.softmax(scores, axis=-1))
    return jnp.einsum('kgts,skd->tkgd', probs, values, precision=highest)

def slot_table(route_ids):
    devices_all = TOKENS // TOK_DEV
    pairs_dev = TOK_DEV * TOP
    flat_routes = route_ids.reshape(devices_all, pairs_dev)
    expert_hits = (flat_routes[:, :, None] == jnp.arange(EXPERTS, dtype=jnp.int32)[None, None, :]).astype(jnp.int32)
    slot_rank = lax.optimization_barrier(jnp.sum((jnp.cumsum(expert_hits, axis=1) - 1) * expert_hits, axis=2))
    device_ids = jnp.arange(devices_all, dtype=jnp.int32)[:, None]
    position = device_ids * CAP + slot_rank
    pair_ids = jnp.arange(TOKENS * TOP, dtype=jnp.int32).reshape(devices_all, pairs_dev)
    table = jnp.full((EXPERTS, devices_all * CAP), TOKENS * TOP, jnp.int32)
    return table.at[flat_routes.reshape(-1), position.reshape(-1)].set(pair_ids.reshape(-1))

def layer(params, layer_input, seq_offsets, table, route_ids):
    w_query, w_key, w_value, w_out, gain_attn, gain_moe, w_router, w_gate, w_up, w_down = params
    share = HEADS // KV_HEADS
    attn_in = low(rms_scaled(layer_input, gain_attn))
    positions = jnp.arange(TOKENS, dtype=jnp.int32) % GROUP - seq_offsets
    query_lin = low_back(matmul(attn_in, w_query)).reshape(TOKENS, HEADS, HEAD)
    key_lin = low_back(matmul(attn_in, w_key)).reshape(TOKENS, KV_HEADS, HEAD)
    value_new = low(low_back(matmul(attn_in, w_value)))
    query_rot = low(rotate(query_lin, positions)).reshape(N_DP, GROUP, KV_HEADS, share, HEAD)
    key_rot = low(rotate(key_lin, positions)).reshape(N_DP, GROUP, KV_HEADS, HEAD)
    value_grid = value_new.reshape(N_DP, GROUP, KV_HEADS, HEAD)
    attended = lax.map(jax.checkpoint(attend), (query_rot, key_rot, value_grid, seq_offsets.reshape(N_DP, GROUP)))
    attended = low_back(low(attended.reshape(TOKENS, HEADS * HEAD)))
    hidden = layer_input + low_back(matmul(attended, w_out))
    moe_in = low(rms_scaled(hidden, gain_moe))
    logits = low_back(matmul(moe_in, w_router))
    gates = jax.nn.softmax(jnp.take_along_axis(logits, route_ids, axis=1), axis=-1)
    padded_in = jnp.concatenate([moe_in, jnp.zeros((1, D), jnp.float32)], axis=0)
    padded_gates = jnp.concatenate([gates.reshape(-1), jnp.zeros((1,), jnp.float32)], axis=0)

    def expert_step(mixture, item):
        gate_weight, up_weight, down_weight, slots = item
        token_of = slots // TOP
        expert_rows = low_back(padded_in[token_of])
        gate_lin = low_back(matmul(expert_rows, gate_weight))
        up_lin = low_back(matmul(expert_rows, up_weight))
        inner = low(jax.nn.silu(gate_lin) * up_lin)
        produced = low_back(low(jnp.einsum('rf,df->rd', inner, down_weight, precision=highest)))
        mixture = mixture.at[token_of].add(padded_gates[slots][:, None] * produced)
        return (mixture, None)
    mixture, unused = lax.scan(jax.checkpoint(expert_step), jnp.zeros((TOKENS + 1, D), jnp.float32), (w_gate, w_up, w_down, table))
    return hidden + mixture[:TOKENS]

def reference(inputs, cotangent, offsets, routes, w_query, w_key, w_value, w_out, norm_attn, norm_moe, w_router, w_gate, w_up, w_down):
    params = tuple((weight.astype(jnp.float32) for weight in (w_query, w_key, w_value, w_out, norm_attn, norm_moe, w_router, w_gate, w_up, w_down)))
    start = inputs.astype(jnp.float32)
    probe = jnp.zeros((MICRO, TOKENS, D), jnp.float32)
    tables = [[slot_table(routes[layer_index, batch_index]) for batch_index in range(MICRO)] for layer_index in range(2)]

    def forward(weights, layer_input, probe_in):
        mids, finals = ([], [])
        for batch_index in range(MICRO):
            first_out = layer(tuple((weight[0] for weight in weights)), layer_input[batch_index], offsets[batch_index], tables[0][batch_index], routes[0, batch_index])
            middle = low_back(low(first_out)) + probe_in[batch_index]
            second_out = layer(tuple((weight[1] for weight in weights)), middle, offsets[batch_index], tables[1][batch_index], routes[1, batch_index])
            mids.append(middle)
            finals.append(second_out)
        return (jnp.stack(finals), jnp.stack(mids))
    finals, vjp_fn, mids = jax.vjp(forward, params, start, probe, has_aux=True)
    param_grads, input_grad, middle_grad = vjp_fn(cotangent.astype(jnp.float32))
    acts = jnp.stack([mids, finals]).astype(jnp.bfloat16)
    in_grads = jnp.stack([input_grad, middle_grad]).astype(jnp.bfloat16)
    grad_query, grad_key, grad_value, grad_out, grad_norm_attn, grad_norm_moe, grad_router, grad_gate, grad_up, grad_down = param_grads
    return (acts, in_grads, grad_query, grad_key, grad_value, grad_out, grad_norm_attn, grad_norm_moe, grad_router, grad_gate, grad_up, grad_down)
```

```python
import jax
import jax.numpy as jnp
from jax import lax
from jax.experimental import pallas as pl
from jax.experimental.pallas import tpu as pltpu

from jax.sharding import PartitionSpec as P

HEAD = 64
MESH = pl.DeviceIdType.MESH
bf16 = jnp.bfloat16
f32 = jnp.float32
norm_eps = 1e-06
masked_score = -1e30
rope_base = 10000.0


def ring_places():
    me = lax.axis_index("expert")
    z, x = lax.div(me, 4), lax.rem(me, 4)
    xr, xl = lax.rem(x + 1, 4), lax.rem(x + 3, 4)
    zr, zl = lax.rem(z + 1, 4), lax.rem(z + 3, 4)
    near = (z * 4 + xr, z * 4 + xl, zr * 4 + x, zl * 4 + x)
    return z, x, xr, xl, zr, zl, near


def greet(near):
    barrier = pltpu.get_barrier_semaphore()
    for other in near:
        pl.semaphore_signal(barrier, inc=1, device_id={"expert": other}, device_id_type=MESH)
    pl.semaphore_wait(barrier, 4)


def gather_kernel(x_ref, out_ref, send, recv, own_sem):
    z, x, xr, xl, zr, zl, (dxr, dxl, dzr, dzl) = ring_places()
    rows = x_ref.shape[0]
    half, quarter = rows // 2, rows // 4
    own = pltpu.make_async_copy(x_ref, out_ref.at[z, x], own_sem)
    own.start()
    greet((dxr, dxl, dzr, dzl))

    def copy(i, src, dst, to):
        c = pltpu.make_async_remote_copy(
            src_ref=src, dst_ref=dst, send_sem=send.at[i], recv_sem=recv.at[i],
            device_id={"expert": to}, device_id_type=MESH)
        c.start()
        return c

    A, B = pl.ds(0, half), pl.ds(half, half)
    A0, A1 = pl.ds(0, quarter), pl.ds(quarter, quarter)
    B0, B1 = pl.ds(half, quarter), pl.ds(half + quarter, quarter)
    a_r = copy(0, x_ref.at[A], out_ref.at[z, x, A], dxr)
    a_l = copy(1, x_ref.at[A], out_ref.at[z, x, A], dxl)
    b_r = copy(2, x_ref.at[B], out_ref.at[z, x, B], dzr)
    b_l = copy(3, x_ref.at[B], out_ref.at[z, x, B], dzl)
    a_r.wait_recv()
    a2_r = copy(4, out_ref.at[z, xl, A0], out_ref.at[z, xl, A0], dxr)
    a_l.wait_recv()
    a2_l = copy(5, out_ref.at[z, xr, A1], out_ref.at[z, xr, A1], dxl)
    b_r.wait_recv()
    b2_r = copy(6, out_ref.at[zl, x, B0], out_ref.at[zl, x, B0], dzr)
    b_l.wait_recv()
    b2_l = copy(7, out_ref.at[zr, x, B1], out_ref.at[zr, x, B1], dzl)
    own.wait()
    a2_r.wait_recv()
    a2_l.wait_recv()
    c_r = copy(8, out_ref.at[z, :, A], out_ref.at[z, :, A], dzr)
    c_l = copy(9, out_ref.at[z, :, A], out_ref.at[z, :, A], dzl)
    b2_r.wait_recv()
    b2_l.wait_recv()
    d_r = copy(10, out_ref.at[:, x, B], out_ref.at[:, x, B], dxr)
    d_l = copy(11, out_ref.at[:, x, B], out_ref.at[:, x, B], dxl)
    c_r.wait_recv()
    c2_r = copy(12, out_ref.at[zl, :, A0], out_ref.at[zl, :, A0], dzr)
    c_l.wait_recv()
    c2_l = copy(13, out_ref.at[zr, :, A1], out_ref.at[zr, :, A1], dzl)
    d_r.wait_recv()
    d2_r = copy(14, out_ref.at[:, xl, B0], out_ref.at[:, xl, B0], dxr)
    d_l.wait_recv()
    d2_l = copy(15, out_ref.at[:, xr, B1], out_ref.at[:, xr, B1], dxl)
    for c in (c2_r, c2_l, d2_r, d2_l):
        c.wait_recv()
    for c in (a_r, a_l, b_r, b_l, a2_r, a2_l, b2_r, b2_l, c_r, c_l, d_r, d_l, c2_r, c2_l, d2_r, d2_l):
        c.wait_send()


def gather_rows(x, ident):
    rows, cols = x.shape
    out = pl.pallas_call(
        gather_kernel,
        out_shape=jax.ShapeDtypeStruct((4, 4, rows, cols), x.dtype),
        in_specs=[pl.BlockSpec(memory_space=pl.ANY)],
        out_specs=pl.BlockSpec(memory_space=pl.ANY),
        scratch_shapes=[
            pltpu.SemaphoreType.DMA((16,)),
            pltpu.SemaphoreType.DMA((16,)),
            pltpu.SemaphoreType.DMA,
        ],
        compiler_params=pltpu.CompilerParams(collective_id=ident, has_side_effects=True),
        name="gather_rows",
    )(x)
    return out.reshape(16 * rows, cols)


def scatter_kernel(x_ref, out_ref, s1, l1, s2, l2, t0, m1, n1, m2, n2, send, recv):
    z, x, xr, xl, zr, zl, (dxr, dxl, dzr, dzl) = ring_places()
    x2, z2 = lax.rem(x + 2, 4), lax.rem(z + 2, 4)
    rows = x_ref.shape[2]
    half, quarter = rows // 2, rows // 4
    greet((dxr, dxl, dzr, dzl))

    def copy(i, src, dst, to):
        c = pltpu.make_async_remote_copy(
            src_ref=src, dst_ref=dst, send_sem=send.at[i], recv_sem=recv.at[i],
            device_id={"expert": to}, device_id_type=MESH)
        c.start()
        return c

    A0, A1 = pl.ds(0, quarter), pl.ds(quarter, quarter)
    B0, B1 = pl.ds(half, quarter), pl.ds(half + quarter, quarter)

    def total(*parts):
        acc = parts[0].astype(f32)
        for p in parts[1:]:
            acc = acc + p.astype(f32)
        return acc

    c0 = copy(0, x_ref.at[z2, :, A0], l1.at[0], dzr)
    c1 = copy(1, x_ref.at[z2, :, A1], l1.at[1], dzl)
    c2 = copy(2, x_ref.at[:, x2, B0], l1.at[2], dxr)
    c3 = copy(3, x_ref.at[:, x2, B1], l1.at[3], dxl)
    c4 = copy(4, x_ref.at[zr, :, A1], l2.at[0, 1], dzr)
    c5 = copy(5, x_ref.at[zl, :, A0], l2.at[1, 0], dzl)
    c6 = copy(6, x_ref.at[:, xr, B1], l2.at[2, 1], dxr)
    c7 = copy(7, x_ref.at[:, xl, B0], l2.at[3, 0], dxl)
    c0.wait_recv()
    s1[0] = total(x_ref[zr, :, A0], l1[0]).astype(s1.dtype)
    c8 = copy(8, s1.at[0], l2.at[0, 0], dzr)
    c1.wait_recv()
    s1[1] = total(x_ref[zl, :, A1], l1[1]).astype(s1.dtype)
    c9 = copy(9, s1.at[1], l2.at[1, 1], dzl)
    c2.wait_recv()
    s1[2] = total(x_ref[:, xr, B0], l1[2]).astype(s1.dtype)
    c10 = copy(10, s1.at[2], l2.at[2, 0], dxr)
    c3.wait_recv()
    s1[3] = total(x_ref[:, xl, B1], l1[3]).astype(s1.dtype)
    c11 = copy(11, s1.at[3], l2.at[3, 1], dxl)
    c4.wait_recv()
    c9.wait_recv()
    t0[0, 1] = total(x_ref[z, :, A1], l2[0, 1], l2[1, 1]).astype(t0.dtype)
    c5.wait_recv()
    c8.wait_recv()
    t0[0, 0] = total(x_ref[z, :, A0], l2[0, 0], l2[1, 0]).astype(t0.dtype)
    e0 = copy(12, t0.at[0, 0, x2], m1.at[0], dxr)
    e1 = copy(13, t0.at[0, 1, x2], m1.at[1], dxl)
    e4 = copy(14, t0.at[0, 1, xr], m2.at[0, 1], dxr)
    e5 = copy(15, t0.at[0, 0, xl], m2.at[1, 0], dxl)
    c6.wait_recv()
    c11.wait_recv()
    t0[1, 1] = total(x_ref[:, x, B1], l2[2, 1], l2[3, 1]).astype(t0.dtype)
    c7.wait_recv()
    c10.wait_recv()
    t0[1, 0] = total(x_ref[:, x, B0], l2[2, 0], l2[3, 0]).astype(t0.dtype)
    e2 = copy(16, t0.at[1, 0, z2], m1.at[2], dzr)
    e3 = copy(17, t0.at[1, 1, z2], m1.at[3], dzl)
    e6 = copy(18, t0.at[1, 1, zr], m2.at[2, 1], dzr)
    e7 = copy(19, t0.at[1, 0, zl], m2.at[3, 0], dzl)
    e0.wait_recv()
    n1[0] = total(t0[0, 0, xr], m1[0]).astype(n1.dtype)
    e8 = copy(20, n1.at[0], m2.at[0, 0], dxr)
    e1.wait_recv()
    n1[1] = total(t0[0, 1, xl], m1[1]).astype(n1.dtype)
    e9 = copy(21, n1.at[1], m2.at[1, 1], dxl)
    e2.wait_recv()
    n1[2] = total(t0[1, 0, zr], m1[2]).astype(n1.dtype)
    e10 = copy(22, n1.at[2], m2.at[2, 0], dzr)
    e3.wait_recv()
    n1[3] = total(t0[1, 1, zl], m1[3]).astype(n1.dtype)
    e11 = copy(23, n1.at[3], m2.at[3, 1], dzl)
    e4.wait_recv()
    e9.wait_recv()
    out_ref[A1] = total(t0[0, 1, x], m2[0, 1], m2[1, 1])
    e5.wait_recv()
    e8.wait_recv()
    out_ref[A0] = total(t0[0, 0, x], m2[0, 0], m2[1, 0])
    e6.wait_recv()
    e11.wait_recv()
    out_ref[B1] = total(t0[1, 1, z], m2[2, 1], m2[3, 1])
    e7.wait_recv()
    e10.wait_recv()
    out_ref[B0] = total(t0[1, 0, z], m2[2, 0], m2[3, 0])
    for c in (c0, c1, c2, c3, c4, c5, c6, c7, c8, c9, c10, c11,
              e0, e1, e2, e3, e4, e5, e6, e7, e8, e9, e10, e11):
        c.wait_send()


def scatter_sum(x, ident):
    rows, cols = x.shape[0] // 16, x.shape[1]
    q = rows // 4
    return pl.pallas_call(
        scatter_kernel,
        out_shape=jax.ShapeDtypeStruct((rows, cols), jnp.float32),
        in_specs=[pl.BlockSpec(memory_space=pltpu.VMEM)],
        out_specs=pl.BlockSpec(memory_space=pltpu.VMEM),
        scratch_shapes=[
            pltpu.VMEM((4, 4, q, cols), bf16),
            pltpu.VMEM((4, 4, q, cols), bf16),
            pltpu.VMEM((1, 1, 16, 128), bf16),
            pltpu.VMEM((4, 2, 4, q, cols), bf16),
            pltpu.VMEM((2, 2, 4, q, cols), bf16),
            pltpu.VMEM((4, q, cols), bf16),
            pltpu.VMEM((4, q, cols), bf16),
            pltpu.VMEM((4, 2, q, cols), bf16),
            pltpu.VMEM((1, 16, 128), bf16),
            pltpu.SemaphoreType.DMA((24,)),
            pltpu.SemaphoreType.DMA((24,)),
        ],
        compiler_params=pltpu.CompilerParams(
            collective_id=ident, has_side_effects=True, vmem_limit_bytes=48 << 20),
        name="scatter_sum",
    )(x.reshape(4, 4, rows, cols))


def spec(shape, index):
    return pl.BlockSpec(shape, index)


def fixed(shape):
    return pl.BlockSpec(shape, lambda *_: (0,) * len(shape), pipeline_mode=pl.Buffered(1))


def whole():
    return pl.BlockSpec(memory_space=pltpu.VMEM)


def local_call(kernel, outs, name, grid=None, in_specs=None, out_specs=None, flops=0, moved=0):
    params = pltpu.CompilerParams(vmem_limit_bytes=52 << 20)
    kinds = dict(
        out_shape=[jax.ShapeDtypeStruct(s, d) for s, d in outs],
        compiler_params=params,
        name=name,
        cost_estimate=pl.CostEstimate(flops=flops, bytes_accessed=moved, transcendentals=0),
    )
    if grid is None:
        kinds["out_specs"] = [whole()] * len(outs)
        return lambda *a: pl.pallas_call(kernel, in_specs=[whole()] * len(a), **kinds)(*a)
    return pl.pallas_call(kernel, grid=grid, in_specs=in_specs, out_specs=out_specs, **kinds)


def dot(a, b):
    return jnp.dot(a, b, preferred_element_type=f32)


def dot_t(a, b):
    return lax.dot_general(a, b, (((1,), (1,)), ((), ())), preferred_element_type=f32)


def t_dot(a, b):
    return lax.dot_general(a, b, (((0,), (0,)), ((), ())), preferred_element_type=f32)


def lanes(shape):
    return lax.broadcasted_iota(jnp.int32, shape, len(shape) - 1)


def turned(u, cosine, sine):
    chunks = []
    for c in range(u.shape[1] // 128):
        part = u[:, 128 * c : 128 * c + 128]
        low = lax.rem(lanes(part.shape), 64) < 32
        rot = jnp.where(low, -pltpu.roll(part, 96, 1), pltpu.roll(part, 32, 1))
        chunks.append(part * cosine + rot * sine)
    return jnp.concatenate(chunks, axis=1)


def rms(x):
    return lax.rsqrt(jnp.mean(x * x, axis=-1, keepdims=True) + norm_eps)


def pre_kernel(x_ref, gain_ref, cos_ref, sin_ref, wq_ref, wk_ref, wv_ref, a_ref, q_ref, kv_ref):
    x = x_ref[...].astype(f32)
    a = (x * rms(x) * gain_ref[...]).astype(bf16)
    a_ref[...] = a
    cosine, sine = cos_ref[...], sin_ref[...]
    q_ref[...] = turned(dot(a, wq_ref[...]), cosine, sine).astype(bf16)
    kv_ref[:, :512] = turned(dot(a, wk_ref[...]), cosine, sine).astype(bf16)
    kv_ref[:, 512:] = dot(a, wv_ref[...]).astype(bf16)


def head_rows(q):
    q = q.astype(f32)
    left, right = q[:, :128], q[:, 128:]
    low = lanes(left.shape) < 64
    parts = [
        jnp.where(low, left, 0.0),
        jnp.where(low, pltpu.roll(left, 64, 1), 0.0),
        jnp.where(low, 0.0, pltpu.roll(right, 64, 1)),
        jnp.where(low, 0.0, right),
    ]
    return parts


def head_lanes(p0, p1, p2, p3):
    low = lanes(p0.shape) < 64
    left = jnp.where(low, p0, pltpu.roll(p1, 64, 1))
    right = jnp.where(low, pltpu.roll(p2, 64, 1), p3)
    return jnp.concatenate([left, right], axis=1)


def attend_kernel(q_ref, k_ref, v_ref, lo_ref, hi_ref, o_ref, p_ref):
    key = lax.broadcasted_iota(jnp.int32, (128, 2048), 1)
    seen = (key >= lo_ref[...]) & (key <= hi_ref[...])
    k, v = k_ref[...], v_ref[...]
    outs = []
    for h, q in enumerate(head_rows(q_ref[...])):
        s = dot_t((q * 0.125).astype(bf16), k)
        s = jnp.where(seen, s, masked_score)
        e = jnp.exp(s - jnp.max(s, axis=-1, keepdims=True))
        p = (e * (1.0 / jnp.sum(e, axis=-1, keepdims=True))).astype(bf16)
        p_ref[0, 128 * h : 128 * h + 128, :] = p
        outs.append(dot(p, v))
    o_ref[...] = head_lanes(*outs).astype(bf16)


def attend(q, kv, lo, hi):
    return local_call(
        attend_kernel,
        [((128, 1024), bf16), ((4, 512, 2048), bf16)],
        "attend",
        grid=(4,),
        in_specs=[
            spec((128, 256), lambda i: (0, i)),
            spec((2048, 128), lambda i: (0, i)),
            spec((2048, 128), lambda i: (0, i + 4)),
            fixed((128, 1)),
            fixed((128, 1)),
        ],
        out_specs=[
            spec((128, 256), lambda i: (0, i)),
            spec((1, 512, 2048), lambda i: (i, 0, 0)),
        ],
        flops=2 * 2 * 2048 * 2048 * 128,
        moved=13 << 20,
    )(q, kv, kv, lo, hi)


def attend_back_kernel(q_ref, o_ref, do_ref, k_ref, v_ref, p_ref, dq_ref, dkv_ref):
    k, v = k_ref[...], v_ref[...]
    do = do_ref[...]
    prod = do.astype(f32) * o_ref[...].astype(f32)
    low = lanes((128, 128)) < 64
    left, right = prod[:, :128], prod[:, 128:]
    deltas = [
        jnp.sum(jnp.where(low, left, 0.0), axis=1, keepdims=True),
        jnp.sum(jnp.where(low, 0.0, left), axis=1, keepdims=True),
        jnp.sum(jnp.where(low, right, 0.0), axis=1, keepdims=True),
        jnp.sum(jnp.where(low, 0.0, right), axis=1, keepdims=True),
    ]
    do_rows = [r.astype(bf16) for r in head_rows(do)]
    q_rows = [(r * 0.125).astype(bf16) for r in head_rows(q_ref[...])]
    dqs, dss = [], []
    for h in range(4):
        dp = dot_t(do_rows[h], v)
        p = p_ref[0, 128 * h : 128 * h + 128, :].astype(f32)
        ds = (p * (dp - deltas[h])).astype(bf16)
        dss.append(ds)
        dqs.append(dot(ds, k) * 0.125)
    dq_ref[...] = head_lanes(*dqs)
    dkv_ref[:, :128] = t_dot(jnp.concatenate(dss, axis=0), jnp.concatenate(q_rows, axis=0)).astype(bf16)
    dkv_ref[:, 128:] = t_dot(p_ref[0], jnp.concatenate(do_rows, axis=0)).astype(bf16)


def attend_back(q, o, do, kv, probs):
    side = spec((128, 256), lambda i: (0, i))
    return local_call(
        attend_back_kernel,
        [((128, 1024), f32), ((2048, 1024), bf16)],
        "attend_back",
        grid=(4,),
        in_specs=[
            side,
            side,
            side,
            spec((2048, 128), lambda i: (0, i)),
            spec((2048, 128), lambda i: (0, i + 4)),
            spec((1, 512, 2048), lambda i: (i, 0, 0)),
        ],
        out_specs=[side, spec((2048, 256), lambda i: (0, i))],
        flops=4 * 2 * 2048 * 2048 * 128,
        moved=17 << 20,
    )(q, o, do, kv, kv, probs)


def post_kernel(x_ref, o_ref, wo_ref, gain_ref, h_ref, b_ref):
    h = x_ref[...].astype(f32) + dot(o_ref[...], wo_ref[...])
    h_ref[...] = h
    b_ref[...] = (h * rms(h) * gain_ref[...]).astype(bf16)


def chosen_gates(b, wr, mask):
    logits = dot(b, wr)
    chosen = mask.astype(f32) > 0.5
    top = jnp.max(jnp.where(chosen, logits, masked_score), axis=-1, keepdims=True)
    e = jnp.where(chosen, jnp.exp(jnp.where(chosen, logits - top, 0.0)), 0.0)
    return e / jnp.sum(e, axis=-1, keepdims=True)


def experts_kernel(b_ref, mask_ref, wr_ref, pick_ref, wg_ref, wu_ref, wd_ref, y_ref, gu_ref, gate_ref):
    b = b_ref[...]
    gates = chosen_gates(b, wr_ref[...], mask_ref[...])
    cols = []
    y = None
    for j in range(2):
        gate = jnp.sum(gates * pick_ref[j : j + 1, :], axis=1, keepdims=True)
        cols.append(gate)
        g = dot(b, wg_ref[j])
        u = dot(b, wu_ref[j])
        gu_ref[:, 1024 * j : 1024 * j + 512] = g.astype(bf16)
        gu_ref[:, 1024 * j + 512 : 1024 * j + 1024] = u.astype(bf16)
        inner = g * jax.nn.sigmoid(g) * u
        part = dot_t((inner * gate).astype(bf16), wd_ref[j])
        y = part if y is None else y + part
    y_ref[...] = y.astype(bf16)
    lane = lanes(gate_ref.shape)
    gate_ref[...] = jnp.where(lane == 0, cols[0], jnp.where(lane == 1, cols[1], 0.0))


TILE = 256


def tile(cols):
    return spec((TILE, cols), lambda i: (i, 0))


def experts(b_all, mask_all, wr, pick, wg, wu, wd):
    rows = b_all.shape[0]
    return local_call(
        experts_kernel,
        [((rows, 1024), bf16), ((rows, 2048), bf16), ((rows, 128), f32)],
        "experts",
        grid=(rows // TILE,),
        in_specs=[
            tile(1024),
            tile(32),
            fixed((1024, 32)),
            fixed((8, 32)),
            fixed((2, 1024, 512)),
            fixed((2, 1024, 512)),
            fixed((2, 1024, 512)),
        ],
        out_specs=[tile(1024), tile(2048), tile(128)],
        flops=6 * 2 * 2048 * 1024 * 512,
        moved=24 << 20,
    )(b_all, mask_all, wr, pick, wg, wu, wd)


def experts_back_kernel(
    dout_ref, gu_ref, gate_ref, wr_ref, pick_ref, wg_ref, wu_ref, wd_ref, db_ref, dgu_ref, in_ref, coef_ref
):
    dout = dout_ref[...]
    lane = lanes(gate_ref.shape)
    all_gates = gate_ref[...]
    db = None
    coef = None
    for j in range(2):
        gate = jnp.sum(jnp.where(lane == j, all_gates, 0.0), axis=1, keepdims=True)
        g = gu_ref[:, 1024 * j : 1024 * j + 512].astype(f32)
        u = gu_ref[:, 1024 * j + 512 : 1024 * j + 1024].astype(f32)
        back = dot(dout, wd_ref[j])
        sig = jax.nn.sigmoid(g)
        silu = g * sig
        inner = silu * u
        dgate = jnp.sum(inner * back, axis=1, keepdims=True)
        in_ref[:, 512 * j : 512 * j + 512] = (inner * gate).astype(bf16)
        dinner = back * gate
        dg = (dinner * u * sig * (1.0 + g * (1.0 - sig))).astype(bf16)
        du = (dinner * silu).astype(bf16)
        dgu_ref[:, 1024 * j : 1024 * j + 512] = dg
        dgu_ref[:, 1024 * j + 512 : 1024 * j + 1024] = du
        part = dot_t(dg, wg_ref[j]) + dot_t(du, wu_ref[j])
        share = gate * dgate * pick_ref[j : j + 1, :]
        db = part if db is None else db + part
        coef = share if coef is None else coef + share
    coef = coef.astype(bf16)
    coef_ref[...] = coef
    db_ref[...] = (db + dot_t(coef, wr_ref[...])).astype(bf16)


def experts_back(dout_all, gu, gate, wr, pick, wg, wu, wd):
    rows = dout_all.shape[0]
    return local_call(
        experts_back_kernel,
        [((rows, 1024), bf16), ((rows, 2048), bf16), ((rows, 1024), bf16), ((rows, 32), bf16)],
        "experts_back",
        grid=(rows // TILE,),
        in_specs=[
            tile(1024),
            tile(2048),
            tile(128),
            fixed((1024, 32)),
            fixed((8, 32)),
            fixed((2, 1024, 512)),
            fixed((2, 1024, 512)),
            fixed((2, 1024, 512)),
        ],
        out_specs=[tile(1024), tile(2048), tile(1024), tile(32)],
        flops=6 * 2 * 2048 * 1024 * 512,
        moved=36 << 20,
    )(dout_all, gu, gate, wr, pick, wg, wu, wd)


def mid_back_kernel(
    sum_ref, dout_ref, mix_ref, h_ref, b_ref, gain_ref, wr_ref, mask_ref, wo_ref,
    dh_ref, dattn_ref, do_ref, router_ref, gain_grad_ref,
):
    dout = dout_ref[...].astype(f32)
    b = b_ref[...]
    wr = wr_ref[...]
    h = h_ref[...]
    r = rms(h)
    n = h * r
    gates = chosen_gates(b, wr, mask_ref[...])
    level = jnp.sum(dout * mix_ref[...], axis=-1, keepdims=True)
    taken = (gates * -level).astype(bf16)
    router_ref[...] = t_dot(b, taken)
    db = sum_ref[...] + dot_t(taken, wr)
    gain_grad_ref[...] = jnp.broadcast_to(jnp.sum(db * n, axis=0, keepdims=True), gain_grad_ref.shape)
    ng = db * gain_ref[...]
    dh = dout + r * (ng - n * jnp.mean(ng * n, axis=-1, keepdims=True))
    dh_ref[...] = dh
    dattn = dh.astype(bf16)
    dattn_ref[...] = dattn
    do_ref[...] = dot_t(dattn, wo_ref[...]).astype(bf16)


def end_back_kernel(
    dq_ref, dkv_ref, cos_ref, sin_ref, wq_ref, wk_ref, wv_ref, x_ref, gain_ref, dh_ref,
    dq_lin_ref, dkv_lin_ref, dx_ref, gain_grad_ref,
):
    cosine, sine = cos_ref[...], -sin_ref[...]
    dq = turned(dq_ref[...], cosine, sine).astype(bf16)
    dkv = dkv_ref[...]
    dk = jnp.concatenate([dkv[:, 256 * i : 256 * i + 128] for i in range(4)], axis=1)
    dv = jnp.concatenate([dkv[:, 256 * i + 128 : 256 * i + 256] for i in range(4)], axis=1)
    dk = turned(dk, cosine, sine).astype(bf16)
    dv = dv.astype(bf16)
    dq_lin_ref[...] = dq
    dkv_lin_ref[:, :512] = dk
    dkv_lin_ref[:, 512:] = dv
    da = dot_t(dq, wq_ref[...]) + dot_t(dk, wk_ref[...]) + dot_t(dv, wv_ref[...])
    x = x_ref[...].astype(f32)
    r = rms(x)
    n = x * r
    gain_grad_ref[...] = jnp.broadcast_to(jnp.sum(da * n, axis=0, keepdims=True), gain_grad_ref.shape)
    ng = da * gain_ref[...]
    dx = dh_ref[...] + r * (ng - n * jnp.mean(ng * n, axis=-1, keepdims=True))
    dx_ref[...] = dx.astype(bf16)


def dense_grads_kernel(a_ref, o_ref, dq_ref, dkv_ref, dattn_ref, *rest):
    small_ref, out_ref = rest if len(rest) == 2 else (None, rest[0])
    a = a_ref[...]
    gq = t_dot(a, dq_ref[...]).astype(bf16)
    gkv = t_dot(a, dkv_ref[...]).astype(bf16)
    go = t_dot(o_ref[...], dattn_ref[...]).astype(bf16)
    for t in range(2):
        part = slice(64 * t, 64 * t + 64)
        out_ref[t, 0:64, 0:1024] = gq[part]
        out_ref[t, 64:128, 0:1024] = gkv[part]
        out_ref[t, 128:192, 0:1024] = go[part]
        if small_ref is not None:
            out_ref[t, 0:64, 1024:1152] = small_ref[part, :]
            out_ref[t, 64:192, 1024:1152] = jnp.zeros((128, 128), bf16)


def dense_grads(a, o, dq, dkv, dattn, small=None):
    cols = 1024 if small is None else 1152
    narrow = spec((128, 128), lambda i: (0, i))
    args = (a, o, dq, dkv, dattn) + (() if small is None else (small,))
    return local_call(
        dense_grads_kernel,
        [((16, 192, cols), bf16)],
        "dense_grads",
        grid=(8,),
        in_specs=[narrow, narrow] + [fixed((128, 1024))] * 3
        + ([] if small is None else [spec((128, 128), lambda i: (i, 0))]),
        out_specs=[spec((2, 192, cols), lambda i: (i, 0, 0))],
        flops=3 * 2 * 128 * 1024 * 1024,
        moved=8 << 20,
    )(*args)[0]


def cross_kernel(own_ref, other_ref, out_ref, land, mine, send, recv):
    section, dp = lax.axis_index("section"), lax.axis_index("dp")
    partners = (
        {"section": 1 - section},
        {"dp": dp + 1 - 2 * lax.rem(dp, 2)},
        {"dp": lax.rem(dp + 2, 4)},
    )
    barrier = pltpu.get_barrier_semaphore()
    for to in partners:
        pl.semaphore_signal(barrier, inc=1, device_id=to, device_id_type=MESH)
    pl.semaphore_wait(barrier, 3)
    copies = []
    for i, to in enumerate(partners):
        src = other_ref if i == 0 else mine.at[i - 1]
        c = pltpu.make_async_remote_copy(
            src_ref=src, dst_ref=land.at[i], send_sem=send.at[i], recv_sem=recv.at[i],
            device_id=to, device_id_type=MESH)
        c.start()
        copies.append(c)
        c.wait_recv()
        before = own_ref[...] if i == 0 else mine[i - 1].astype(f32)
        after = (before + land[i].astype(f32)).astype(bf16)
        if i < 2:
            mine[i] = after
        else:
            out_ref[...] = after
    for c in copies:
        c.wait_send()


def cross_sum(own, other, ident):
    rows, cols = own.shape
    return pl.pallas_call(
        cross_kernel,
        out_shape=jax.ShapeDtypeStruct((rows, cols), bf16),
        in_specs=[whole(), whole()],
        out_specs=whole(),
        scratch_shapes=[
            pltpu.VMEM((3, rows, cols), bf16),
            pltpu.VMEM((2, rows, cols), bf16),
            pltpu.SemaphoreType.DMA((3,)),
            pltpu.SemaphoreType.DMA((3,)),
        ],
        compiler_params=pltpu.CompilerParams(
            collective_id=ident, has_side_effects=True, vmem_limit_bytes=24 << 20),
        name="cross_sum",
    )(own, other)


def forward(x, place, dense, experts_w, masks):
    cosine, sine, lo, hi, pick = place
    wq, wk, wv, wo, gain_attn, gain_moe, wr = dense
    mask_all = masks[1]
    a, q, kv = local_call(
        pre_kernel, [((128, 1024), bf16)] * 3, "pre", flops=2 * 128 * 1024 * 2048, moved=6 << 20
    )(x, gain_attn, cosine, sine, wq, wk, wv)
    kv_all = gather_rows(kv, 1)
    o, probs = attend(q, kv_all, lo, hi)
    h, b = local_call(
        post_kernel, [((128, 1024), f32), ((128, 1024), bf16)], "post",
        flops=2 * 128 * 1024 * 1024, moved=4 << 20,
    )(x, o, wo, gain_moe)
    b_all = gather_rows(b, 1)
    y, gu, gate = experts(b_all, mask_all, wr, pick, *experts_w)
    mix = scatter_sum(y, 2)
    out = (h + mix).astype(bf16)
    return out, (x, a, q, kv_all, o, probs, h, b, b_all, gu, gate, mix)


def backward(dout, saved, place, dense, experts_w, masks):
    cosine, sine, lo, hi, pick = place
    wq, wk, wv, wo, gain_attn, gain_moe, wr = dense
    mask_own = masks[0]
    x, a, q, kv_all, o, probs, h, b, b_all, gu, gate, mix = saved
    dout_all = gather_rows(dout, 1)
    db_part, dgu, inner, coef = experts_back(dout_all, gu, gate, wr, pick, *experts_w)
    db_sum = scatter_sum(db_part, 2)
    up_grad = lax.dot_general(b_all, dgu, (((0,), (0,)), ((), ())), preferred_element_type=f32)
    down_grad = lax.dot_general(dout_all, inner, (((0,), (0,)), ((), ())), preferred_element_type=f32)
    expert_grad = jnp.concatenate([up_grad.astype(bf16), down_grad.astype(bf16)], axis=1)
    expert_grad = lax.psum_scatter(expert_grad, "dp", scatter_dimension=0, tiled=True)
    router_part = lax.dot_general(b_all, coef, (((0,), (0,)), ((), ())), preferred_element_type=f32)
    dh, dattn, do, router_own, gain_moe_grad = local_call(
        mid_back_kernel,
        [((128, 1024), f32), ((128, 1024), bf16), ((128, 1024), bf16), ((1024, 32), f32), ((8, 1024), f32)],
        "mid_back", flops=2 * 128 * 1024 * 1024, moved=5 << 20,
    )(db_sum, dout, mix, h, b, gain_moe, wr, mask_own, wo)
    dq, dkv = attend_back(q, o, do, kv_all, probs)
    dkv_sum = scatter_sum(dkv, 2)
    dq_lin, dkv_lin, dx, gain_attn_grad = local_call(
        end_back_kernel,
        [((128, 1024), bf16), ((128, 1024), bf16), ((128, 1024), bf16), ((8, 1024), f32)],
        "end_back", flops=2 * 128 * 1024 * 2048, moved=8 << 20,
    )(dq, dkv_sum, cosine, sine, wq, wk, wv, x, gain_attn, dh)
    small = jnp.concatenate(
        [
            router_part + router_own,
            gain_attn_grad[0][:, None],
            gain_moe_grad[0][:, None],
            jnp.zeros((1024, 30), f32),
        ],
        axis=1,
    ).astype(bf16)
    return dx, expert_grad, (a, o, dq_lin, dkv_lin, dattn), small


def swapped(x):
    return lax.ppermute(x, "section", [(0, 1), (1, 0)])


def on_device(
    inputs, cotangent, offsets, routes, w_query, w_key, w_value, w_out,
    norm_attn, norm_moe, w_router, w_gate, w_up, w_down,
):
    section = lax.axis_index("section")
    expert = lax.axis_index("expert")
    first = section == 0

    def by_layer(own, other):
        return jnp.where(first, own, other), jnp.where(first, other, own)

    def mine(pair):
        return jnp.where(first, pair[0], pair[1])

    ids = lax.broadcasted_iota(jnp.int32, (1, 1, 1, 32), 3)
    mask_both = jnp.any(routes[0][:, :, :, None] == ids, axis=2).astype(bf16)
    mask_own = mine(mask_both)
    mask_away = jnp.where(first, mask_both[1], mask_both[0])
    start = expert * 64

    def part(w):
        return lax.dynamic_slice_in_dim(w, start, 64, axis=0)

    rows = jnp.concatenate(
        [part(w_query[0]), jnp.concatenate([part(w_key[0]), part(w_value[0])], axis=1), part(w_out[0])],
        axis=0,
    )
    small = jnp.concatenate(
        [part(w_router[0]), part(norm_attn[0][:, None]), part(norm_moe[0][:, None]),
         jnp.zeros((64, 30), bf16)], axis=1)
    extra = jnp.concatenate([mask_away, jnp.zeros((128, 32), bf16)], axis=1)
    extra = jnp.concatenate([extra, small], axis=0)
    extra = jnp.concatenate([extra, jnp.zeros((192, 64), bf16)], axis=1)
    payload = swapped(jnp.concatenate([rows, extra], axis=1))
    mask_other = payload[0:128, 1024:1056]
    own_rows = jnp.concatenate([mask_own, jnp.zeros((64, 32), bf16)], axis=0)
    payload = jnp.concatenate([payload[:, :1088], own_rows, payload[:, 1120:]], axis=1)
    got = gather_rows(payload, 3).reshape(16, 192, 1152)
    other_q = got[:, 0:64, :1024].reshape(1024, 1024)
    other_kv = got[:, 64:128, :1024].reshape(1024, 1024)
    other_o = got[:, 128:192, :1024].reshape(1024, 1024)
    other_small = got[:, 128:192, 1024:1088].reshape(1024, 64)
    all_other = got[:, 0:128, 1024:1056].reshape(2048, 32)
    all_own = got[:, 0:128, 1088:1120].reshape(2048, 32)
    pairs = [
        by_layer(w_query[0], other_q),
        by_layer(w_key[0], other_kv[:, :512]),
        by_layer(w_value[0], other_kv[:, 512:]),
        by_layer(w_out[0], other_o),
        by_layer(norm_attn.astype(f32), other_small[:, 32][None].astype(f32)),
        by_layer(norm_moe.astype(f32), other_small[:, 33][None].astype(f32)),
        by_layer(w_router[0], other_small[:, :32]),
    ]
    dense = [tuple(p[l] for p in pairs) for l in range(2)]
    masks_own = by_layer(mask_own, mask_other)
    masks_all = by_layer(all_own, all_other)
    masks = [(masks_own[l], masks_all[l]) for l in range(2)]

    shards = (w_gate[0], w_up[0], w_down[0])
    away = tuple(swapped(w) for w in shards)
    expert_w = []
    for l in range(2):
        expert_w.append(tuple(
            lax.all_gather(by_layer(w, v)[l], "dp", axis=1, tiled=True) for w, v in zip(shards, away)))

    seq = mine(offsets)
    local = expert * 128 + jnp.arange(128, dtype=jnp.int32)
    steps = jnp.arange(HEAD // 2, dtype=f32) * 2.0 / HEAD
    angles = (local - seq).astype(f32)[:, None] * (rope_base ** (-steps))[None, :]
    cosine = jnp.tile(jnp.cos(angles), (1, 4))
    sine = jnp.tile(jnp.sin(angles), (1, 4))
    pick = (
        lax.broadcasted_iota(jnp.int32, (8, 32), 1)
        == 2 * expert + lax.broadcasted_iota(jnp.int32, (8, 32), 0)
    ).astype(f32)
    place = (cosine, sine, seq[:, None], local[:, None], pick)

    x0 = mine(inputs)
    out0, saved0 = forward(x0, place, dense[0], expert_w[0], masks[0])
    out1, saved1 = forward(out0, place, dense[1], expert_w[1], masks[1])
    cot = mine(cotangent)
    dx1, eg1, dg1, small1 = backward(cot, saved1, place, dense[1], expert_w[1], masks[1])
    dense1 = scatter_sum(dense_grads(*dg1).reshape(3072, 1024), 4)
    dx0, eg0, dg0, small0 = backward(dx1, saved0, place, dense[0], expert_w[0], masks[0])
    dense0 = scatter_sum(
        dense_grads(*dg0, jnp.concatenate([small0, small1], axis=1)).reshape(3072, 1152), 5)

    def in_place(l0, l1):
        got = swapped(jnp.where(first, l1, l0))
        own = jnp.where(first, l0, l1)
        return jnp.stack([jnp.where(first, own, got), jnp.where(first, got, own)])[None]

    acts = in_place(out0, out1)
    in_grads = in_place(dx0, dx1)

    blank = jnp.zeros((192, 64), f32)
    full0 = jnp.concatenate([dense0[:, :1088], blank], axis=1)
    full1 = jnp.concatenate([dense1, dense0[:, 1088:], blank], axis=1)
    own = jnp.where(first, full0, full1)
    other = jnp.where(first, full1, full0).astype(bf16)
    summed = gather_rows(cross_sum(own, other, 6), 3).reshape(16, 192, 1152)
    grad_query = summed[:, 0:64, :1024].reshape(1024, 1024).astype(f32)
    grad_kv = summed[:, 64:128, :1024].reshape(1024, 1024).astype(f32)
    grad_out = summed[:, 128:192, :1024].reshape(1024, 1024).astype(f32)
    grad_small = summed[:, 0:64, 1024:1088].reshape(1024, 64).astype(f32)

    eg_away = swapped(jnp.where(first, eg1, eg0))
    eg = jnp.where(first, eg0, eg1).astype(f32) + eg_away.astype(f32)

    def both(lo, hi):
        return jnp.stack([eg[:, lo : lo + 512], eg[:, hi : hi + 512]])[None]

    return (
        acts,
        in_grads,
        grad_query[None],
        grad_kv[None, :, :512],
        grad_kv[None, :, 512:],
        grad_out[None],
        grad_small[:, 32][None],
        grad_small[:, 33][None],
        grad_small[None, :, :32],
        both(0, 1024),
        both(512, 1536),
        both(2048, 2560),
    )


def solution(mesh):
    token = P(None, ("dp", "expert"), None)
    layer_token = P("section", None, ("dp", "expert"), None)
    matrix = P("section", None, None)
    gain = P("section", None)
    expert = P("section", "expert", "dp", None)
    return jax.shard_map(
        on_device,
        mesh=mesh,
        in_specs=(
            token, token, P(None, ("dp", "expert")), layer_token,
            matrix, matrix, matrix, matrix, gain, gain, matrix, expert, expert, expert,
        ),
        out_specs=(
            layer_token, layer_token, matrix, matrix, matrix, matrix, gain, gain, matrix,
            expert, expert, expert,
        ),
        check_vma=False,
    )
```

```python
import functools

import jax
import jax.numpy as jnp
from jax import lax
from jax.experimental import pallas as pl
from jax.experimental.pallas import tpu as pltpu

from jax.sharding import PartitionSpec as P

HEAD = 64
MESH = pl.DeviceIdType.MESH
bf16 = jnp.bfloat16
f32 = jnp.float32
norm_eps = 1e-06
masked_score = -1e30
rope_base = 10000.0


def ring_places():
    me = lax.axis_index("expert")
    z, x = lax.div(me, 4), lax.rem(me, 4)
    xr, xl = lax.rem(x + 1, 4), lax.rem(x + 3, 4)
    zr, zl = lax.rem(z + 1, 4), lax.rem(z + 3, 4)
    near = (z * 4 + xr, z * 4 + xl, zr * 4 + x, zl * 4 + x)
    return z, x, xr, xl, zr, zl, near


def gather_kernel(kind, x_ref, *refs):
    split = kind != "plain"
    if kind == "weights":
        side_ref, wq_ref, wk_ref, wv_ref, wo_ref, out_all, side_out = refs[:7]
    elif split:
        side_ref, out_all, side_out = refs[:3]
    else:
        out_all = refs[0]
    send, recv, own_sem = refs[-3:]
    z, x, xr, xl, zr, zl, (dxr, dxl, dzr, dzl) = ring_places()
    x2, z2 = lax.rem(x + 2, 4), lax.rem(z + 2, 4)
    section, dp = lax.axis_index("section"), lax.axis_index("dp")
    core = lax.rem(dp, 2)
    rows, cols = x_ref.shape
    half, quarter = rows // 2, rows // 4
    locals_ = []
    if kind == "weights":
        out_ref = out_all.at[1 - section, core]
        moves = (
            (wq_ref.at[:, :, :, pl.ds(0, 512)], 0, 0),
            (wq_ref.at[:, :, :, pl.ds(512, 512)], 1, 0),
            (wk_ref, 0, 64),
            (wv_ref, 1, 64),
            (wo_ref.at[:, :, :, pl.ds(0, 512)], 0, 128),
            (wo_ref.at[:, :, :, pl.ds(512, 512)], 1, 128),
        )
        for i, (src, side, row) in enumerate(moves):
            dst = out_all.at[section, side, :, :, pl.ds(row, 64), pl.ds(0, 512)]
            c = pltpu.make_async_copy(src, dst, own_sem.at[1 + i])
            c.start()
            locals_.append(c)
    elif split:
        out_ref = out_all.at[core]
    else:
        out_ref = out_all
    own = pltpu.make_async_copy(x_ref, out_ref.at[z, x], own_sem.at[0])
    own.start()
    other_core, other_section = {"dp": dp + 1 - 2 * core}, {"section": 1 - section}
    barrier = pltpu.get_barrier_semaphore()
    greeted = [{"expert": d} for d in (dxr, dxl, dzr, dzl)]
    if split:
        greeted += [other_core, other_section]
    for to in greeted:
        pl.semaphore_signal(barrier, inc=1, device_id=to, device_id_type=MESH)
    pl.semaphore_wait(barrier, len(greeted))

    def send_to(i, src, dst, to):
        c = pltpu.make_async_remote_copy(
            src_ref=src, dst_ref=dst, send_sem=send.at[i], recv_sem=recv.at[i],
            device_id=to, device_id_type=MESH)
        c.start()
        return c

    def copy(i, src, dst, to):
        return send_to(i, src, dst, {"expert": to})

    forwards = []

    def forward(*piece):
        if split:
            there = out_ref.at[piece]
            forwards.append(send_to(17 + len(forwards), there, there, other_core))

    A, B = pl.ds(0, half), pl.ds(half, half)
    A0, A1 = pl.ds(0, quarter), pl.ds(quarter, quarter)
    B0, B1 = pl.ds(half, quarter), pl.ds(half + quarter, quarter)
    every = slice(None)
    a_r = copy(0, x_ref.at[A], out_ref.at[z, x, A], dxr)
    a_l = copy(1, x_ref.at[A], out_ref.at[z, x, A], dxl)
    b_r = copy(2, x_ref.at[B], out_ref.at[z, x, B], dzr)
    b_l = copy(3, x_ref.at[B], out_ref.at[z, x, B], dzl)
    if split:
        swap = send_to(16, side_ref, side_out, other_section)
    a_r.wait_recv()
    a2_r = copy(4, out_ref.at[z, xl, A0], out_ref.at[z, xl, A0], dxr)
    a_l.wait_recv()
    a2_l = copy(5, out_ref.at[z, xr, A1], out_ref.at[z, xr, A1], dxl)
    b_r.wait_recv()
    b2_r = copy(6, out_ref.at[zl, x, B0], out_ref.at[zl, x, B0], dzr)
    b_l.wait_recv()
    b2_l = copy(7, out_ref.at[zr, x, B1], out_ref.at[zr, x, B1], dzl)
    own.wait()
    a2_r.wait_recv()
    a2_l.wait_recv()
    c_r = copy(8, out_ref.at[z, :, A], out_ref.at[z, :, A], dzr)
    c_l = copy(9, out_ref.at[z, :, A], out_ref.at[z, :, A], dzl)
    b2_r.wait_recv()
    b2_l.wait_recv()
    d_r = copy(10, out_ref.at[:, x, B], out_ref.at[:, x, B], dxr)
    d_l = copy(11, out_ref.at[:, x, B], out_ref.at[:, x, B], dxl)
    forward(z, every, A)
    forward(every, x, B)
    c_r.wait_recv()
    c2_r = copy(12, out_ref.at[zl, :, A0], out_ref.at[zl, :, A0], dzr)
    c_l.wait_recv()
    c2_l = copy(13, out_ref.at[zr, :, A1], out_ref.at[zr, :, A1], dzl)
    d_r.wait_recv()
    d2_r = copy(14, out_ref.at[:, xl, B0], out_ref.at[:, xl, B0], dxr)
    d_l.wait_recv()
    d2_l = copy(15, out_ref.at[:, xr, B1], out_ref.at[:, xr, B1], dxl)
    forward(zl, every, A)
    forward(zr, every, A)
    forward(every, xl, B)
    forward(every, xr, B)
    c2_r.wait_recv()
    forward(z2, every, A0)
    c2_l.wait_recv()
    forward(z2, every, A1)
    d2_r.wait_recv()
    forward(every, x2, B0)
    d2_l.wait_recv()
    forward(every, x2, B1)
    for c in (a_r, a_l, b_r, b_l, a2_r, a2_l, b2_r, b2_l, c_r, c_l, d_r, d_l, c2_r, c2_l, d2_r, d2_l):
        c.wait_send()
    if split:
        for c in forwards + [swap]:
            c.wait_recv()
            c.wait_send()
    for c in locals_:
        c.wait()


def gather_call(ident, kind, outs, in_memory, *args):
    anywhere, memory = pl.BlockSpec(memory_space=pl.ANY), pl.BlockSpec(memory_space=pltpu.VMEM)
    return pl.pallas_call(
        functools.partial(gather_kernel, kind),
        out_shape=outs,
        in_specs=[memory if held else anywhere for held in in_memory],
        out_specs=[anywhere] * len(outs),
        scratch_shapes=[
            pltpu.SemaphoreType.DMA((27,)),
            pltpu.SemaphoreType.DMA((27,)),
            pltpu.SemaphoreType.DMA((7,)),
        ],
        compiler_params=pltpu.CompilerParams(
            collective_id=ident, has_side_effects=True, vmem_limit_bytes=56 << 20),
        name="gather_" + kind,
    )(*args)


def gather_rows(x, ident):
    rows, cols = x.shape
    out = gather_call(ident, "plain", [jax.ShapeDtypeStruct((4, 4, rows, cols), x.dtype)], (True,), x)[0]
    return out.reshape(16 * rows, cols)


def gather_split(x, side, ident):
    rows, cols = x.shape
    out, side_out = gather_call(
        ident, "split",
        [jax.ShapeDtypeStruct((2, 4, 4, rows, cols), x.dtype), jax.ShapeDtypeStruct(side.shape, side.dtype)],
        (True, False), x, side)
    return out.reshape(2, 16, rows, cols), side_out


def gather_weights(x, side, wq, wk, wv, wo, ident):
    rows, cols = x.shape
    parts = [w.reshape(4, 4, 64, w.shape[1]) for w in (wq, wk, wv, wo)]
    out, side_out = gather_call(
        ident, "weights",
        [jax.ShapeDtypeStruct((2, 2, 4, 4, rows, cols), x.dtype), jax.ShapeDtypeStruct(side.shape, side.dtype)],
        (True, False) + (True,) * 4, x, side, *parts)
    return out.reshape(2, 2, 16, rows, cols), side_out


def scatter_kernel(split, x_ref, out_ref, loc, *refs):
    if split:
        land, core_send, core_recv = refs[0], refs[-2], refs[-1]
        refs = refs[1:-2]
    s1, l1, l2, t0, m1, n1, m2, send, recv, loc_sem = refs
    z, x, xr, xl, zr, zl, (dxr, dxl, dzr, dzl) = ring_places()
    x2, z2 = lax.rem(x + 2, 4), lax.rem(z + 2, 4)
    dp = lax.axis_index("dp")
    core = lax.rem(dp, 2)
    rows = x_ref.shape[-2]
    half, quarter = rows // 2, rows // 4
    A0, A1 = pl.ds(0, quarter), pl.ds(quarter, quarter)
    B0, B1 = pl.ds(half, quarter), pl.ds(half + quarter, quarter)
    every = slice(None)
    pieces = (
        (z2, every, A0), (z2, every, A1), (every, x2, B0), (every, x2, B1),
        (zr, every, A1), (zl, every, A0), (every, xr, B1), (every, xl, B0),
        (zr, every, A0), (zl, every, A1), (every, xr, B0), (every, xl, B1),
        (z, every, A0), (z, every, A1), (every, x, B0), (every, x, B1),
    )
    part = x_ref.at[core] if split else x_ref
    skip = 0 if split else 8
    held = []
    for i, piece in enumerate(pieces[skip:]):
        c = pltpu.make_async_copy(part.at[piece], loc.at[i], loc_sem.at[i])
        c.start()
        held.append(c)
    other_core = {"dp": dp + 1 - 2 * core}
    barrier = pltpu.get_barrier_semaphore()
    greeted = [{"expert": d} for d in (dxr, dxl, dzr, dzl)] + ([other_core] if split else [])
    for to in greeted:
        pl.semaphore_signal(barrier, inc=1, device_id=to, device_id_type=MESH)
    pl.semaphore_wait(barrier, len(greeted))
    away = []
    if split:
        for i, piece in enumerate(pieces):
            c = pltpu.make_async_remote_copy(
                src_ref=x_ref.at[(1 - core,) + piece], dst_ref=land.at[i], send_sem=core_send.at[i],
                recv_sem=core_recv.at[i], device_id=other_core, device_id_type=MESH)
            c.start()
            away.append(c)

    def copy(i, src, dst, to):
        c = pltpu.make_async_remote_copy(
            src_ref=src, dst_ref=dst, send_sem=send.at[i], recv_sem=recv.at[i],
            device_id={"expert": to}, device_id_type=MESH)
        c.start()
        return c

    def total(*parts):
        acc = parts[0].astype(f32)
        for p in parts[1:]:
            acc = acc + p.astype(f32)
        return acc

    def ready(i):
        if i < skip:
            return x_ref.at[pieces[i]]
        held[i - skip].wait()
        if split:
            away[i].wait_recv()
            loc[i] = total(loc[i], land[i]).astype(bf16)
        return loc.at[i - skip]

    c0 = copy(0, ready(0), l1.at[0], dzr)
    c1 = copy(1, ready(1), l1.at[1], dzl)
    c2 = copy(2, ready(2), l1.at[2], dxr)
    c3 = copy(3, ready(3), l1.at[3], dxl)
    c4 = copy(4, ready(4), l2.at[0, 1], dzr)
    c5 = copy(5, ready(5), l2.at[1, 0], dzl)
    c6 = copy(6, ready(6), l2.at[2, 1], dxr)
    c7 = copy(7, ready(7), l2.at[3, 0], dxl)
    mine = ready(8)
    c0.wait_recv()
    s1[0] = total(mine[...], l1[0]).astype(bf16)
    c8 = copy(8, s1.at[0], l2.at[0, 0], dzr)
    mine = ready(9)
    c1.wait_recv()
    s1[1] = total(mine[...], l1[1]).astype(bf16)
    c9 = copy(9, s1.at[1], l2.at[1, 1], dzl)
    mine = ready(10)
    c2.wait_recv()
    s1[2] = total(mine[...], l1[2]).astype(bf16)
    c10 = copy(10, s1.at[2], l2.at[2, 0], dxr)
    mine = ready(11)
    c3.wait_recv()
    s1[3] = total(mine[...], l1[3]).astype(bf16)
    c11 = copy(11, s1.at[3], l2.at[3, 1], dxl)
    mine = ready(13)
    c4.wait_recv()
    c9.wait_recv()
    t0[0, 1] = total(mine[...], l2[0, 1], l2[1, 1]).astype(bf16)
    mine = ready(12)
    c5.wait_recv()
    c8.wait_recv()
    t0[0, 0] = total(mine[...], l2[0, 0], l2[1, 0]).astype(bf16)
    e0 = copy(12, t0.at[0, 0, x2], m1.at[0], dxr)
    e1 = copy(13, t0.at[0, 1, x2], m1.at[1], dxl)
    e4 = copy(14, t0.at[0, 1, xr], m2.at[0, 1], dxr)
    e5 = copy(15, t0.at[0, 0, xl], m2.at[1, 0], dxl)
    mine = ready(15)
    c6.wait_recv()
    c11.wait_recv()
    t0[1, 1] = total(mine[...], l2[2, 1], l2[3, 1]).astype(bf16)
    mine = ready(14)
    c7.wait_recv()
    c10.wait_recv()
    t0[1, 0] = total(mine[...], l2[2, 0], l2[3, 0]).astype(bf16)
    e2 = copy(16, t0.at[1, 0, z2], m1.at[2], dzr)
    e3 = copy(17, t0.at[1, 1, z2], m1.at[3], dzl)
    e6 = copy(18, t0.at[1, 1, zr], m2.at[2, 1], dzr)
    e7 = copy(19, t0.at[1, 0, zl], m2.at[3, 0], dzl)
    e0.wait_recv()
    n1[0] = total(t0[0, 0, xr], m1[0]).astype(bf16)
    e8 = copy(20, n1.at[0], m2.at[0, 0], dxr)
    e1.wait_recv()
    n1[1] = total(t0[0, 1, xl], m1[1]).astype(bf16)
    e9 = copy(21, n1.at[1], m2.at[1, 1], dxl)
    e2.wait_recv()
    n1[2] = total(t0[1, 0, zr], m1[2]).astype(bf16)
    e10 = copy(22, n1.at[2], m2.at[2, 0], dzr)
    e3.wait_recv()
    n1[3] = total(t0[1, 1, zl], m1[3]).astype(bf16)
    e11 = copy(23, n1.at[3], m2.at[3, 1], dzl)
    e4.wait_recv()
    e9.wait_recv()
    out_ref[A1] = total(t0[0, 1, x], m2[0, 1], m2[1, 1])
    e5.wait_recv()
    e8.wait_recv()
    out_ref[A0] = total(t0[0, 0, x], m2[0, 0], m2[1, 0])
    e6.wait_recv()
    e11.wait_recv()
    out_ref[B1] = total(t0[1, 1, z], m2[2, 1], m2[3, 1])
    e7.wait_recv()
    e10.wait_recv()
    out_ref[B0] = total(t0[1, 0, z], m2[2, 0], m2[3, 0])
    for c in (c0, c1, c2, c3, c4, c5, c6, c7, c8, c9, c10, c11,
              e0, e1, e2, e3, e4, e5, e6, e7, e8, e9, e10, e11):
        c.wait_send()
    for c in away:
        c.wait_send()


def scatter_sum(x, ident, split=False):
    rows, cols = x.shape[-2] // 16, x.shape[-1]
    q = rows // 4
    piece = (4, q, cols)
    count = 16 if split else 8
    scratch = [pltpu.VMEM((count,) + piece, bf16)]
    if split:
        scratch.append(pltpu.VMEM((16,) + piece, bf16))
    scratch += [
        pltpu.VMEM((4,) + piece, bf16),
        pltpu.VMEM((4,) + piece, bf16),
        pltpu.VMEM((4, 2) + piece, bf16),
        pltpu.VMEM((2, 2) + piece, bf16),
        pltpu.VMEM(piece, bf16),
        pltpu.VMEM(piece, bf16),
        pltpu.VMEM((4, 2, q, cols), bf16),
        pltpu.SemaphoreType.DMA((24,)),
        pltpu.SemaphoreType.DMA((24,)),
        pltpu.SemaphoreType.DMA((count,)),
    ]
    if split:
        scratch += [pltpu.SemaphoreType.DMA((16,)), pltpu.SemaphoreType.DMA((16,))]
    return pl.pallas_call(
        functools.partial(scatter_kernel, split),
        out_shape=jax.ShapeDtypeStruct((rows, cols), f32),
        in_specs=[pl.BlockSpec(memory_space=pl.ANY)],
        out_specs=pl.BlockSpec(memory_space=pltpu.VMEM),
        scratch_shapes=scratch,
        compiler_params=pltpu.CompilerParams(
            collective_id=ident, has_side_effects=True, vmem_limit_bytes=56 << 20),
        name="scatter_split" if split else "scatter_sum",
    )(x.reshape(x.shape[:-2] + (4, 4, rows, cols)))


def spec(shape, index):
    return pl.BlockSpec(shape, index)


def fixed(shape):
    return pl.BlockSpec(shape, lambda *_: (0,) * len(shape), pipeline_mode=pl.Buffered(1))


def whole():
    return pl.BlockSpec(memory_space=pltpu.VMEM)


def local_call(kernel, outs, name, grid=None, in_specs=None, out_specs=None, flops=0, moved=0):
    params = pltpu.CompilerParams(vmem_limit_bytes=52 << 20)
    kinds = dict(
        out_shape=[jax.ShapeDtypeStruct(s, d) for s, d in outs],
        compiler_params=params,
        name=name,
        cost_estimate=pl.CostEstimate(flops=flops, bytes_accessed=moved, transcendentals=0),
    )
    if grid is None:
        kinds["out_specs"] = [spec(s, lambda i, n=len(s): (0,) * n) for s, _ in outs]
        blocks = in_specs or {}

        def call(*args):
            ins = [blocks.get(i) or spec(a.shape, lambda i, n=a.ndim: (0,) * n) for i, a in enumerate(args)]
            return pl.pallas_call(kernel, grid=(1,), in_specs=ins, **kinds)(*args)

        return call
    return pl.pallas_call(kernel, grid=grid, in_specs=in_specs, out_specs=out_specs, **kinds)


def dot(a, b):
    return jnp.dot(a, b, preferred_element_type=f32)


def dot_t(a, b):
    return lax.dot_general(a, b, (((1,), (1,)), ((), ())), preferred_element_type=f32)


def t_dot(a, b):
    return lax.dot_general(a, b, (((0,), (0,)), ((), ())), preferred_element_type=f32)


def lanes(shape):
    return lax.broadcasted_iota(jnp.int32, shape, len(shape) - 1)


def turned(u, cosine, sine):
    chunks = []
    for c in range(u.shape[1] // 128):
        part = u[:, 128 * c : 128 * c + 128]
        low = lax.rem(lanes(part.shape), 64) < 32
        rot = jnp.where(low, -pltpu.roll(part, 96, 1), pltpu.roll(part, 32, 1))
        chunks.append(part * cosine + rot * sine)
    return jnp.concatenate(chunks, axis=1)


def rms(x):
    return lax.rsqrt(jnp.mean(x * x, axis=-1, keepdims=True) + norm_eps)


def halves(w_ref, row):
    return tuple(w_ref[0, h, :, row : row + 64, 0:512].reshape(1024, 512) for h in range(2))


def pre_kernel(x_ref, gain_ref, cos_ref, sin_ref, w_ref, a_ref, q_ref, kv_ref):
    x = x_ref[...].astype(f32)
    a = (x * rms(x) * gain_ref[...]).astype(bf16)
    a_ref[...] = a
    cosine, sine = cos_ref[...], sin_ref[...]
    for h, w in enumerate(halves(w_ref, 0)):
        q_ref[:, 512 * h : 512 * h + 512] = turned(dot(a, w), cosine, sine).astype(bf16)
    wk, wv = halves(w_ref, 64)
    kv_ref[:, :512] = turned(dot(a, wk), cosine, sine).astype(bf16)
    kv_ref[:, 512:] = dot(a, wv).astype(bf16)


def head_rows(q):
    q = q.astype(f32)
    left, right = q[:, :128], q[:, 128:]
    low = lanes(left.shape) < 64
    parts = [
        jnp.where(low, left, 0.0),
        jnp.where(low, pltpu.roll(left, 64, 1), 0.0),
        jnp.where(low, 0.0, pltpu.roll(right, 64, 1)),
        jnp.where(low, 0.0, right),
    ]
    return parts


def head_lanes(p0, p1, p2, p3):
    low = lanes(p0.shape) < 64
    left = jnp.where(low, p0, pltpu.roll(p1, 64, 1))
    right = jnp.where(low, pltpu.roll(p2, 64, 1), p3)
    return jnp.concatenate([left, right], axis=1)


def attend_kernel(q_ref, k_ref, v_ref, lo_ref, hi_ref, o_ref, p_ref):
    key = lax.broadcasted_iota(jnp.int32, (128, 2048), 1)
    seen = (key >= lo_ref[...]) & (key <= hi_ref[...])
    k, v = k_ref[...], v_ref[...]
    outs = []
    for h, q in enumerate(head_rows(q_ref[...])):
        s = dot_t((q * 0.125).astype(bf16), k)
        s = jnp.where(seen, s, masked_score)
        e = jnp.exp(s - jnp.max(s, axis=-1, keepdims=True))
        p = (e * (1.0 / jnp.sum(e, axis=-1, keepdims=True))).astype(bf16)
        p_ref[0, 128 * h : 128 * h + 128, :] = p
        outs.append(dot(p, v))
    o_ref[...] = head_lanes(*outs).astype(bf16)


def attend(q, kv, lo, hi):
    return local_call(
        attend_kernel,
        [((128, 1024), bf16), ((4, 512, 2048), bf16)],
        "attend",
        grid=(4,),
        in_specs=[
            spec((128, 256), lambda i: (0, i)),
            spec((2048, 128), lambda i: (0, i)),
            spec((2048, 128), lambda i: (0, i + 4)),
            fixed((128, 1)),
            fixed((128, 1)),
        ],
        out_specs=[
            spec((128, 256), lambda i: (0, i)),
            spec((1, 512, 2048), lambda i: (i, 0, 0)),
        ],
        flops=2 * 2 * 2048 * 2048 * 128,
        moved=13 << 20,
    )(q, kv, kv, lo, hi)


def attend_back_kernel(q_ref, o_ref, do_ref, k_ref, v_ref, p_ref, dq_ref, dkv_ref):
    k, v = k_ref[...], v_ref[...]
    do = do_ref[...]
    prod = do.astype(f32) * o_ref[...].astype(f32)
    low = lanes((128, 128)) < 64
    left, right = prod[:, :128], prod[:, 128:]
    deltas = [
        jnp.sum(jnp.where(low, left, 0.0), axis=1, keepdims=True),
        jnp.sum(jnp.where(low, 0.0, left), axis=1, keepdims=True),
        jnp.sum(jnp.where(low, right, 0.0), axis=1, keepdims=True),
        jnp.sum(jnp.where(low, 0.0, right), axis=1, keepdims=True),
    ]
    do_rows = [r.astype(bf16) for r in head_rows(do)]
    q_rows = [(r * 0.125).astype(bf16) for r in head_rows(q_ref[...])]
    dqs, dss = [], []
    for h in range(4):
        dp = dot_t(do_rows[h], v)
        p = p_ref[0, 128 * h : 128 * h + 128, :].astype(f32)
        ds = (p * (dp - deltas[h])).astype(bf16)
        dss.append(ds)
        dqs.append(dot(ds, k) * 0.125)
    dq_ref[...] = head_lanes(*dqs)
    dkv_ref[:, :128] = t_dot(jnp.concatenate(dss, axis=0), jnp.concatenate(q_rows, axis=0)).astype(bf16)
    dkv_ref[:, 128:] = t_dot(p_ref[0], jnp.concatenate(do_rows, axis=0)).astype(bf16)


def attend_back(q, o, do, kv, probs):
    side = spec((128, 256), lambda i: (0, i))
    return local_call(
        attend_back_kernel,
        [((128, 1024), f32), ((2048, 1024), bf16)],
        "attend_back",
        grid=(4,),
        in_specs=[
            side,
            side,
            side,
            spec((2048, 128), lambda i: (0, i)),
            spec((2048, 128), lambda i: (0, i + 4)),
            spec((1, 512, 2048), lambda i: (i, 0, 0)),
        ],
        out_specs=[side, spec((2048, 256), lambda i: (0, i))],
        flops=4 * 2 * 2048 * 2048 * 128,
        moved=17 << 20,
    )(q, o, do, kv, kv, probs)


def post_kernel(x_ref, o_ref, wo_ref, gain_ref, h_ref, b_ref):
    o = o_ref[...]
    h = x_ref[...].astype(f32) + jnp.concatenate([dot(o, w) for w in halves(wo_ref, 0)], axis=1)
    h_ref[...] = h
    b_ref[...] = (h * rms(h) * gain_ref[...]).astype(bf16)


def chosen_gates(b, wr, mask):
    logits = dot(b, wr)
    chosen = mask.astype(f32) > 0.5
    top = jnp.max(jnp.where(chosen, logits, masked_score), axis=-1, keepdims=True)
    e = jnp.where(chosen, jnp.exp(jnp.where(chosen, logits - top, 0.0)), 0.0)
    return e / jnp.sum(e, axis=-1, keepdims=True)


SLOTS = 80
ROWS = 1024


def experts_kernel(b_ref, mask_ref, wr_ref, pick_ref, w_ref, y_ref, x_ref, gu_ref, s_ref, gate_ref):
    row, col = lax.broadcasted_iota(jnp.int32, (256, 256), 0), lanes((256, 256))
    before = ((row < col) & ((row < 128) == (col < 128))).astype(bf16)
    slot_ids = lax.broadcasted_iota(jnp.int32, (SLOTS, 256), 0)
    second = jnp.where(lanes((1, 256)) < 128, 0.0, SLOTS // 2)
    for p in range(ROWS // 256):
        b = b_ref[256 * p : 256 * p + 256, :]
        mask = mask_ref[:, 256 * p : 256 * p + 256]
        chosen = mask.astype(f32) > 0.5
        logits = lax.dot_general(wr_ref[...], b, (((0,), (1,)), ((), ())), preferred_element_type=f32)
        top = jnp.max(jnp.where(chosen, logits, masked_score), axis=0, keepdims=True)
        e = jnp.where(chosen, jnp.exp(jnp.where(chosen, logits - top, 0.0)), 0.0)
        gates = e / jnp.sum(e, axis=0, keepdims=True)
        rank = dot(mask, before)
        for j in range(2):
            one = pick_ref[:, j : j + 1]
            gate = jnp.sum(gates * one, axis=0, keepdims=True)
            used = jnp.sum(mask.astype(f32) * one, axis=0, keepdims=True)
            place = jnp.sum(rank * one, axis=0, keepdims=True) + second
            hit = (slot_ids == place.astype(jnp.int32)) & (used > 0.5)
            s = jnp.where(hit, 1.0, 0.0)
            part = slice(SLOTS * p, SLOTS * p + SLOTS)
            gate_ref[j, part, :] = jnp.sum(s * gate, axis=1, keepdims=True)
            s = s.astype(bf16)
            s_ref[p, SLOTS * j : SLOTS * j + SLOTS, :] = s
            x_ref[j, part, :] = dot(s, b).astype(bf16)
    ys = []
    for j in range(2):
        x = x_ref[j]
        g = dot(x, w_ref[j, :, 0:512])
        u = dot(x, w_ref[j, :, 512:1024])
        gu_ref[j, :, 0:512] = g.astype(bf16)
        gu_ref[j, :, 512:1024] = u.astype(bf16)
        inner = g * jax.nn.sigmoid(g) * u
        ys.append(dot_t((inner * gate_ref[j]).astype(bf16), w_ref[j, :, 1024:1536]).astype(bf16))
    for p in range(ROWS // 256):
        part = slice(SLOTS * p, SLOTS * p + SLOTS)
        both = jnp.concatenate([ys[0][part], ys[1][part]], axis=0)
        y_ref[256 * p : 256 * p + 256, :] = t_dot(s_ref[p], both).astype(bf16)


HALF = SLOTS * ROWS // 256
FULL = 2 * HALF


def compact(cols):
    return spec((2, HALF, cols), lambda i: (0, i, 0))


def tokens(cols):
    return spec((ROWS, cols), lambda i: (i, 0))


choice = spec((ROWS // 256, 2 * SLOTS, 256), lambda i: (i, 0, 0))


def experts(b_all, mask_all, wr, pick, w):
    rows = b_all.shape[0]
    return local_call(
        experts_kernel,
        [
            ((rows, 1024), bf16), ((2, FULL, 1024), bf16), ((2, FULL, 1024), bf16),
            ((rows // 256, 2 * SLOTS, 256), bf16), ((2, FULL, 1), f32),
        ],
        "experts",
        grid=(rows // ROWS,),
        in_specs=[
            tokens(1024),
            spec((32, ROWS), lambda i: (0, i)),
            fixed((1024, 32)),
            fixed((32, 8)),
            fixed((2, 1024, 1536)),
        ],
        out_specs=[tokens(1024), compact(1024), compact(1024), choice, compact(1)],
        flops=8 * 2 * 1280 * 1024 * 512,
        moved=20 << 20,
    )(b_all, mask_all, wr, pick, w)


def experts_back_kernel(
    dout_ref, s_ref, gu_ref, gate_ref, wcol_ref, w_ref, db_ref, d_ref, dgu_ref, in_ref, coef_ref
):
    for p in range(ROWS // 256):
        rows = dot(s_ref[p], dout_ref[256 * p : 256 * p + 256, :]).astype(bf16)
        for j in range(2):
            d_ref[j, SLOTS * p : SLOTS * p + SLOTS, :] = rows[SLOTS * j : SLOTS * j + SLOTS]
    dbs = []
    for j in range(2):
        gate = gate_ref[j]
        g = gu_ref[j, :, 0:512].astype(f32)
        u = gu_ref[j, :, 512:1024].astype(f32)
        back = dot(d_ref[j], w_ref[j, :, 1024:1536])
        sig = jax.nn.sigmoid(g)
        silu = g * sig
        inner = silu * u
        coef = gate * jnp.sum(inner * back, axis=1, keepdims=True)
        coef_ref[j] = coef
        in_ref[j] = (inner * gate).astype(bf16)
        dinner = back * gate
        dg = (dinner * u * sig * (1.0 + g * (1.0 - sig))).astype(bf16)
        du = (dinner * silu).astype(bf16)
        dgu_ref[j, :, 0:512] = dg
        dgu_ref[j, :, 512:1024] = du
        db = dot_t(dg, w_ref[j, :, 0:512]) + dot_t(du, w_ref[j, :, 512:1024])
        dbs.append((db + coef * wcol_ref[j : j + 1, :]).astype(bf16))
    for p in range(ROWS // 256):
        part = slice(SLOTS * p, SLOTS * p + SLOTS)
        both = jnp.concatenate([dbs[0][part], dbs[1][part]], axis=0)
        db_ref[256 * p : 256 * p + 256, :] = t_dot(s_ref[p], both).astype(bf16)


def experts_back(dout_all, choices, gu, gate, wcol, w):
    rows = dout_all.shape[0]
    return local_call(
        experts_back_kernel,
        [
            ((rows, 1024), bf16), ((2, FULL, 1024), bf16), ((2, FULL, 1024), bf16),
            ((2, FULL, 512), bf16), ((2, FULL, 1), f32),
        ],
        "experts_back",
        grid=(rows // ROWS,),
        in_specs=[
            tokens(1024), choice, compact(1024), compact(1), fixed((8, 1024)), fixed((2, 1024, 1536)),
        ],
        out_specs=[tokens(1024), compact(1024), compact(1024), compact(512), compact(1)],
        flops=8 * 2 * 1280 * 1024 * 512,
        moved=24 << 20,
    )(dout_all, choices, gu, gate, wcol, w)


def expert_grads_kernel(x_ref, d_ref, dgu_ref, in_ref, out_ref):
    which = pl.program_id(1)

    @pl.when(which < 2)
    def _():
        out_ref[0] = t_dot(x_ref[0], dgu_ref[0]).astype(bf16)

    @pl.when(which == 2)
    def _():
        out_ref[0] = t_dot(d_ref[0], in_ref[0]).astype(bf16)


def expert_grads(x, d, dgu, inner):
    return local_call(
        expert_grads_kernel,
        [((2, 1024, 1536), bf16)],
        "expert_grads",
        grid=(2, 3),
        in_specs=[
            spec((1, FULL, 1024), lambda j, c: (j, 0, 0)),
            spec((1, FULL, 1024), lambda j, c: (j, 0, 0)),
            spec((1, FULL, 512), lambda j, c: (j, 0, jnp.minimum(c, 1))),
            spec((1, FULL, 512), lambda j, c: (j, 0, 0)),
        ],
        out_specs=[spec((1, 1024, 512), lambda j, c: (j, 0, c))],
        flops=3 * 2 * 1280 * 1024 * 512,
        moved=16 << 20,
    )(x, d, dgu, inner)[0]


def mid_back_kernel(
    sum_ref, dout_ref, mix_ref, h_ref, b_ref, gain_ref, wr_ref, mask_ref, wo_ref,
    dh_ref, dattn_ref, do_ref, router_ref, gain_grad_ref,
):
    dout = dout_ref[...].astype(f32)
    b = b_ref[...]
    wr = wr_ref[...]
    h = h_ref[...]
    r = rms(h)
    n = h * r
    gates = chosen_gates(b, wr, mask_ref[...])
    level = jnp.sum(dout * mix_ref[...], axis=-1, keepdims=True)
    taken = (gates * -level).astype(bf16)
    router_ref[...] = t_dot(b, taken)
    db = sum_ref[...] + dot_t(taken, wr)
    gain_grad_ref[...] = jnp.broadcast_to(jnp.sum(db * n, axis=0, keepdims=True), gain_grad_ref.shape)
    ng = db * gain_ref[...]
    dh = dout + r * (ng - n * jnp.mean(ng * n, axis=-1, keepdims=True))
    dh_ref[...] = dh
    dattn = dh.astype(bf16)
    dattn_ref[...] = dattn
    w0, w1 = halves(wo_ref, 0)
    do_ref[...] = (dot_t(dattn[:, :512], w0) + dot_t(dattn[:, 512:], w1)).astype(bf16)


def end_back_kernel(
    dq_ref, dkv_ref, cos_ref, sin_ref, w_ref, x_ref, gain_ref, dh_ref,
    dq_lin_ref, dkv_lin_ref, dx_ref, gain_grad_ref,
):
    cosine, sine = cos_ref[...], -sin_ref[...]
    dq = turned(dq_ref[...], cosine, sine).astype(bf16)
    dkv = dkv_ref[...]
    dk = jnp.concatenate([dkv[:, 256 * i : 256 * i + 128] for i in range(4)], axis=1)
    dv = jnp.concatenate([dkv[:, 256 * i + 128 : 256 * i + 256] for i in range(4)], axis=1)
    dk = turned(dk, cosine, sine).astype(bf16)
    dv = dv.astype(bf16)
    dq_lin_ref[...] = dq
    dkv_lin_ref[:, :512] = dk
    dkv_lin_ref[:, 512:] = dv
    (q0, q1), (wk, wv) = halves(w_ref, 0), halves(w_ref, 64)
    da = dot_t(dq[:, :512], q0) + dot_t(dq[:, 512:], q1) + dot_t(dk, wk) + dot_t(dv, wv)
    x = x_ref[...].astype(f32)
    r = rms(x)
    n = x * r
    gain_grad_ref[...] = jnp.broadcast_to(jnp.sum(da * n, axis=0, keepdims=True), gain_grad_ref.shape)
    ng = da * gain_ref[...]
    dx = dh_ref[...] + r * (ng - n * jnp.mean(ng * n, axis=-1, keepdims=True))
    dx_ref[...] = dx.astype(bf16)


def dense_grads_kernel(a_ref, o_ref, dq_ref, dkv_ref, dattn_ref, *rest):
    small_ref, out_ref = rest if len(rest) == 2 else (None, rest[0])
    a = a_ref[...]
    gq = t_dot(a, dq_ref[...]).astype(bf16)
    gkv = t_dot(a, dkv_ref[...]).astype(bf16)
    go = t_dot(o_ref[...], dattn_ref[...]).astype(bf16)
    for t in range(2):
        part = slice(64 * t, 64 * t + 64)
        for h in range(2):
            side = slice(512 * h, 512 * h + 512)
            out_ref[h, t, 0:64, 0:512] = gq[part, side]
            out_ref[h, t, 64:128, 0:512] = gkv[part, side]
            out_ref[h, t, 128:192, 0:512] = go[part, side]
            if small_ref is not None:
                out_ref[h, t, 0:64, 512:640] = small_ref[h, part, :]
                out_ref[h, t, 64:192, 512:640] = jnp.zeros((128, 128), bf16)


def dense_grads(a, o, dq, dkv, dattn, small=None):
    cols = 512 if small is None else 640
    narrow = spec((128, 128), lambda i: (0, i))
    args = (a, o, dq, dkv, dattn) + (() if small is None else (small,))
    out = local_call(
        dense_grads_kernel,
        [((2, 16, 192, cols), bf16)],
        "dense_grads",
        grid=(8,),
        in_specs=[narrow, narrow] + [fixed((128, 1024))] * 3
        + ([] if small is None else [spec((2, 128, 128), lambda i: (0, i, 0))]),
        out_specs=[spec((2, 2, 192, cols), lambda i: (0, i, 0, 0))],
        flops=3 * 2 * 128 * 1024 * 1024,
        moved=8 << 20,
    )(*args)[0]
    return out.reshape(2, 3072, cols)


def cross_kernel(own_ref, other_ref, out_ref, land, mine, send, recv):
    section, dp = lax.axis_index("section"), lax.axis_index("dp")
    partners = (
        {"section": 1 - section},
        {"dp": lax.rem(dp + 2, 4)},
    )
    barrier = pltpu.get_barrier_semaphore()
    for to in partners:
        pl.semaphore_signal(barrier, inc=1, device_id=to, device_id_type=MESH)
    pl.semaphore_wait(barrier, 2)
    copies = []
    for i, to in enumerate(partners):
        src = other_ref if i == 0 else mine
        c = pltpu.make_async_remote_copy(
            src_ref=src, dst_ref=land.at[i], send_sem=send.at[i], recv_sem=recv.at[i],
            device_id=to, device_id_type=MESH)
        c.start()
        copies.append(c)
        c.wait_recv()
        before = own_ref[...] if i == 0 else mine[...].astype(f32)
        after = (before + land[i].astype(f32)).astype(bf16)
        if i == 0:
            mine[...] = after
        else:
            out_ref[...] = after
    for c in copies:
        c.wait_send()


def cross_sum(own, other, ident):
    rows, cols = own.shape
    return pl.pallas_call(
        cross_kernel,
        out_shape=jax.ShapeDtypeStruct((rows, cols), bf16),
        in_specs=[whole(), whole()],
        out_specs=whole(),
        scratch_shapes=[
            pltpu.VMEM((2, rows, cols), bf16),
            pltpu.VMEM((rows, cols), bf16),
            pltpu.SemaphoreType.DMA((2,)),
            pltpu.SemaphoreType.DMA((2,)),
        ],
        compiler_params=pltpu.CompilerParams(
            collective_id=ident, has_side_effects=True, vmem_limit_bytes=24 << 20),
        name="cross_sum",
    )(own, other)


def qkv_block(layer):
    return spec((1, 2, 16, 128, 640), lambda i: (layer, 0, 0, 0, 0))


def out_block(layer):
    return spec((1, 2, 16, 64, 640), lambda i: (layer, 0, 0, 2, 0))


def forward(x, layer, place, weights, dense, w, masks):
    cosine, sine, lo, hi, pick, _ = place
    gain_attn, gain_moe, wr = dense
    a, q, kv = local_call(
        pre_kernel, [((128, 1024), bf16)] * 3, "pre", in_specs={4: qkv_block(layer)},
        flops=2 * 128 * 1024 * 2048, moved=6 << 20,
    )(x, gain_attn, cosine, sine, weights)
    kv_all = gather_rows(kv, 1)
    o, probs = attend(q, kv_all, lo, hi)
    h, b = local_call(
        post_kernel, [((128, 1024), f32), ((128, 1024), bf16)], "post", in_specs={2: out_block(layer)},
        flops=2 * 128 * 1024 * 1024, moved=4 << 20,
    )(x, o, weights, gain_moe)
    b_all = gather_rows(b, 1)
    y, rows, gu, choices, gate = experts(b_all, masks[1], wr, pick, w)
    mix = scatter_sum(y, 2)
    out = (h + mix).astype(bf16)
    return out, (x, a, q, kv_all, o, probs, h, b, rows, gu, choices, gate, mix)


def backward(dout, saved, layer, place, weights, dense, w, masks):
    cosine, sine, lo, hi, pick, pick_rows = place
    gain_attn, gain_moe, wr = dense
    x, a, q, kv_all, o, probs, h, b, rows, gu, choices, gate, mix = saved
    dout_all = gather_rows(dout, 1)
    wcol = dot_t(pick_rows.astype(bf16), wr)
    db_part, drows, dgu, inner, coef = experts_back(dout_all, choices, gu, gate, wcol, w)
    db_sum = scatter_sum(db_part, 2)
    expert_grad = lax.psum_scatter(
        expert_grads(rows, drows, dgu, inner), "dp", scatter_dimension=1, tiled=True)
    router_cols = jnp.einsum("jrd,jr->jd", rows, coef[:, :, 0].astype(bf16), preferred_element_type=f32)
    router_part = jnp.einsum(
        "jd,je->de", router_cols, pick_rows[:2], preferred_element_type=f32, precision=lax.Precision.HIGHEST)
    dh, dattn, do, router_own, gain_moe_grad = local_call(
        mid_back_kernel,
        [((128, 1024), f32), ((128, 1024), bf16), ((128, 1024), bf16), ((1024, 32), f32), ((8, 1024), f32)],
        "mid_back", in_specs={8: out_block(layer)}, flops=2 * 128 * 1024 * 1024, moved=5 << 20,
    )(db_sum, dout, mix, h, b, gain_moe, wr, masks[0], weights)
    dq, dkv = attend_back(q, o, do, kv_all, probs)
    dkv_sum = scatter_sum(dkv, 2)
    dq_lin, dkv_lin, dx, gain_attn_grad = local_call(
        end_back_kernel,
        [((128, 1024), bf16), ((128, 1024), bf16), ((128, 1024), bf16), ((8, 1024), f32)],
        "end_back", in_specs={4: qkv_block(layer)}, flops=2 * 128 * 1024 * 2048, moved=8 << 20,
    )(dq, dkv_sum, cosine, sine, weights, x, gain_attn, dh)
    small = jnp.concatenate(
        [
            router_part + router_own,
            gain_attn_grad[0][:, None],
            gain_moe_grad[0][:, None],
            jnp.zeros((1024, 30), f32),
        ],
        axis=1,
    ).astype(bf16)
    return dx, expert_grad, (a, o, dq_lin, dkv_lin, dattn), small


def results_kernel(s_ref, query_ref, key_ref, value_ref, out_ref):
    for h in range(2):
        side = slice(512 * h, 512 * h + 512)
        query_ref[:, side] = s_ref[h, :, 0:64, 0:512].reshape(256, 512).astype(f32)
        out_ref[:, side] = s_ref[h, :, 128:192, 0:512].reshape(256, 512).astype(f32)
    key_ref[...] = s_ref[0, :, 64:128, 0:512].reshape(256, 512).astype(f32)
    value_ref[...] = s_ref[1, :, 64:128, 0:512].reshape(256, 512).astype(f32)


def results(summed):
    return local_call(
        results_kernel,
        [((1024, 1024), f32), ((1024, 512), f32), ((1024, 512), f32), ((1024, 1024), f32)],
        "results",
        grid=(4,),
        in_specs=[spec((2, 4, 192, 640), lambda i: (0, i, 0, 0))],
        out_specs=[spec((256, n), lambda i: (i, 0)) for n in (1024, 512, 512, 1024)],
        moved=20 << 20,
    )(summed)


def swapped(x):
    return lax.ppermute(x, "section", [(0, 1), (1, 0)])


def on_device(
    inputs, cotangent, offsets, routes, w_query, w_key, w_value, w_out,
    norm_attn, norm_moe, w_router, w_gate, w_up, w_down,
):
    section = lax.axis_index("section")
    expert = lax.axis_index("expert")
    first = section == 0

    def by_layer(own, other):
        return jnp.where(first, own, other), jnp.where(first, other, own)

    def mine(pair):
        return jnp.where(first, pair[0], pair[1])

    ids = lax.broadcasted_iota(jnp.int32, (1, 1, 1, 32), 3)
    mask_both = jnp.any(routes[0][:, :, :, None] == ids, axis=2).astype(bf16)
    mask_own = mine(mask_both)
    mask_away = jnp.where(first, mask_both[1], mask_both[0])
    start = expert * 64
    left = lax.rem(lax.axis_index("dp"), 2) == 0

    def part(w, there=True):
        if not there:
            return lax.dynamic_slice_in_dim(w, start, 64, axis=0)
        return lax.dynamic_slice(w, (start, jnp.where(left, 0, 512)), (64, 512))

    rows = jnp.concatenate(
        [part(w_query[0]), jnp.where(left, part(w_key[0], False), part(w_value[0], False)), part(w_out[0])],
        axis=0,
    )
    small = jnp.concatenate(
        [part(w_router[0], False), part(norm_attn[0][:, None], False), part(norm_moe[0][:, None], False),
         jnp.zeros((64, 30), bf16)], axis=1)
    extra = jnp.concatenate([mask_away, jnp.zeros((128, 32), bf16)], axis=1)
    extra = jnp.concatenate([extra, small], axis=0)
    extra = jnp.concatenate([extra, jnp.zeros((192, 64), bf16)], axis=1)
    payload = swapped(jnp.concatenate([rows, extra], axis=1))
    mask_other = payload[0:128, 512:544]
    own_rows = jnp.concatenate([mask_own, jnp.zeros((64, 32), bf16)], axis=0)
    payload = jnp.concatenate([payload[:, :576], own_rows, payload[:, 608:]], axis=1)
    shards = jnp.concatenate([w_gate[0], w_up[0], w_down[0]], axis=2)
    weights, away = gather_weights(payload, shards, w_query[0], w_key[0], w_value[0], w_out[0], 3)
    got = jnp.where(
        first,
        jnp.where(left, weights[1, 0, :, :, 512:], weights[1, 1, :, :, 512:]),
        jnp.where(left, weights[0, 0, :, :, 512:], weights[0, 1, :, :, 512:]),
    )
    other_small = got[:, 128:192, 0:64].reshape(1024, 64)
    all_other = got[:, 0:128, 0:32].reshape(2048, 32).T
    all_own = got[:, 0:128, 64:96].reshape(2048, 32).T
    pairs = [
        by_layer(norm_attn.astype(f32), other_small[:, 32][None].astype(f32)),
        by_layer(norm_moe.astype(f32), other_small[:, 33][None].astype(f32)),
        by_layer(w_router[0], other_small[:, :32]),
    ]
    dense = [tuple(p[l] for p in pairs) for l in range(2)]
    masks_own = by_layer(mask_own, mask_other)
    masks_all = by_layer(all_own, all_other)
    masks = [(masks_own[l], masks_all[l]) for l in range(2)]
    expert_w = [lax.all_gather(w, "dp", axis=1, tiled=True) for w in by_layer(shards, away)]

    seq = mine(offsets)
    local = expert * 128 + jnp.arange(128, dtype=jnp.int32)
    steps = jnp.arange(HEAD // 2, dtype=f32) * 2.0 / HEAD
    angles = (local - seq).astype(f32)[:, None] * (rope_base ** (-steps))[None, :]
    cosine = jnp.tile(jnp.cos(angles), (1, 4))
    sine = jnp.tile(jnp.sin(angles), (1, 4))
    pick_rows = (
        lax.broadcasted_iota(jnp.int32, (8, 32), 1)
        == 2 * expert + lax.broadcasted_iota(jnp.int32, (8, 32), 0)
    ).astype(f32)
    place = (cosine, sine, seq[:, None], local[:, None], pick_rows.T, pick_rows)

    x0 = mine(inputs)
    out0, saved0 = forward(x0, 0, place, weights, dense[0], expert_w[0], masks[0])
    out1, saved1 = forward(out0, 1, place, weights, dense[1], expert_w[1], masks[1])
    cot = mine(cotangent)
    dx1, eg1, dg1, small1 = backward(cot, saved1, 1, place, weights, dense[1], expert_w[1], masks[1])
    dense1 = scatter_sum(dense_grads(*dg1), 4, split=True)
    dx0, eg0, dg0, small0 = backward(dx1, saved0, 0, place, weights, dense[0], expert_w[0], masks[0])
    both_small = jnp.pad(jnp.stack([small0, small1]), ((0, 0), (0, 0), (0, 64)))
    dense0 = scatter_sum(dense_grads(*dg0, both_small), 5, split=True)

    def in_place(l0, l1):
        got = swapped(jnp.where(first, l1, l0))
        own = jnp.where(first, l0, l1)
        return jnp.stack([jnp.where(first, own, got), jnp.where(first, got, own)])[None]

    acts = in_place(out0, out1)
    in_grads = in_place(dx0, dx1)

    full1 = jnp.concatenate([dense1, dense0[:, 512:]], axis=1)
    own = jnp.where(first, dense0, full1)
    other = jnp.where(first, full1, dense0).astype(bf16)
    eg_sent = jnp.where(first, eg1, eg0)
    summed, eg_away = gather_split(cross_sum(own, other, 6), eg_sent, 7)
    grad_query, grad_key, grad_value, grad_out = results(summed)
    grad_small = mine(summed[:, :, 0:64, 512:576]).reshape(1024, 64).astype(f32)
    eg = jnp.where(first, eg0, eg1).astype(f32) + eg_away.astype(f32)
    return (
        acts,
        in_grads,
        grad_query[None],
        grad_key[None],
        grad_value[None],
        grad_out[None],
        grad_small[:, 32][None],
        grad_small[:, 33][None],
        grad_small[None, :, :32],
        eg[None, :, :, 0:512],
        eg[None, :, :, 512:1024],
        eg[None, :, :, 1024:1536],
    )


def solution(mesh):
    token = P(None, ("dp", "expert"), None)
    layer_token = P("section", None, ("dp", "expert"), None)
    matrix = P("section", None, None)
    gain = P("section", None)
    expert = P("section", "expert", "dp", None)
    return jax.shard_map(
        on_device,
        mesh=mesh,
        in_specs=(
            token, token, P(None, ("dp", "expert")), layer_token,
            matrix, matrix, matrix, matrix, gain, gain, matrix, expert, expert, expert,
        ),
        out_specs=(
            layer_token, layer_token, matrix, matrix, matrix, matrix, gain, gain, matrix,
            expert, expert, expert,
        ),
        check_vma=False,
    )
```

```python
import functools

import jax
import jax.numpy as jnp
from jax import lax
from jax.experimental import pallas as pl
from jax.experimental.pallas import tpu as pltpu

from jax.sharding import PartitionSpec as P

HEAD = 64
MESH = pl.DeviceIdType.MESH
bf16 = jnp.bfloat16
f32 = jnp.float32
norm_eps = 1e-06
masked_score = -1e30
rope_base = 10000.0


def ring_places():
    me = lax.axis_index("expert")
    z, x = lax.div(me, 4), lax.rem(me, 4)
    xr, xl = lax.rem(x + 1, 4), lax.rem(x + 3, 4)
    zr, zl = lax.rem(z + 1, 4), lax.rem(z + 3, 4)
    near = (z * 4 + xr, z * 4 + xl, zr * 4 + x, zl * 4 + x)
    return z, x, xr, xl, zr, zl, near


def gather_kernel(kind, x_ref, *refs):
    split = kind in ("split", "weights")
    sided = kind in ("swap", "weights")
    if kind == "weights":
        side_ref, wq_ref, wk_ref, wv_ref, wo_ref, out_all, side_out = refs[:7]
    elif sided:
        side_ref, out_all, side_out = refs[:3]
    else:
        out_all = refs[0]
    send, recv, own_sem = refs[-3:]
    z, x, xr, xl, zr, zl, (dxr, dxl, dzr, dzl) = ring_places()
    x2, z2 = lax.rem(x + 2, 4), lax.rem(z + 2, 4)
    section, dp = lax.axis_index("section"), lax.axis_index("dp")
    core = lax.rem(dp, 2)
    rows, cols = x_ref.shape
    half, quarter = rows // 2, rows // 4
    locals_ = []
    if kind == "weights":
        out_ref = out_all.at[1 - section, core]
        moves = (
            (wq_ref.at[:, :, :, pl.ds(0, 512)], 0, 0),
            (wq_ref.at[:, :, :, pl.ds(512, 512)], 1, 0),
            (wk_ref, 0, 64),
            (wv_ref, 1, 64),
            (wo_ref.at[:, :, :, pl.ds(0, 512)], 0, 128),
            (wo_ref.at[:, :, :, pl.ds(512, 512)], 1, 128),
        )
        for i, (src, side, row) in enumerate(moves):
            dst = out_all.at[section, side, :, :, pl.ds(row, 64), pl.ds(0, 512)]
            c = pltpu.make_async_copy(src, dst, own_sem.at[1 + i])
            c.start()
            locals_.append(c)
    elif split:
        out_ref = out_all.at[core]
    else:
        out_ref = out_all
    own = pltpu.make_async_copy(x_ref, out_ref.at[z, x], own_sem.at[0])
    own.start()
    other_core, other_section = {"dp": dp + 1 - 2 * core}, {"section": 1 - section}
    barrier = pltpu.get_barrier_semaphore()
    greeted = [{"expert": d} for d in (dxr, dxl, dzr, dzl)]
    if split:
        greeted.append(other_core)
    if sided:
        greeted.append(other_section)
    for to in greeted:
        pl.semaphore_signal(barrier, inc=1, device_id=to, device_id_type=MESH)
    pl.semaphore_wait(barrier, len(greeted))

    def send_to(i, src, dst, to):
        c = pltpu.make_async_remote_copy(
            src_ref=src, dst_ref=dst, send_sem=send.at[i], recv_sem=recv.at[i],
            device_id=to, device_id_type=MESH)
        c.start()
        return c

    def copy(i, src, dst, to):
        return send_to(i, src, dst, {"expert": to})

    forwards = []

    def forward(*piece):
        if split:
            there = out_ref.at[piece]
            forwards.append(send_to(45 + len(forwards), there, there, other_core))

    A, B = pl.ds(0, half), pl.ds(half, half)
    A0, A1 = pl.ds(0, quarter), pl.ds(quarter, quarter)
    B0, B1 = pl.ds(half, quarter), pl.ds(half + quarter, quarter)
    every = slice(None)
    began = []

    def pair(piece, to_r, to_l, src=None):
        out = []
        for to in (to_r, to_l):
            there = out_ref.at[piece]
            out.append(copy(len(began), there if src is None else src, there, to))
            began.append(out[-1])
        return out

    def single(piece, to):
        there = out_ref.at[piece]
        began.append(copy(len(began), there, there, to))
        return began[-1]

    a_r, a_l = pair((z, x, A), dxr, dxl, x_ref.at[A])
    b_r, b_l = pair((z, x, B), dzr, dzl, x_ref.at[B])
    c_r, c_l = pair((z, x, A), dzr, dzl, x_ref.at[A])
    d_r, d_l = pair((z, x, B), dxr, dxl, x_ref.at[B])
    if sided:
        swap = send_to(44, side_ref, side_out, other_section)
    a_r.wait_recv()
    a2_r = single((z, xl, A0), dxr)
    c1_r, c1_l = pair((z, xl, A), dzr, dzl)
    a_l.wait_recv()
    a2_l = single((z, xr, A1), dxl)
    c2_r, c2_l = pair((z, xr, A), dzr, dzl)
    b_r.wait_recv()
    b2_r = single((zl, x, B0), dzr)
    d1_r, d1_l = pair((zl, x, B), dxr, dxl)
    b_l.wait_recv()
    b2_l = single((zr, x, B1), dzl)
    d2_r, d2_l = pair((zr, x, B), dxr, dxl)
    last = []
    c_r.wait_recv()
    last.append(single((zl, x, A0), dzr))
    c_l.wait_recv()
    last.append(single((zr, x, A1), dzl))
    d_r.wait_recv()
    last.append(single((z, xl, B0), dxr))
    d_l.wait_recv()
    last.append(single((z, xr, B1), dxl))
    a2_r.wait_recv()
    c3_r, c3_l = pair((z, x2, A0), dzr, dzl)
    a2_l.wait_recv()
    c4_r, c4_l = pair((z, x2, A1), dzr, dzl)
    b2_r.wait_recv()
    d3_r, d3_l = pair((z2, x, B0), dxr, dxl)
    b2_l.wait_recv()
    d4_r, d4_l = pair((z2, x, B1), dxr, dxl)
    c1_r.wait_recv()
    last.append(single((zl, xl, A0), dzr))
    c1_l.wait_recv()
    last.append(single((zr, xl, A1), dzl))
    d1_r.wait_recv()
    last.append(single((zl, xl, B0), dxr))
    d1_l.wait_recv()
    last.append(single((zl, xr, B1), dxl))
    own.wait()
    forward(z, every, A)
    forward(every, x, B)
    c2_r.wait_recv()
    last.append(single((zl, xr, A0), dzr))
    c2_l.wait_recv()
    last.append(single((zr, xr, A1), dzl))
    d2_r.wait_recv()
    last.append(single((zr, xl, B0), dxr))
    d2_l.wait_recv()
    last.append(single((zr, xr, B1), dxl))
    c3_r.wait_recv()
    last.append(single((zl, x2, A0), dzr))
    c4_l.wait_recv()
    last.append(single((zr, x2, A1), dzl))
    d3_r.wait_recv()
    last.append(single((z2, xl, B0), dxr))
    d4_l.wait_recv()
    last.append(single((z2, xr, B1), dxl))
    c3_l.wait_recv()
    c4_r.wait_recv()
    forward(zl, every, A)
    forward(zr, every, A)
    d3_l.wait_recv()
    d4_r.wait_recv()
    forward(every, xl, B)
    forward(every, xr, B)
    for c in last:
        c.wait_recv()
    forward(z2, every, A)
    forward(every, x2, B)
    for c in began:
        c.wait_send()
    for c in forwards + ([swap] if sided else []):
        c.wait_recv()
        c.wait_send()
    for c in locals_:
        c.wait()


def gather_call(ident, kind, outs, in_memory, *args):
    anywhere, memory = pl.BlockSpec(memory_space=pl.ANY), pl.BlockSpec(memory_space=pltpu.VMEM)
    return pl.pallas_call(
        functools.partial(gather_kernel, kind),
        out_shape=outs,
        in_specs=[memory if held else anywhere for held in in_memory],
        out_specs=[anywhere] * len(outs),
        scratch_shapes=[
            pltpu.SemaphoreType.DMA((53,)),
            pltpu.SemaphoreType.DMA((53,)),
            pltpu.SemaphoreType.DMA((7,)),
        ],
        compiler_params=pltpu.CompilerParams(
            collective_id=ident, has_side_effects=True, vmem_limit_bytes=56 << 20),
        name="gather_" + kind,
    )(*args)


def gather_rows(x, ident):
    rows, cols = x.shape
    out = gather_call(ident, "plain", [jax.ShapeDtypeStruct((4, 4, rows, cols), x.dtype)], (True,), x)[0]
    return out.reshape(16 * rows, cols)


def gather_swap(x, side, ident):
    rows, cols = x.shape
    out, side_out = gather_call(
        ident, "swap",
        [jax.ShapeDtypeStruct((4, 4, rows, cols), x.dtype), jax.ShapeDtypeStruct(side.shape, side.dtype)],
        (True, False), x, side)
    return out.reshape(16 * rows, cols), side_out


def gather_split(x, ident):
    rows, cols = x.shape
    out = gather_call(ident, "split", [jax.ShapeDtypeStruct((2, 4, 4, rows, cols), x.dtype)], (True,), x)[0]
    return out.reshape(2, 16, rows, cols)


def gather_weights(x, side, wq, wk, wv, wo, ident):
    rows, cols = x.shape
    parts = [w.reshape(4, 4, 64, w.shape[1]) for w in (wq, wk, wv, wo)]
    out, side_out = gather_call(
        ident, "weights",
        [jax.ShapeDtypeStruct((2, 2, 4, 4, rows, cols), x.dtype), jax.ShapeDtypeStruct(side.shape, side.dtype)],
        (True, False) + (True,) * 4, x, side, *parts)
    return out.reshape(2, 2, 16, rows, cols), side_out


def scatter_kernel(split, x_ref, *refs):
    if split:
        side_ref, out_ref, side_out, loc, land = refs[:5]
        core_send, core_recv = refs[-2:]
        refs = refs[5:-2]
    else:
        out_ref, loc = refs[:2]
        refs = refs[2:]
    s1, l1, l2, t0, m1, n1, m2, send, recv, loc_sem = refs
    z, x, xr, xl, zr, zl, (dxr, dxl, dzr, dzl) = ring_places()
    x2, z2 = lax.rem(x + 2, 4), lax.rem(z + 2, 4)
    dp = lax.axis_index("dp")
    core = lax.rem(dp, 2)
    rows = x_ref.shape[-2]
    half, quarter = rows // 2, rows // 4
    A0, A1 = pl.ds(0, quarter), pl.ds(quarter, quarter)
    B0, B1 = pl.ds(half, quarter), pl.ds(half + quarter, quarter)
    every = slice(None)
    pieces = (
        (z2, every, A0), (z2, every, A1), (every, x2, B0), (every, x2, B1),
        (zr, every, A1), (zl, every, A0), (every, xr, B1), (every, xl, B0),
        (zr, every, A0), (zl, every, A1), (every, xr, B0), (every, xl, B1),
        (z, every, A0), (z, every, A1), (every, x, B0), (every, x, B1),
    )
    part = x_ref.at[core] if split else x_ref
    skip = 0 if split else 8
    held = []
    for i, piece in enumerate(pieces[skip:]):
        c = pltpu.make_async_copy(part.at[piece], loc.at[i], loc_sem.at[i])
        c.start()
        held.append(c)
    other_core, other_section = {"dp": dp + 1 - 2 * core}, {"section": 1 - lax.axis_index("section")}
    barrier = pltpu.get_barrier_semaphore()
    greeted = [{"expert": d} for d in (dxr, dxl, dzr, dzl)] + ([other_core, other_section] if split else [])
    for to in greeted:
        pl.semaphore_signal(barrier, inc=1, device_id=to, device_id_type=MESH)
    pl.semaphore_wait(barrier, len(greeted))
    away = []
    if split:
        for i, piece in enumerate(pieces):
            c = pltpu.make_async_remote_copy(
                src_ref=x_ref.at[(1 - core,) + piece], dst_ref=land.at[i], send_sem=core_send.at[i],
                recv_sem=core_recv.at[i], device_id=other_core, device_id_type=MESH)
            c.start()
            away.append(c)
        swap = pltpu.make_async_remote_copy(
            src_ref=side_ref, dst_ref=side_out, send_sem=core_send.at[16], recv_sem=core_recv.at[16],
            device_id=other_section, device_id_type=MESH)
        swap.start()

    def copy(i, src, dst, to):
        c = pltpu.make_async_remote_copy(
            src_ref=src, dst_ref=dst, send_sem=send.at[i], recv_sem=recv.at[i],
            device_id={"expert": to}, device_id_type=MESH)
        c.start()
        return c

    def total(*parts):
        acc = parts[0].astype(f32)
        for p in parts[1:]:
            acc = acc + p.astype(f32)
        return acc

    def ready(i):
        if i < skip:
            return x_ref.at[pieces[i]]
        held[i - skip].wait()
        if split:
            away[i].wait_recv()
            loc[i] = total(loc[i], land[i]).astype(bf16)
        return loc.at[i - skip]

    c0 = copy(0, ready(0), l1.at[0], dzr)
    c1 = copy(1, ready(1), l1.at[1], dzl)
    c2 = copy(2, ready(2), l1.at[2], dxr)
    c3 = copy(3, ready(3), l1.at[3], dxl)
    c4 = copy(4, ready(4), l2.at[0, 1], dzr)
    c5 = copy(5, ready(5), l2.at[1, 0], dzl)
    c6 = copy(6, ready(6), l2.at[2, 1], dxr)
    c7 = copy(7, ready(7), l2.at[3, 0], dxl)
    mine = ready(8)
    c0.wait_recv()
    s1[0] = total(mine[...], l1[0]).astype(bf16)
    c8 = copy(8, s1.at[0], l2.at[0, 0], dzr)
    mine = ready(9)
    c1.wait_recv()
    s1[1] = total(mine[...], l1[1]).astype(bf16)
    c9 = copy(9, s1.at[1], l2.at[1, 1], dzl)
    mine = ready(10)
    c2.wait_recv()
    s1[2] = total(mine[...], l1[2]).astype(bf16)
    c10 = copy(10, s1.at[2], l2.at[2, 0], dxr)
    mine = ready(11)
    c3.wait_recv()
    s1[3] = total(mine[...], l1[3]).astype(bf16)
    c11 = copy(11, s1.at[3], l2.at[3, 1], dxl)
    mine = ready(13)
    c4.wait_recv()
    c9.wait_recv()
    t0[0, 1] = total(mine[...], l2[0, 1], l2[1, 1]).astype(bf16)
    mine = ready(12)
    c5.wait_recv()
    c8.wait_recv()
    t0[0, 0] = total(mine[...], l2[0, 0], l2[1, 0]).astype(bf16)
    e0 = copy(12, t0.at[0, 0, x2], m1.at[0], dxr)
    e1 = copy(13, t0.at[0, 1, x2], m1.at[1], dxl)
    e4 = copy(14, t0.at[0, 1, xr], m2.at[0, 1], dxr)
    e5 = copy(15, t0.at[0, 0, xl], m2.at[1, 0], dxl)
    mine = ready(15)
    c6.wait_recv()
    c11.wait_recv()
    t0[1, 1] = total(mine[...], l2[2, 1], l2[3, 1]).astype(bf16)
    mine = ready(14)
    c7.wait_recv()
    c10.wait_recv()
    t0[1, 0] = total(mine[...], l2[2, 0], l2[3, 0]).astype(bf16)
    e2 = copy(16, t0.at[1, 0, z2], m1.at[2], dzr)
    e3 = copy(17, t0.at[1, 1, z2], m1.at[3], dzl)
    e6 = copy(18, t0.at[1, 1, zr], m2.at[2, 1], dzr)
    e7 = copy(19, t0.at[1, 0, zl], m2.at[3, 0], dzl)
    e0.wait_recv()
    n1[0] = total(t0[0, 0, xr], m1[0]).astype(bf16)
    e8 = copy(20, n1.at[0], m2.at[0, 0], dxr)
    e1.wait_recv()
    n1[1] = total(t0[0, 1, xl], m1[1]).astype(bf16)
    e9 = copy(21, n1.at[1], m2.at[1, 1], dxl)
    e2.wait_recv()
    n1[2] = total(t0[1, 0, zr], m1[2]).astype(bf16)
    e10 = copy(22, n1.at[2], m2.at[2, 0], dzr)
    e3.wait_recv()
    n1[3] = total(t0[1, 1, zl], m1[3]).astype(bf16)
    e11 = copy(23, n1.at[3], m2.at[3, 1], dzl)
    e4.wait_recv()
    e9.wait_recv()
    out_ref[A1] = total(t0[0, 1, x], m2[0, 1], m2[1, 1])
    e5.wait_recv()
    e8.wait_recv()
    out_ref[A0] = total(t0[0, 0, x], m2[0, 0], m2[1, 0])
    e6.wait_recv()
    e11.wait_recv()
    out_ref[B1] = total(t0[1, 1, z], m2[2, 1], m2[3, 1])
    e7.wait_recv()
    e10.wait_recv()
    out_ref[B0] = total(t0[1, 0, z], m2[2, 0], m2[3, 0])
    for c in (c0, c1, c2, c3, c4, c5, c6, c7, c8, c9, c10, c11,
              e0, e1, e2, e3, e4, e5, e6, e7, e8, e9, e10, e11):
        c.wait_send()
    for c in away:
        c.wait_send()
    if split:
        swap.wait_recv()
        swap.wait_send()


def scatter_sum(x, ident, side=None):
    split = side is not None
    anywhere = pl.BlockSpec(memory_space=pl.ANY)
    summed, held = jax.ShapeDtypeStruct((x.shape[-2] // 16, x.shape[-1]), f32), whole()
    rows, cols = x.shape[-2] // 16, x.shape[-1]
    q = rows // 4
    piece = (4, q, cols)
    count = 16 if split else 8
    scratch = [pltpu.VMEM((count,) + piece, bf16)]
    if split:
        scratch.append(pltpu.VMEM((16,) + piece, bf16))
    scratch += [
        pltpu.VMEM((4,) + piece, bf16),
        pltpu.VMEM((4,) + piece, bf16),
        pltpu.VMEM((4, 2) + piece, bf16),
        pltpu.VMEM((2, 2) + piece, bf16),
        pltpu.VMEM(piece, bf16),
        pltpu.VMEM(piece, bf16),
        pltpu.VMEM((4, 2, q, cols), bf16),
        pltpu.SemaphoreType.DMA((24,)),
        pltpu.SemaphoreType.DMA((24,)),
        pltpu.SemaphoreType.DMA((count,)),
    ]
    if split:
        scratch += [pltpu.SemaphoreType.DMA((17,)), pltpu.SemaphoreType.DMA((17,))]
    return pl.pallas_call(
        functools.partial(scatter_kernel, split),
        out_shape=[summed, jax.ShapeDtypeStruct(side.shape, side.dtype)] if split else summed,
        in_specs=[anywhere] * (2 if split else 1),
        out_specs=[held, anywhere] if split else held,
        scratch_shapes=scratch,
        compiler_params=pltpu.CompilerParams(
            collective_id=ident, has_side_effects=True, vmem_limit_bytes=56 << 20),
        name="scatter_split" if split else "scatter_sum",
    )(x.reshape(x.shape[:-2] + (4, 4, rows, cols)), *([side] if split else []))


def spec(shape, index):
    return pl.BlockSpec(shape, index)


def fixed(shape):
    return pl.BlockSpec(shape, lambda *_: (0,) * len(shape), pipeline_mode=pl.Buffered(1))


def whole():
    return pl.BlockSpec(memory_space=pltpu.VMEM)


def local_call(kernel, outs, name, grid=None, in_specs=None, out_specs=None, flops=0, moved=0):
    params = pltpu.CompilerParams(vmem_limit_bytes=52 << 20)
    kinds = dict(
        out_shape=[jax.ShapeDtypeStruct(s, d) for s, d in outs],
        compiler_params=params,
        name=name,
        cost_estimate=pl.CostEstimate(flops=flops, bytes_accessed=moved, transcendentals=0),
    )
    if grid is None:
        kinds["out_specs"] = [spec(s, lambda i, n=len(s): (0,) * n) for s, _ in outs]
        blocks = in_specs or {}

        def call(*args):
            ins = [blocks.get(i) or spec(a.shape, lambda i, n=a.ndim: (0,) * n) for i, a in enumerate(args)]
            return pl.pallas_call(kernel, grid=(1,), in_specs=ins, **kinds)(*args)

        return call
    return pl.pallas_call(kernel, grid=grid, in_specs=in_specs, out_specs=out_specs, **kinds)


def dot(a, b):
    return jnp.dot(a, b, preferred_element_type=f32)


def dot_t(a, b):
    return lax.dot_general(a, b, (((1,), (1,)), ((), ())), preferred_element_type=f32)


def t_dot(a, b):
    return lax.dot_general(a, b, (((0,), (0,)), ((), ())), preferred_element_type=f32)


def lanes(shape):
    return lax.broadcasted_iota(jnp.int32, shape, len(shape) - 1)


def turned(u, cosine, sine):
    chunks = []
    for c in range(u.shape[1] // 128):
        part = u[:, 128 * c : 128 * c + 128]
        low = lax.rem(lanes(part.shape), 64) < 32
        rot = jnp.where(low, -pltpu.roll(part, 96, 1), pltpu.roll(part, 32, 1))
        chunks.append(part * cosine + rot * sine)
    return jnp.concatenate(chunks, axis=1)


def rms(x):
    return lax.rsqrt(jnp.mean(x * x, axis=-1, keepdims=True) + norm_eps)


def halves(w_ref, row):
    return tuple(w_ref[0, h, :, row : row + 64, 0:512].reshape(1024, 512) for h in range(2))


def pre_kernel(x_ref, gain_ref, cos_ref, sin_ref, w_ref, a_ref, q_ref, kv_ref):
    x = x_ref[...].astype(f32)
    a = (x * rms(x) * gain_ref[...]).astype(bf16)
    a_ref[...] = a
    cosine, sine = cos_ref[...], sin_ref[...]
    for h, w in enumerate(halves(w_ref, 0)):
        q_ref[:, 512 * h : 512 * h + 512] = turned(dot(a, w), cosine, sine).astype(bf16)
    wk, wv = halves(w_ref, 64)
    kv_ref[:, :512] = turned(dot(a, wk), cosine, sine).astype(bf16)
    kv_ref[:, 512:] = dot(a, wv).astype(bf16)


def head_rows(q):
    q = q.astype(f32)
    left, right = q[:, :128], q[:, 128:]
    low = lanes(left.shape) < 64
    parts = [
        jnp.where(low, left, 0.0),
        jnp.where(low, pltpu.roll(left, 64, 1), 0.0),
        jnp.where(low, 0.0, pltpu.roll(right, 64, 1)),
        jnp.where(low, 0.0, right),
    ]
    return parts


def head_lanes(p0, p1, p2, p3):
    low = lanes(p0.shape) < 64
    left = jnp.where(low, p0, pltpu.roll(p1, 64, 1))
    right = jnp.where(low, pltpu.roll(p2, 64, 1), p3)
    return jnp.concatenate([left, right], axis=1)


def attend_kernel(q_ref, k_ref, v_ref, lo_ref, hi_ref, o_ref, p_ref):
    key = lax.broadcasted_iota(jnp.int32, (128, 2048), 1)
    seen = (key >= lo_ref[...]) & (key <= hi_ref[...])
    k, v = k_ref[...], v_ref[...]
    outs = []
    for h, q in enumerate(head_rows(q_ref[...])):
        s = dot_t((q * 0.125).astype(bf16), k)
        s = jnp.where(seen, s, masked_score)
        e = jnp.exp(s - jnp.max(s, axis=-1, keepdims=True))
        p = (e * (1.0 / jnp.sum(e, axis=-1, keepdims=True))).astype(bf16)
        p_ref[0, 128 * h : 128 * h + 128, :] = p
        outs.append(dot(p, v))
    o_ref[...] = head_lanes(*outs).astype(bf16)


def attend(q, kv, lo, hi):
    return local_call(
        attend_kernel,
        [((128, 1024), bf16), ((4, 512, 2048), bf16)],
        "attend",
        grid=(4,),
        in_specs=[
            spec((128, 256), lambda i: (0, i)),
            spec((2048, 128), lambda i: (0, i)),
            spec((2048, 128), lambda i: (0, i + 4)),
            fixed((128, 1)),
            fixed((128, 1)),
        ],
        out_specs=[
            spec((128, 256), lambda i: (0, i)),
            spec((1, 512, 2048), lambda i: (i, 0, 0)),
        ],
        flops=2 * 2 * 2048 * 2048 * 128,
        moved=13 << 20,
    )(q, kv, kv, lo, hi)


def attend_back_kernel(q_ref, o_ref, do_ref, k_ref, v_ref, p_ref, dq_ref, dkv_ref):
    k, v = k_ref[...], v_ref[...]
    do = do_ref[...]
    prod = do.astype(f32) * o_ref[...].astype(f32)
    low = lanes((128, 128)) < 64
    left, right = prod[:, :128], prod[:, 128:]
    deltas = [
        jnp.sum(jnp.where(low, left, 0.0), axis=1, keepdims=True),
        jnp.sum(jnp.where(low, 0.0, left), axis=1, keepdims=True),
        jnp.sum(jnp.where(low, right, 0.0), axis=1, keepdims=True),
        jnp.sum(jnp.where(low, 0.0, right), axis=1, keepdims=True),
    ]
    do_rows = [r.astype(bf16) for r in head_rows(do)]
    q_rows = [(r * 0.125).astype(bf16) for r in head_rows(q_ref[...])]
    dqs, dss = [], []
    for h in range(4):
        dp = dot_t(do_rows[h], v)
        p = p_ref[0, 128 * h : 128 * h + 128, :].astype(f32)
        ds = (p * (dp - deltas[h])).astype(bf16)
        dss.append(ds)
        dqs.append(dot(ds, k) * 0.125)
    dq_ref[...] = head_lanes(*dqs)
    dkv_ref[:, :128] = t_dot(jnp.concatenate(dss, axis=0), jnp.concatenate(q_rows, axis=0)).astype(bf16)
    dkv_ref[:, 128:] = t_dot(p_ref[0], jnp.concatenate(do_rows, axis=0)).astype(bf16)


def attend_back(q, o, do, kv, probs):
    side = spec((128, 256), lambda i: (0, i))
    return local_call(
        attend_back_kernel,
        [((128, 1024), f32), ((2048, 1024), bf16)],
        "attend_back",
        grid=(4,),
        in_specs=[
            side,
            side,
            side,
            spec((2048, 128), lambda i: (0, i)),
            spec((2048, 128), lambda i: (0, i + 4)),
            spec((1, 512, 2048), lambda i: (i, 0, 0)),
        ],
        out_specs=[side, spec((2048, 256), lambda i: (0, i))],
        flops=4 * 2 * 2048 * 2048 * 128,
        moved=17 << 20,
    )(q, o, do, kv, kv, probs)


def post_kernel(x_ref, o_ref, wo_ref, gain_ref, h_ref, b_ref):
    o = o_ref[...]
    h = x_ref[...].astype(f32) + jnp.concatenate([dot(o, w) for w in halves(wo_ref, 0)], axis=1)
    h_ref[...] = h
    b_ref[...] = (h * rms(h) * gain_ref[...]).astype(bf16)


def chosen_gates(b, wr, mask):
    logits = dot(b, wr)
    chosen = mask.astype(f32) > 0.5
    top = jnp.max(jnp.where(chosen, logits, masked_score), axis=-1, keepdims=True)
    e = jnp.where(chosen, jnp.exp(jnp.where(chosen, logits - top, 0.0)), 0.0)
    return e / jnp.sum(e, axis=-1, keepdims=True)


SLOTS = 80
ROWS = 1024


def experts_kernel(b_ref, mask_ref, wr_ref, pick_ref, w0_ref, w1_ref, y_ref, x_ref, gu_ref, s_ref, gate_ref):
    row, col = lax.broadcasted_iota(jnp.int32, (256, 256), 0), lanes((256, 256))
    before = ((row < col) & ((row < 128) == (col < 128))).astype(bf16)
    slot_ids = lax.broadcasted_iota(jnp.int32, (SLOTS, 256), 0)
    second = jnp.where(lanes((1, 256)) < 128, 0.0, SLOTS // 2)
    for p in range(ROWS // 256):
        b = b_ref[256 * p : 256 * p + 256, :]
        mask = mask_ref[:, 256 * p : 256 * p + 256]
        chosen = mask.astype(f32) > 0.5
        logits = lax.dot_general(wr_ref[...], b, (((0,), (1,)), ((), ())), preferred_element_type=f32)
        top = jnp.max(jnp.where(chosen, logits, masked_score), axis=0, keepdims=True)
        e = jnp.where(chosen, jnp.exp(jnp.where(chosen, logits - top, 0.0)), 0.0)
        gates = e / jnp.sum(e, axis=0, keepdims=True)
        rank = dot(mask, before)
        for j in range(2):
            one = pick_ref[:, j : j + 1]
            gate = jnp.sum(gates * one, axis=0, keepdims=True)
            used = jnp.sum(mask.astype(f32) * one, axis=0, keepdims=True)
            place = jnp.sum(rank * one, axis=0, keepdims=True) + second
            hit = (slot_ids == place.astype(jnp.int32)) & (used > 0.5)
            s = jnp.where(hit, 1.0, 0.0)
            part = slice(SLOTS * p, SLOTS * p + SLOTS)
            gate_ref[j, part, :] = jnp.sum(s * gate, axis=1, keepdims=True)
            s = s.astype(bf16)
            s_ref[p, SLOTS * j : SLOTS * j + SLOTS, :] = s
            x_ref[j, part, :] = dot(s, b).astype(bf16)
    ys = []
    for j in range(2):
        x = x_ref[j]
        g = dot(x, (w0_ref, w1_ref)[j][0, :, 0:512])
        u = dot(x, (w0_ref, w1_ref)[j][0, :, 512:1024])
        gu_ref[j, :, 0:512] = g.astype(bf16)
        gu_ref[j, :, 512:1024] = u.astype(bf16)
        inner = g * jax.nn.sigmoid(g) * u
        ys.append(dot_t((inner * gate_ref[j]).astype(bf16), (w0_ref, w1_ref)[j][0, :, 1024:1536]).astype(bf16))
    for p in range(ROWS // 256):
        part = slice(SLOTS * p, SLOTS * p + SLOTS)
        both = jnp.concatenate([ys[0][part], ys[1][part]], axis=0)
        y_ref[256 * p : 256 * p + 256, :] = t_dot(s_ref[p], both).astype(bf16)


HALF = SLOTS * ROWS // 256
FULL = 2 * HALF


def compact(cols):
    return spec((2, HALF, cols), lambda i: (0, i, 0))


def tokens(cols):
    return spec((ROWS, cols), lambda i: (i, 0))


choice = spec((ROWS // 256, 2 * SLOTS, 256), lambda i: (i, 0, 0))


def experts(b_all, mask_all, wr, pick, w):
    rows = b_all.shape[0]
    return local_call(
        experts_kernel,
        [
            ((rows, 1024), bf16), ((2, FULL, 1024), bf16), ((2, FULL, 1024), bf16),
            ((rows // 256, 2 * SLOTS, 256), bf16), ((2, FULL, 1), f32),
        ],
        "experts",
        grid=(rows // ROWS,),
        in_specs=[
            tokens(1024),
            spec((32, ROWS), lambda i: (0, i)),
            fixed((1024, 32)),
            fixed((32, 8)),
            fixed((1, 1024, 1536)),
            fixed((1, 1024, 1536)),
        ],
        out_specs=[tokens(1024), compact(1024), compact(1024), choice, compact(1)],
        flops=8 * 2 * 1280 * 1024 * 512,
        moved=20 << 20,
    )(b_all, mask_all, wr, pick, *w)


def experts_back_kernel(
    dout_ref, s_ref, gu_ref, gate_ref, wcol_ref, w0_ref, w1_ref, db_ref, d_ref, dgu_ref, in_ref, coef_ref
):
    for p in range(ROWS // 256):
        rows = dot(s_ref[p], dout_ref[256 * p : 256 * p + 256, :]).astype(bf16)
        for j in range(2):
            d_ref[j, SLOTS * p : SLOTS * p + SLOTS, :] = rows[SLOTS * j : SLOTS * j + SLOTS]
    dbs = []
    for j in range(2):
        gate = gate_ref[j]
        g = gu_ref[j, :, 0:512].astype(f32)
        u = gu_ref[j, :, 512:1024].astype(f32)
        back = dot(d_ref[j], (w0_ref, w1_ref)[j][0, :, 1024:1536])
        sig = jax.nn.sigmoid(g)
        silu = g * sig
        inner = silu * u
        coef = gate * jnp.sum(inner * back, axis=1, keepdims=True)
        coef_ref[j] = coef
        in_ref[j] = (inner * gate).astype(bf16)
        dinner = back * gate
        dg = (dinner * u * sig * (1.0 + g * (1.0 - sig))).astype(bf16)
        du = (dinner * silu).astype(bf16)
        dgu_ref[j, :, 0:512] = dg
        dgu_ref[j, :, 512:1024] = du
        db = dot_t(dg, (w0_ref, w1_ref)[j][0, :, 0:512]) + dot_t(du, (w0_ref, w1_ref)[j][0, :, 512:1024])
        dbs.append((db + coef * wcol_ref[j : j + 1, :]).astype(bf16))
    for p in range(ROWS // 256):
        part = slice(SLOTS * p, SLOTS * p + SLOTS)
        both = jnp.concatenate([dbs[0][part], dbs[1][part]], axis=0)
        db_ref[256 * p : 256 * p + 256, :] = t_dot(s_ref[p], both).astype(bf16)


def experts_back(dout_all, choices, gu, gate, wcol, w):
    rows = dout_all.shape[0]
    return local_call(
        experts_back_kernel,
        [
            ((rows, 1024), bf16), ((2, FULL, 1024), bf16), ((2, FULL, 1024), bf16),
            ((2, FULL, 512), bf16), ((2, FULL, 1), f32),
        ],
        "experts_back",
        grid=(rows // ROWS,),
        in_specs=[
            tokens(1024), choice, compact(1024), compact(1), fixed((8, 1024)), fixed((1, 1024, 1536)),
            fixed((1, 1024, 1536)),
        ],
        out_specs=[tokens(1024), compact(1024), compact(1024), compact(512), compact(1)],
        flops=8 * 2 * 1280 * 1024 * 512,
        moved=24 << 20,
    )(dout_all, choices, gu, gate, wcol, *w)


def expert_grads_kernel(x_ref, d_ref, dgu_ref, in_ref, out_ref):
    which = pl.program_id(1)

    @pl.when(which < 2)
    def _():
        out_ref[0] = t_dot(x_ref[0], dgu_ref[0]).astype(bf16)

    @pl.when(which == 2)
    def _():
        out_ref[0] = t_dot(d_ref[0], in_ref[0]).astype(bf16)


def expert_grads(x, d, dgu, inner):
    return local_call(
        expert_grads_kernel,
        [((2, 1024, 1536), bf16)],
        "expert_grads",
        grid=(2, 3),
        in_specs=[
            spec((1, FULL, 1024), lambda j, c: (j, 0, 0)),
            spec((1, FULL, 1024), lambda j, c: (j, 0, 0)),
            spec((1, FULL, 512), lambda j, c: (j, 0, jnp.minimum(c, 1))),
            spec((1, FULL, 512), lambda j, c: (j, 0, 0)),
        ],
        out_specs=[spec((1, 1024, 512), lambda j, c: (j, 0, c))],
        flops=3 * 2 * 1280 * 1024 * 512,
        moved=16 << 20,
    )(x, d, dgu, inner)[0]


def mid_back_kernel(
    sum_ref, dout_ref, mix_ref, h_ref, b_ref, gain_ref, wr_ref, mask_ref, wo_ref,
    dh_ref, dattn_ref, do_ref, router_ref, gain_grad_ref,
):
    dout = dout_ref[...].astype(f32)
    b = b_ref[...]
    wr = wr_ref[...]
    h = h_ref[...]
    r = rms(h)
    n = h * r
    gates = chosen_gates(b, wr, mask_ref[...])
    level = jnp.sum(dout * mix_ref[...], axis=-1, keepdims=True)
    taken = (gates * -level).astype(bf16)
    router_ref[...] = t_dot(b, taken)
    db = sum_ref[...] + dot_t(taken, wr)
    gain_grad_ref[...] = jnp.broadcast_to(jnp.sum(db * n, axis=0, keepdims=True), gain_grad_ref.shape)
    ng = db * gain_ref[...]
    dh = dout + r * (ng - n * jnp.mean(ng * n, axis=-1, keepdims=True))
    dh_ref[...] = dh
    dattn = dh.astype(bf16)
    dattn_ref[...] = dattn
    w0, w1 = halves(wo_ref, 0)
    do_ref[...] = (dot_t(dattn[:, :512], w0) + dot_t(dattn[:, 512:], w1)).astype(bf16)


def end_back_kernel(
    dq_ref, dkv_ref, cos_ref, sin_ref, w_ref, x_ref, gain_ref, dh_ref,
    dq_lin_ref, dkv_lin_ref, dx_ref, gain_grad_ref,
):
    cosine, sine = cos_ref[...], -sin_ref[...]
    dq = turned(dq_ref[...], cosine, sine).astype(bf16)
    dkv = dkv_ref[...]
    dk = jnp.concatenate([dkv[:, 256 * i : 256 * i + 128] for i in range(4)], axis=1)
    dv = jnp.concatenate([dkv[:, 256 * i + 128 : 256 * i + 256] for i in range(4)], axis=1)
    dk = turned(dk, cosine, sine).astype(bf16)
    dv = dv.astype(bf16)
    dq_lin_ref[...] = dq
    dkv_lin_ref[:, :512] = dk
    dkv_lin_ref[:, 512:] = dv
    (q0, q1), (wk, wv) = halves(w_ref, 0), halves(w_ref, 64)
    da = dot_t(dq[:, :512], q0) + dot_t(dq[:, 512:], q1) + dot_t(dk, wk) + dot_t(dv, wv)
    x = x_ref[...].astype(f32)
    r = rms(x)
    n = x * r
    gain_grad_ref[...] = jnp.broadcast_to(jnp.sum(da * n, axis=0, keepdims=True), gain_grad_ref.shape)
    ng = da * gain_ref[...]
    dx = dh_ref[...] + r * (ng - n * jnp.mean(ng * n, axis=-1, keepdims=True))
    dx_ref[...] = dx.astype(bf16)


def dense_grads_kernel(*refs):
    small_ref, out_ref = refs[10:]
    for layer in range(2):
        a_ref, o_ref, dq_ref, dkv_ref, dattn_ref = refs[5 * layer : 5 * layer + 5]
        a = a_ref[...]
        gq = t_dot(a, dq_ref[...]).astype(bf16)
        gkv = t_dot(a, dkv_ref[...]).astype(bf16)
        go = t_dot(o_ref[...], dattn_ref[...]).astype(bf16)
        cols = slice(512 * layer, 512 * layer + 512)
        for t in range(2):
            part = slice(64 * t, 64 * t + 64)
            for h in range(2):
                side = slice(512 * h, 512 * h + 512)
                out_ref[h, t, 0:64, cols] = gq[part, side]
                out_ref[h, t, 64:128, cols] = gkv[part, side]
                out_ref[h, t, 128:192, cols] = go[part, side]
    for t in range(2):
        for h in range(2):
            out_ref[h, t, 0:64, 1024:1152] = small_ref[h, 64 * t : 64 * t + 64, :]
            out_ref[h, t, 64:192, 1024:1152] = jnp.zeros((128, 128), bf16)


def dense_grads(layer0, layer1, small):
    narrow = spec((128, 128), lambda i: (0, i))
    out = local_call(
        dense_grads_kernel,
        [((2, 16, 192, 1152), bf16)],
        "dense_grads",
        grid=(8,),
        in_specs=([narrow, narrow] + [fixed((128, 1024))] * 3) * 2 + [spec((2, 128, 128), lambda i: (0, i, 0))],
        out_specs=[spec((2, 2, 192, 1152), lambda i: (0, i, 0, 0))],
        flops=6 * 2 * 128 * 1024 * 1024,
        moved=18 << 20,
    )(*layer0, *layer1, small)[0]
    return out.reshape(2, 3072, 1152)


def cross_kernel(own_ref, other_ref, out_ref, land, mine, send, recv):
    section, dp = lax.axis_index("section"), lax.axis_index("dp")
    partners = (
        {"section": 1 - section},
        {"dp": lax.rem(dp + 2, 4)},
    )
    barrier = pltpu.get_barrier_semaphore()
    for to in partners:
        pl.semaphore_signal(barrier, inc=1, device_id=to, device_id_type=MESH)
    pl.semaphore_wait(barrier, 2)
    copies = []
    for i, to in enumerate(partners):
        src = other_ref if i == 0 else mine
        c = pltpu.make_async_remote_copy(
            src_ref=src, dst_ref=land.at[i], send_sem=send.at[i], recv_sem=recv.at[i],
            device_id=to, device_id_type=MESH)
        c.start()
        copies.append(c)
        c.wait_recv()
        before = own_ref[...] if i == 0 else mine[...].astype(f32)
        after = (before + land[i].astype(f32)).astype(bf16)
        if i == 0:
            mine[...] = after
        else:
            out_ref[...] = after
    for c in copies:
        c.wait_send()


def cross_sum(own, other, ident):
    rows, cols = own.shape
    return pl.pallas_call(
        cross_kernel,
        out_shape=jax.ShapeDtypeStruct((rows, cols), bf16),
        in_specs=[whole(), whole()],
        out_specs=whole(),
        scratch_shapes=[
            pltpu.VMEM((2, rows, cols), bf16),
            pltpu.VMEM((rows, cols), bf16),
            pltpu.SemaphoreType.DMA((2,)),
            pltpu.SemaphoreType.DMA((2,)),
        ],
        compiler_params=pltpu.CompilerParams(
            collective_id=ident, has_side_effects=True, vmem_limit_bytes=24 << 20),
        name="cross_sum",
    )(own, other)


def qkv_block(layer):
    return spec((1, 2, 16, 128, 640), lambda i: (layer, 0, 0, 0, 0))


def out_block(layer):
    return spec((1, 2, 16, 64, 640), lambda i: (layer, 0, 0, 2, 0))


def forward(x, layer, place, weights, dense, w, masks):
    cosine, sine, lo, hi, pick, _ = place
    gain_attn, gain_moe, wr = dense
    a, q, kv = local_call(
        pre_kernel, [((128, 1024), bf16)] * 3, "pre", in_specs={4: qkv_block(layer)},
        flops=2 * 128 * 1024 * 2048, moved=6 << 20,
    )(x, gain_attn, cosine, sine, weights)
    if callable(w):
        kv_all, w = w(kv)
    else:
        kv_all = gather_rows(kv, 1)
    o, probs = attend(q, kv_all, lo, hi)
    h, b = local_call(
        post_kernel, [((128, 1024), f32), ((128, 1024), bf16)], "post", in_specs={2: out_block(layer)},
        flops=2 * 128 * 1024 * 1024, moved=4 << 20,
    )(x, o, weights, gain_moe)
    b_all = gather_rows(b, 1)
    y, rows, gu, choices, gate = experts(b_all, masks[1], wr, pick, w)
    mix = scatter_sum(y, 2)
    out = (h + mix).astype(bf16)
    return out, w, (x, a, q, kv_all, o, probs, h, b, rows, gu, choices, gate, mix)


def backward(dout, dout_all, saved, layer, place, weights, dense, w, masks):
    cosine, sine, lo, hi, pick, pick_rows = place
    gain_attn, gain_moe, wr = dense
    x, a, q, kv_all, o, probs, h, b, rows, gu, choices, gate, mix = saved
    if dout_all is None:
        dout_all = gather_rows(dout, 1)
    wcol = dot_t(pick_rows.astype(bf16), wr)
    db_part, drows, dgu, inner, coef = experts_back(dout_all, choices, gu, gate, wcol, w)
    db_sum = scatter_sum(db_part, 2)
    expert_grad = lax.psum_scatter(
        expert_grads(rows, drows, dgu, inner), "dp", scatter_dimension=1, tiled=True)
    router_cols = jnp.einsum("jrd,jr->jd", rows, coef[:, :, 0].astype(bf16), preferred_element_type=f32)
    router_part = jnp.einsum(
        "jd,je->de", router_cols, pick_rows[:2], preferred_element_type=f32, precision=lax.Precision.HIGHEST)
    dh, dattn, do, router_own, gain_moe_grad = local_call(
        mid_back_kernel,
        [((128, 1024), f32), ((128, 1024), bf16), ((128, 1024), bf16), ((1024, 32), f32), ((8, 1024), f32)],
        "mid_back", in_specs={8: out_block(layer)}, flops=2 * 128 * 1024 * 1024, moved=5 << 20,
    )(db_sum, dout, mix, h, b, gain_moe, wr, masks[0], weights)
    dq, dkv = attend_back(q, o, do, kv_all, probs)
    dkv_sum = scatter_sum(dkv, 2)
    dq_lin, dkv_lin, dx, gain_attn_grad = local_call(
        end_back_kernel,
        [((128, 1024), bf16), ((128, 1024), bf16), ((128, 1024), bf16), ((8, 1024), f32)],
        "end_back", in_specs={4: qkv_block(layer)}, flops=2 * 128 * 1024 * 2048, moved=8 << 20,
    )(dq, dkv_sum, cosine, sine, weights, x, gain_attn, dh)
    small = jnp.concatenate(
        [
            router_part + router_own,
            gain_attn_grad[0][:, None],
            gain_moe_grad[0][:, None],
            jnp.zeros((1024, 30), f32),
        ],
        axis=1,
    ).astype(bf16)
    return dx, expert_grad, (a, o, dq_lin, dkv_lin, dattn), small


def results_kernel(s_ref, query_ref, key_ref, value_ref, out_ref):
    for h in range(2):
        side = slice(512 * h, 512 * h + 512)
        query_ref[:, side] = s_ref[h, :, 0:64, 0:512].reshape(256, 512).astype(f32)
        out_ref[:, side] = s_ref[h, :, 128:192, 0:512].reshape(256, 512).astype(f32)
    key_ref[...] = s_ref[0, :, 64:128, 0:512].reshape(256, 512).astype(f32)
    value_ref[...] = s_ref[1, :, 64:128, 0:512].reshape(256, 512).astype(f32)


def results(summed):
    return local_call(
        results_kernel,
        [((1024, 1024), f32), ((1024, 512), f32), ((1024, 512), f32), ((1024, 1024), f32)],
        "results",
        grid=(4,),
        in_specs=[spec((2, 4, 192, 640), lambda i: (0, i, 0, 0))],
        out_specs=[spec((256, n), lambda i: (i, 0)) for n in (1024, 512, 512, 1024)],
        moved=20 << 20,
    )(summed)


def swapped(x):
    return lax.ppermute(x, "section", [(0, 1), (1, 0)])


def on_device(
    inputs, cotangent, offsets, routes, w_query, w_key, w_value, w_out,
    norm_attn, norm_moe, w_router, w_gate, w_up, w_down,
):
    section = lax.axis_index("section")
    expert = lax.axis_index("expert")
    first = section == 0

    def by_layer(own, other):
        return jnp.where(first, own, other), jnp.where(first, other, own)

    def mine(pair):
        return jnp.where(first, pair[0], pair[1])

    ids = lax.broadcasted_iota(jnp.int32, (1, 1, 1, 32), 3)
    mask_both = jnp.any(routes[0][:, :, :, None] == ids, axis=2).astype(bf16)
    mask_own = mine(mask_both)
    mask_away = jnp.where(first, mask_both[1], mask_both[0])
    start = expert * 64
    left = lax.rem(lax.axis_index("dp"), 2) == 0

    def part(w, there=True):
        if not there:
            return lax.dynamic_slice_in_dim(w, start, 64, axis=0)
        return lax.dynamic_slice(w, (start, jnp.where(left, 0, 512)), (64, 512))

    rows = jnp.concatenate(
        [part(w_query[0]), jnp.where(left, part(w_key[0], False), part(w_value[0], False)), part(w_out[0])],
        axis=0,
    )
    small = jnp.concatenate(
        [part(w_router[0], False), part(norm_attn[0][:, None], False), part(norm_moe[0][:, None], False),
         jnp.zeros((64, 30), bf16)], axis=1)
    extra = jnp.concatenate([mask_away, jnp.zeros((128, 32), bf16)], axis=1)
    extra = jnp.concatenate([extra, small], axis=0)
    extra = jnp.concatenate([extra, jnp.zeros((192, 64), bf16)], axis=1)
    payload = swapped(jnp.concatenate([rows, extra], axis=1))
    mask_other = payload[0:128, 512:544]
    own_rows = jnp.concatenate([mask_own, jnp.zeros((64, 32), bf16)], axis=0)
    payload = jnp.concatenate([payload[:, :576], own_rows, payload[:, 608:]], axis=1)
    shards = jnp.concatenate([w_gate[0], w_up[0], w_down[0]], axis=2)
    weights, away0 = gather_weights(payload, shards[0:1], w_query[0], w_key[0], w_value[0], w_out[0], 3)
    got = jnp.where(
        first,
        jnp.where(left, weights[1, 0, :, :, 512:], weights[1, 1, :, :, 512:]),
        jnp.where(left, weights[0, 0, :, :, 512:], weights[0, 1, :, :, 512:]),
    )
    other_small = got[:, 128:192, 0:64].reshape(1024, 64)
    all_other = got[:, 0:128, 0:32].reshape(2048, 32).T
    all_own = got[:, 0:128, 64:96].reshape(2048, 32).T
    pairs = [
        by_layer(norm_attn.astype(f32), other_small[:, 32][None].astype(f32)),
        by_layer(norm_moe.astype(f32), other_small[:, 33][None].astype(f32)),
        by_layer(w_router[0], other_small[:, :32]),
    ]
    dense = [tuple(p[l] for p in pairs) for l in range(2)]
    masks_own = by_layer(mask_own, mask_other)
    masks_all = by_layer(all_own, all_other)
    masks = [(masks_own[l], masks_all[l]) for l in range(2)]

    def over_dp(w):
        return lax.all_gather(w, "dp", axis=1, tiled=True)

    def first_kv(kv):
        kv, expert_w[0][0], expert_w[1][0] = lax.optimization_barrier((kv, expert_w[0][0], expert_w[1][0]))
        expert_w[0][0] = over_dp(expert_w[0][0])
        expert_w[1][0] = over_dp(expert_w[1][0])
        kv_all, away1 = gather_swap(kv, shards[1:2], 8)
        second = by_layer(shards[1:2], away1)
        for l in range(2):
            expert_w[l].append(over_dp(second[l]))
        return kv_all, expert_w[0]

    expert_w = [[w] for w in by_layer(shards[0:1], away0)]

    seq = mine(offsets)
    local = expert * 128 + jnp.arange(128, dtype=jnp.int32)
    steps = jnp.arange(HEAD // 2, dtype=f32) * 2.0 / HEAD
    angles = (local - seq).astype(f32)[:, None] * (rope_base ** (-steps))[None, :]
    cosine = jnp.tile(jnp.cos(angles), (1, 4))
    sine = jnp.tile(jnp.sin(angles), (1, 4))
    pick_rows = (
        lax.broadcasted_iota(jnp.int32, (8, 32), 1)
        == 2 * expert + lax.broadcasted_iota(jnp.int32, (8, 32), 0)
    ).astype(f32)
    place = (cosine, sine, seq[:, None], local[:, None], pick_rows.T, pick_rows)

    x0 = mine(inputs)
    out0, _, saved0 = forward(x0, 0, place, weights, dense[0], first_kv, masks[0])
    out1, _, saved1 = forward(out0, 1, place, weights, dense[1], expert_w[1], masks[1])
    cot = mine(cotangent)
    later, _ = lax.optimization_barrier((cot, saved0[4]))
    cot_all = gather_rows(later, 1)
    dx1, eg1, dg1, small1 = backward(cot, cot_all, saved1, 1, place, weights, dense[1], expert_w[1], masks[1])
    dx0, eg0, dg0, small0 = backward(dx1, None, saved0, 0, place, weights, dense[0], expert_w[0], masks[0])
    eg_sent = jnp.where(first, eg1, eg0)
    both_small = jnp.pad(jnp.stack([small0, small1]), ((0, 0), (0, 0), (0, 64)))
    dense_sum, eg_away = scatter_sum(dense_grads(dg0, dg1, both_small), 4, eg_sent)

    def in_place(l0, l1):
        got = swapped(jnp.where(first, l1, l0))
        own = jnp.where(first, l0, l1)
        return jnp.stack([jnp.where(first, own, got), jnp.where(first, got, own)])[None]

    acts = in_place(out0, out1)
    in_grads = in_place(dx0, dx1)

    tail = dense_sum[:, 1024:]
    full0 = jnp.concatenate([dense_sum[:, :512], tail], axis=1)
    full1 = dense_sum[:, 512:]
    own = jnp.where(first, full0, full1)
    other = jnp.where(first, full1, full0).astype(bf16)
    summed = gather_split(cross_sum(own, other, 6), 7)
    grad_query, grad_key, grad_value, grad_out = results(summed)
    grad_small = mine(summed[:, :, 0:64, 512:576]).reshape(1024, 64).astype(f32)
    eg = jnp.where(first, eg0, eg1).astype(f32) + eg_away.astype(f32)
    return (
        acts,
        in_grads,
        grad_query[None],
        grad_key[None],
        grad_value[None],
        grad_out[None],
        grad_small[:, 32][None],
        grad_small[:, 33][None],
        grad_small[None, :, :32],
        eg[None, :, :, 0:512],
        eg[None, :, :, 512:1024],
        eg[None, :, :, 1024:1536],
    )


def solution(mesh):
    token = P(None, ("dp", "expert"), None)
    layer_token = P("section", None, ("dp", "expert"), None)
    matrix = P("section", None, None)
    gain = P("section", None)
    expert = P("section", "expert", "dp", None)
    return jax.shard_map(
        on_device,
        mesh=mesh,
        in_specs=(
            token, token, P(None, ("dp", "expert")), layer_token,
            matrix, matrix, matrix, matrix, gain, gain, matrix, expert, expert, expert,
        ),
        out_specs=(
            layer_token, layer_token, matrix, matrix, matrix, matrix, gain, gain, matrix,
            expert, expert, expert,
        ),
        check_vma=False,
    )
```

```python
import functools

import jax
import jax.numpy as jnp
from jax import lax
from jax.experimental import pallas as pl
from jax.experimental.pallas import tpu as pltpu

from jax.sharding import PartitionSpec as P

HEAD = 64
MESH = pl.DeviceIdType.MESH
bf16 = jnp.bfloat16
f32 = jnp.float32
norm_eps = 1e-06
masked_score = -1e30
rope_base = 10000.0


def ring_places():
    me = lax.axis_index("expert")
    z, x = lax.div(me, 4), lax.rem(me, 4)
    xr, xl = lax.rem(x + 1, 4), lax.rem(x + 3, 4)
    zr, zl = lax.rem(z + 1, 4), lax.rem(z + 3, 4)
    near = (z * 4 + xr, z * 4 + xl, zr * 4 + x, zl * 4 + x)
    return z, x, xr, xl, zr, zl, near


def gather_kernel(kind, x_ref, *refs):
    split = kind in ("split", "weights")
    sided = kind in ("swap", "weights")
    if kind == "weights":
        side_ref, wq_ref, wk_ref, wv_ref, wo_ref, out_all, side_out = refs[:7]
    elif sided:
        side_ref, out_all, side_out = refs[:3]
    else:
        out_all = refs[0]
    send, recv, own_sem = refs[-3:]
    z, x, xr, xl, zr, zl, (dxr, dxl, dzr, dzl) = ring_places()
    x2, z2 = lax.rem(x + 2, 4), lax.rem(z + 2, 4)
    section, dp = lax.axis_index("section"), lax.axis_index("dp")
    core = lax.rem(dp, 2)
    rows, cols = x_ref.shape
    half, quarter = rows // 2, rows // 4
    locals_ = []
    if kind == "weights":
        out_ref = out_all.at[1 - section, core]
        moves = (
            (wq_ref.at[:, :, :, pl.ds(0, 512)], 0, 0),
            (wq_ref.at[:, :, :, pl.ds(512, 512)], 1, 0),
            (wk_ref, 0, 64),
            (wv_ref, 1, 64),
            (wo_ref.at[:, :, :, pl.ds(0, 512)], 0, 128),
            (wo_ref.at[:, :, :, pl.ds(512, 512)], 1, 128),
        )
        for i, (src, side, row) in enumerate(moves):
            dst = out_all.at[section, side, :, :, pl.ds(row, 64), pl.ds(0, 512)]
            c = pltpu.make_async_copy(src, dst, own_sem.at[1 + i])
            c.start()
            locals_.append(c)
    elif split:
        out_ref = out_all.at[core]
    else:
        out_ref = out_all
    own = pltpu.make_async_copy(x_ref, out_ref.at[z, x], own_sem.at[0])
    own.start()
    other_core, other_section = {"dp": dp + 1 - 2 * core}, {"section": 1 - section}
    barrier = pltpu.get_barrier_semaphore()
    greeted = [{"expert": d} for d in (dxr, dxl, dzr, dzl)]
    if split:
        greeted.append(other_core)
    if sided:
        greeted.append(other_section)
    for to in greeted:
        pl.semaphore_signal(barrier, inc=1, device_id=to, device_id_type=MESH)
    pl.semaphore_wait(barrier, len(greeted))

    def send_to(i, src, dst, to):
        c = pltpu.make_async_remote_copy(
            src_ref=src, dst_ref=dst, send_sem=send.at[i], recv_sem=recv.at[i],
            device_id=to, device_id_type=MESH)
        c.start()
        return c

    def copy(i, src, dst, to):
        return send_to(i, src, dst, {"expert": to})

    forwards = []

    def forward(*piece):
        if split:
            there = out_ref.at[piece]
            forwards.append(send_to(45 + len(forwards), there, there, other_core))

    A, B = pl.ds(0, half), pl.ds(half, half)
    A0, A1 = pl.ds(0, quarter), pl.ds(quarter, quarter)
    B0, B1 = pl.ds(half, quarter), pl.ds(half + quarter, quarter)
    every = slice(None)
    began = []

    def pair(piece, to_r, to_l, src=None):
        out = []
        for to in (to_r, to_l):
            there = out_ref.at[piece]
            out.append(copy(len(began), there if src is None else src, there, to))
            began.append(out[-1])
        return out

    def single(piece, to):
        there = out_ref.at[piece]
        began.append(copy(len(began), there, there, to))
        return began[-1]

    a_r, a_l = pair((z, x, A), dxr, dxl, x_ref.at[A])
    b_r, b_l = pair((z, x, B), dzr, dzl, x_ref.at[B])
    c_r, c_l = pair((z, x, A), dzr, dzl, x_ref.at[A])
    d_r, d_l = pair((z, x, B), dxr, dxl, x_ref.at[B])
    if sided:
        swap = send_to(44, side_ref, side_out, other_section)
    a_r.wait_recv()
    a2_r = single((z, xl, A0), dxr)
    c1_r, c1_l = pair((z, xl, A), dzr, dzl)
    a_l.wait_recv()
    a2_l = single((z, xr, A1), dxl)
    c2_r, c2_l = pair((z, xr, A), dzr, dzl)
    b_r.wait_recv()
    b2_r = single((zl, x, B0), dzr)
    d1_r, d1_l = pair((zl, x, B), dxr, dxl)
    b_l.wait_recv()
    b2_l = single((zr, x, B1), dzl)
    d2_r, d2_l = pair((zr, x, B), dxr, dxl)
    last = []
    c_r.wait_recv()
    last.append(single((zl, x, A0), dzr))
    c_l.wait_recv()
    last.append(single((zr, x, A1), dzl))
    d_r.wait_recv()
    last.append(single((z, xl, B0), dxr))
    d_l.wait_recv()
    last.append(single((z, xr, B1), dxl))
    a2_r.wait_recv()
    c3_r, c3_l = pair((z, x2, A0), dzr, dzl)
    a2_l.wait_recv()
    c4_r, c4_l = pair((z, x2, A1), dzr, dzl)
    b2_r.wait_recv()
    d3_r, d3_l = pair((z2, x, B0), dxr, dxl)
    b2_l.wait_recv()
    d4_r, d4_l = pair((z2, x, B1), dxr, dxl)
    c1_r.wait_recv()
    last.append(single((zl, xl, A0), dzr))
    c1_l.wait_recv()
    last.append(single((zr, xl, A1), dzl))
    d1_r.wait_recv()
    last.append(single((zl, xl, B0), dxr))
    d1_l.wait_recv()
    last.append(single((zl, xr, B1), dxl))
    own.wait()
    forward(z, every, A)
    forward(every, x, B)
    c2_r.wait_recv()
    last.append(single((zl, xr, A0), dzr))
    c2_l.wait_recv()
    last.append(single((zr, xr, A1), dzl))
    d2_r.wait_recv()
    last.append(single((zr, xl, B0), dxr))
    d2_l.wait_recv()
    last.append(single((zr, xr, B1), dxl))
    c3_r.wait_recv()
    last.append(single((zl, x2, A0), dzr))
    c4_l.wait_recv()
    last.append(single((zr, x2, A1), dzl))
    d3_r.wait_recv()
    last.append(single((z2, xl, B0), dxr))
    d4_l.wait_recv()
    last.append(single((z2, xr, B1), dxl))
    c3_l.wait_recv()
    c4_r.wait_recv()
    forward(zl, every, A)
    forward(zr, every, A)
    d3_l.wait_recv()
    d4_r.wait_recv()
    forward(every, xl, B)
    forward(every, xr, B)
    for c in last:
        c.wait_recv()
    forward(z2, every, A)
    forward(every, x2, B)
    for c in began:
        c.wait_send()
    for c in forwards + ([swap] if sided else []):
        c.wait_recv()
        c.wait_send()
    for c in locals_:
        c.wait()


def gather_call(ident, kind, outs, in_memory, *args):
    anywhere, memory = pl.BlockSpec(memory_space=pl.ANY), pl.BlockSpec(memory_space=pltpu.VMEM)
    return pl.pallas_call(
        functools.partial(gather_kernel, kind),
        out_shape=outs,
        in_specs=[memory if held else anywhere for held in in_memory],
        out_specs=[anywhere] * len(outs),
        scratch_shapes=[
            pltpu.SemaphoreType.DMA((53,)),
            pltpu.SemaphoreType.DMA((53,)),
            pltpu.SemaphoreType.DMA((7,)),
        ],
        compiler_params=pltpu.CompilerParams(
            collective_id=ident, has_side_effects=True, vmem_limit_bytes=56 << 20),
        name="gather_" + kind,
    )(*args)


def gather_rows(x, ident):
    rows, cols = x.shape
    out = gather_call(ident, "plain", [jax.ShapeDtypeStruct((4, 4, rows, cols), x.dtype)], (True,), x)[0]
    return out.reshape(16 * rows, cols)


def gather_swap(x, side, ident):
    rows, cols = x.shape
    out, side_out = gather_call(
        ident, "swap",
        [jax.ShapeDtypeStruct((4, 4, rows, cols), x.dtype), jax.ShapeDtypeStruct(side.shape, side.dtype)],
        (True, False), x, side)
    return out.reshape(16 * rows, cols), side_out


def gather_split(x, ident):
    rows, cols = x.shape
    out = gather_call(ident, "split", [jax.ShapeDtypeStruct((2, 4, 4, rows, cols), x.dtype)], (True,), x)[0]
    return out.reshape(2, 16, rows, cols)


def gather_weights(x, side, wq, wk, wv, wo, ident):
    rows, cols = x.shape
    parts = [w.reshape(4, 4, 64, w.shape[1]) for w in (wq, wk, wv, wo)]
    out, side_out = gather_call(
        ident, "weights",
        [jax.ShapeDtypeStruct((2, 2, 4, 4, rows, cols), x.dtype), jax.ShapeDtypeStruct(side.shape, side.dtype)],
        (True, False) + (True,) * 4, x, side, *parts)
    return out.reshape(2, 2, 16, rows, cols), side_out


def scatter_kernel(split, x_ref, *refs):
    if split:
        side_ref, out_ref, side_out, loc, land = refs[:5]
        core_send, core_recv = refs[-2:]
        refs = refs[5:-2]
    else:
        out_ref, loc = refs[:2]
        refs = refs[2:]
    s1, l1, l2, t0, m1, n1, m2, send, recv, loc_sem = refs
    z, x, xr, xl, zr, zl, (dxr, dxl, dzr, dzl) = ring_places()
    x2, z2 = lax.rem(x + 2, 4), lax.rem(z + 2, 4)
    dp = lax.axis_index("dp")
    core = lax.rem(dp, 2)
    rows = x_ref.shape[-2]
    half, quarter = rows // 2, rows // 4
    A0, A1 = pl.ds(0, quarter), pl.ds(quarter, quarter)
    B0, B1 = pl.ds(half, quarter), pl.ds(half + quarter, quarter)
    every = slice(None)
    pieces = (
        (z2, every, A0), (z2, every, A1), (every, x2, B0), (every, x2, B1),
        (zr, every, A1), (zl, every, A0), (every, xr, B1), (every, xl, B0),
        (zr, every, A0), (zl, every, A1), (every, xr, B0), (every, xl, B1),
        (z, every, A0), (z, every, A1), (every, x, B0), (every, x, B1),
    )
    part = x_ref.at[core] if split else x_ref
    skip = 0 if split else 8
    held = []
    for i, piece in enumerate(pieces[skip:]):
        c = pltpu.make_async_copy(part.at[piece], loc.at[i], loc_sem.at[i])
        c.start()
        held.append(c)
    other_core, other_section = {"dp": dp + 1 - 2 * core}, {"section": 1 - lax.axis_index("section")}
    barrier = pltpu.get_barrier_semaphore()
    greeted = [{"expert": d} for d in (dxr, dxl, dzr, dzl)] + ([other_core, other_section] if split else [])
    for to in greeted:
        pl.semaphore_signal(barrier, inc=1, device_id=to, device_id_type=MESH)
    pl.semaphore_wait(barrier, len(greeted))
    away = []
    if split:
        for i, piece in enumerate(pieces):
            c = pltpu.make_async_remote_copy(
                src_ref=x_ref.at[(1 - core,) + piece], dst_ref=land.at[i], send_sem=core_send.at[i],
                recv_sem=core_recv.at[i], device_id=other_core, device_id_type=MESH)
            c.start()
            away.append(c)
        swap = pltpu.make_async_remote_copy(
            src_ref=side_ref, dst_ref=side_out, send_sem=core_send.at[16], recv_sem=core_recv.at[16],
            device_id=other_section, device_id_type=MESH)
        swap.start()

    def copy(i, src, dst, to):
        c = pltpu.make_async_remote_copy(
            src_ref=src, dst_ref=dst, send_sem=send.at[i], recv_sem=recv.at[i],
            device_id={"expert": to}, device_id_type=MESH)
        c.start()
        return c

    def total(*parts):
        acc = parts[0].astype(f32)
        for p in parts[1:]:
            acc = acc + p.astype(f32)
        return acc

    def ready(i):
        if i < skip:
            return x_ref.at[pieces[i]]
        held[i - skip].wait()
        if split:
            away[i].wait_recv()
            loc[i] = total(loc[i], land[i]).astype(bf16)
        return loc.at[i - skip]

    c0 = copy(0, ready(0), l1.at[0], dzr)
    c1 = copy(1, ready(1), l1.at[1], dzl)
    c2 = copy(2, ready(2), l1.at[2], dxr)
    c3 = copy(3, ready(3), l1.at[3], dxl)
    c4 = copy(4, ready(4), l2.at[0, 1], dzr)
    c5 = copy(5, ready(5), l2.at[1, 0], dzl)
    c6 = copy(6, ready(6), l2.at[2, 1], dxr)
    c7 = copy(7, ready(7), l2.at[3, 0], dxl)
    mine = ready(8)
    c0.wait_recv()
    s1[0] = total(mine[...], l1[0]).astype(bf16)
    c8 = copy(8, s1.at[0], l2.at[0, 0], dzr)
    mine = ready(9)
    c1.wait_recv()
    s1[1] = total(mine[...], l1[1]).astype(bf16)
    c9 = copy(9, s1.at[1], l2.at[1, 1], dzl)
    mine = ready(10)
    c2.wait_recv()
    s1[2] = total(mine[...], l1[2]).astype(bf16)
    c10 = copy(10, s1.at[2], l2.at[2, 0], dxr)
    mine = ready(11)
    c3.wait_recv()
    s1[3] = total(mine[...], l1[3]).astype(bf16)
    c11 = copy(11, s1.at[3], l2.at[3, 1], dxl)
    mine = ready(13)
    c4.wait_recv()
    c9.wait_recv()
    t0[0, 1] = total(mine[...], l2[0, 1], l2[1, 1]).astype(bf16)
    mine = ready(12)
    c5.wait_recv()
    c8.wait_recv()
    t0[0, 0] = total(mine[...], l2[0, 0], l2[1, 0]).astype(bf16)
    e0 = copy(12, t0.at[0, 0, x2], m1.at[0], dxr)
    e1 = copy(13, t0.at[0, 1, x2], m1.at[1], dxl)
    e4 = copy(14, t0.at[0, 1, xr], m2.at[0, 1], dxr)
    e5 = copy(15, t0.at[0, 0, xl], m2.at[1, 0], dxl)
    mine = ready(15)
    c6.wait_recv()
    c11.wait_recv()
    t0[1, 1] = total(mine[...], l2[2, 1], l2[3, 1]).astype(bf16)
    mine = ready(14)
    c7.wait_recv()
    c10.wait_recv()
    t0[1, 0] = total(mine[...], l2[2, 0], l2[3, 0]).astype(bf16)
    e2 = copy(16, t0.at[1, 0, z2], m1.at[2], dzr)
    e3 = copy(17, t0.at[1, 1, z2], m1.at[3], dzl)
    e6 = copy(18, t0.at[1, 1, zr], m2.at[2, 1], dzr)
    e7 = copy(19, t0.at[1, 0, zl], m2.at[3, 0], dzl)
    e0.wait_recv()
    n1[0] = total(t0[0, 0, xr], m1[0]).astype(bf16)
    e8 = copy(20, n1.at[0], m2.at[0, 0], dxr)
    e1.wait_recv()
    n1[1] = total(t0[0, 1, xl], m1[1]).astype(bf16)
    e9 = copy(21, n1.at[1], m2.at[1, 1], dxl)
    e2.wait_recv()
    n1[2] = total(t0[1, 0, zr], m1[2]).astype(bf16)
    e10 = copy(22, n1.at[2], m2.at[2, 0], dzr)
    e3.wait_recv()
    n1[3] = total(t0[1, 1, zl], m1[3]).astype(bf16)
    e11 = copy(23, n1.at[3], m2.at[3, 1], dzl)
    e4.wait_recv()
    e9.wait_recv()
    out_ref[A1] = total(t0[0, 1, x], m2[0, 1], m2[1, 1])
    e5.wait_recv()
    e8.wait_recv()
    out_ref[A0] = total(t0[0, 0, x], m2[0, 0], m2[1, 0])
    e6.wait_recv()
    e11.wait_recv()
    out_ref[B1] = total(t0[1, 1, z], m2[2, 1], m2[3, 1])
    e7.wait_recv()
    e10.wait_recv()
    out_ref[B0] = total(t0[1, 0, z], m2[2, 0], m2[3, 0])
    for c in (c0, c1, c2, c3, c4, c5, c6, c7, c8, c9, c10, c11,
              e0, e1, e2, e3, e4, e5, e6, e7, e8, e9, e10, e11):
        c.wait_send()
    for c in away:
        c.wait_send()
    if split:
        swap.wait_recv()
        swap.wait_send()


def scatter_sum(x, ident, side=None):
    split = side is not None
    anywhere = pl.BlockSpec(memory_space=pl.ANY)
    summed, held = jax.ShapeDtypeStruct((x.shape[-2] // 16, x.shape[-1]), f32), whole()
    rows, cols = x.shape[-2] // 16, x.shape[-1]
    q = rows // 4
    piece = (4, q, cols)
    count = 16 if split else 8
    scratch = [pltpu.VMEM((count,) + piece, bf16)]
    if split:
        scratch.append(pltpu.VMEM((16,) + piece, bf16))
    scratch += [
        pltpu.VMEM((4,) + piece, bf16),
        pltpu.VMEM((4,) + piece, bf16),
        pltpu.VMEM((4, 2) + piece, bf16),
        pltpu.VMEM((2, 2) + piece, bf16),
        pltpu.VMEM(piece, bf16),
        pltpu.VMEM(piece, bf16),
        pltpu.VMEM((4, 2, q, cols), bf16),
        pltpu.SemaphoreType.DMA((24,)),
        pltpu.SemaphoreType.DMA((24,)),
        pltpu.SemaphoreType.DMA((count,)),
    ]
    if split:
        scratch += [pltpu.SemaphoreType.DMA((17,)), pltpu.SemaphoreType.DMA((17,))]
    return pl.pallas_call(
        functools.partial(scatter_kernel, split),
        out_shape=[summed, jax.ShapeDtypeStruct(side.shape, side.dtype)] if split else summed,
        in_specs=[anywhere] * (2 if split else 1),
        out_specs=[held, anywhere] if split else held,
        scratch_shapes=scratch,
        compiler_params=pltpu.CompilerParams(
            collective_id=ident, has_side_effects=True, vmem_limit_bytes=56 << 20),
        name="scatter_split" if split else "scatter_sum",
    )(x.reshape(x.shape[:-2] + (4, 4, rows, cols)), *([side] if split else []))


def spec(shape, index):
    return pl.BlockSpec(shape, index)


def fixed(shape):
    return pl.BlockSpec(shape, lambda *_: (0,) * len(shape), pipeline_mode=pl.Buffered(1))


def whole():
    return pl.BlockSpec(memory_space=pltpu.VMEM)


def local_call(kernel, outs, name, grid=None, in_specs=None, out_specs=None, flops=0, moved=0):
    params = pltpu.CompilerParams(vmem_limit_bytes=60 << 20)
    kinds = dict(
        out_shape=[jax.ShapeDtypeStruct(s, d) for s, d in outs],
        compiler_params=params,
        name=name,
        cost_estimate=pl.CostEstimate(flops=flops, bytes_accessed=moved, transcendentals=0),
    )
    if grid is None:
        kinds["out_specs"] = [spec(s, lambda i, n=len(s): (0,) * n) for s, _ in outs]
        blocks = in_specs or {}

        def call(*args):
            ins = [blocks.get(i) or spec(a.shape, lambda i, n=a.ndim: (0,) * n) for i, a in enumerate(args)]
            return pl.pallas_call(kernel, grid=(1,), in_specs=ins, **kinds)(*args)

        return call
    return pl.pallas_call(kernel, grid=grid, in_specs=in_specs, out_specs=out_specs, **kinds)


def dot(a, b):
    return jnp.dot(a, b, preferred_element_type=f32)


def dot_t(a, b):
    return lax.dot_general(a, b, (((1,), (1,)), ((), ())), preferred_element_type=f32)


def t_dot(a, b):
    return lax.dot_general(a, b, (((0,), (0,)), ((), ())), preferred_element_type=f32)


def lanes(shape):
    return lax.broadcasted_iota(jnp.int32, shape, len(shape) - 1)


def turned(u, cosine, sine):
    chunks = []
    for c in range(u.shape[1] // 128):
        part = u[:, 128 * c : 128 * c + 128]
        low = lax.rem(lanes(part.shape), 64) < 32
        rot = jnp.where(low, -pltpu.roll(part, 96, 1), pltpu.roll(part, 32, 1))
        chunks.append(part * cosine + rot * sine)
    return jnp.concatenate(chunks, axis=1)


def rms(x):
    return lax.rsqrt(jnp.mean(x * x, axis=-1, keepdims=True) + norm_eps)


def halves(w_ref, row):
    return tuple(w_ref[0, h, :, row : row + 64, 0:512].reshape(1024, 512) for h in range(2))


def pre_kernel(x_ref, gain_ref, cos_ref, sin_ref, w_ref, a_ref, q_ref, kv_ref):
    x = x_ref[...].astype(f32)
    a = (x * rms(x) * gain_ref[...]).astype(bf16)
    a_ref[...] = a
    cosine, sine = cos_ref[...], sin_ref[...]
    for h, w in enumerate(halves(w_ref, 0)):
        q_ref[:, 512 * h : 512 * h + 512] = turned(dot(a, w), cosine, sine).astype(bf16)
    wk, wv = halves(w_ref, 64)
    kv_ref[:, :512] = turned(dot(a, wk), cosine, sine).astype(bf16)
    kv_ref[:, 512:] = dot(a, wv).astype(bf16)


def head_rows(q):
    q = q.astype(f32)
    left, right = q[:, :128], q[:, 128:]
    low = lanes(left.shape) < 64
    parts = [
        jnp.where(low, left, 0.0),
        jnp.where(low, pltpu.roll(left, 64, 1), 0.0),
        jnp.where(low, 0.0, pltpu.roll(right, 64, 1)),
        jnp.where(low, 0.0, right),
    ]
    return parts


def head_lanes(p0, p1, p2, p3):
    low = lanes(p0.shape) < 64
    left = jnp.where(low, p0, pltpu.roll(p1, 64, 1))
    right = jnp.where(low, pltpu.roll(p2, 64, 1), p3)
    return jnp.concatenate([left, right], axis=1)


def attend_kernel(q_ref, k_ref, v_ref, lo_ref, hi_ref, o_ref, p_ref):
    key = lax.broadcasted_iota(jnp.int32, (128, 2048), 1)
    seen = (key >= lo_ref[...]) & (key <= hi_ref[...])
    k, v = k_ref[...], v_ref[...]
    outs = []
    for h, q in enumerate(head_rows(q_ref[...])):
        s = dot_t((q * 0.125).astype(bf16), k)
        s = jnp.where(seen, s, masked_score)
        e = jnp.exp(s - jnp.max(s, axis=-1, keepdims=True))
        p = (e * (1.0 / jnp.sum(e, axis=-1, keepdims=True))).astype(bf16)
        p_ref[0, 128 * h : 128 * h + 128, :] = p
        outs.append(dot(p, v))
    o_ref[...] = head_lanes(*outs).astype(bf16)


def attend(q, kv, lo, hi):
    return local_call(
        attend_kernel,
        [((128, 1024), bf16), ((4, 512, 2048), bf16)],
        "attend",
        grid=(4,),
        in_specs=[
            spec((128, 256), lambda i: (0, i)),
            spec((2048, 128), lambda i: (0, i)),
            spec((2048, 128), lambda i: (0, i + 4)),
            fixed((128, 1)),
            fixed((128, 1)),
        ],
        out_specs=[
            spec((128, 256), lambda i: (0, i)),
            spec((1, 512, 2048), lambda i: (i, 0, 0)),
        ],
        flops=2 * 2 * 2048 * 2048 * 128,
        moved=13 << 20,
    )(q, kv, kv, lo, hi)


def attend_back_kernel(q_ref, o_ref, do_ref, k_ref, v_ref, p_ref, dq_ref, dkv_ref):
    k, v = k_ref[...], v_ref[...]
    do = do_ref[...]
    prod = do.astype(f32) * o_ref[...].astype(f32)
    low = lanes((128, 128)) < 64
    left, right = prod[:, :128], prod[:, 128:]
    deltas = [
        jnp.sum(jnp.where(low, left, 0.0), axis=1, keepdims=True),
        jnp.sum(jnp.where(low, 0.0, left), axis=1, keepdims=True),
        jnp.sum(jnp.where(low, right, 0.0), axis=1, keepdims=True),
        jnp.sum(jnp.where(low, 0.0, right), axis=1, keepdims=True),
    ]
    do_rows = [r.astype(bf16) for r in head_rows(do)]
    q_rows = [(r * 0.125).astype(bf16) for r in head_rows(q_ref[...])]
    dqs, dss = [], []
    for h in range(4):
        dp = dot_t(do_rows[h], v)
        p = p_ref[0, 128 * h : 128 * h + 128, :].astype(f32)
        ds = (p * (dp - deltas[h])).astype(bf16)
        dss.append(ds)
        dqs.append(dot(ds, k) * 0.125)
    dq_ref[...] = head_lanes(*dqs)
    dkv_ref[:, :128] = t_dot(jnp.concatenate(dss, axis=0), jnp.concatenate(q_rows, axis=0)).astype(bf16)
    dkv_ref[:, 128:] = t_dot(p_ref[0], jnp.concatenate(do_rows, axis=0)).astype(bf16)


def attend_back(q, o, do, kv, probs):
    side = spec((128, 256), lambda i: (0, i))
    return local_call(
        attend_back_kernel,
        [((128, 1024), f32), ((2048, 1024), bf16)],
        "attend_back",
        grid=(4,),
        in_specs=[
            side,
            side,
            side,
            spec((2048, 128), lambda i: (0, i)),
            spec((2048, 128), lambda i: (0, i + 4)),
            spec((1, 512, 2048), lambda i: (i, 0, 0)),
        ],
        out_specs=[side, spec((2048, 256), lambda i: (0, i))],
        flops=4 * 2 * 2048 * 2048 * 128,
        moved=17 << 20,
    )(q, o, do, kv, kv, probs)


def post_kernel(x_ref, o_ref, wo_ref, gain_ref, h_ref, b_ref):
    o = o_ref[...]
    h = x_ref[...].astype(f32) + jnp.concatenate([dot(o, w) for w in halves(wo_ref, 0)], axis=1)
    h_ref[...] = h
    b_ref[...] = (h * rms(h) * gain_ref[...]).astype(bf16)


def chosen_gates(b, wr, mask):
    logits = dot(b, wr)
    chosen = mask.astype(f32) > 0.5
    top = jnp.max(jnp.where(chosen, logits, masked_score), axis=-1, keepdims=True)
    e = jnp.where(chosen, jnp.exp(jnp.where(chosen, logits - top, 0.0)), 0.0)
    return e / jnp.sum(e, axis=-1, keepdims=True)


SLOTS = 80
ROWS = 1024


def experts_kernel(b_ref, mask_ref, wr_ref, pick_ref, w0_ref, w1_ref, y_ref, x_ref, gu_ref, s_ref, gate_ref):
    row, col = lax.broadcasted_iota(jnp.int32, (256, 256), 0), lanes((256, 256))
    before = ((row < col) & ((row < 128) == (col < 128))).astype(bf16)
    slot_ids = lax.broadcasted_iota(jnp.int32, (SLOTS, 256), 0)
    second = jnp.where(lanes((1, 256)) < 128, 0.0, SLOTS // 2)
    for p in range(ROWS // 256):
        b = b_ref[256 * p : 256 * p + 256, :]
        mask = mask_ref[:, 256 * p : 256 * p + 256]
        chosen = mask.astype(f32) > 0.5
        logits = dot_t(wr_ref[...], b)
        top = jnp.max(jnp.where(chosen, logits, masked_score), axis=0, keepdims=True)
        e = jnp.where(chosen, jnp.exp(jnp.where(chosen, logits - top, 0.0)), 0.0)
        gates = e / jnp.sum(e, axis=0, keepdims=True)
        rank = dot(mask, before)
        for j in range(2):
            one = pick_ref[:, j : j + 1]
            gate = jnp.sum(gates * one, axis=0, keepdims=True)
            used = jnp.sum(mask.astype(f32) * one, axis=0, keepdims=True)
            place = jnp.sum(rank * one, axis=0, keepdims=True) + second
            hit = (slot_ids == place.astype(jnp.int32)) & (used > 0.5)
            s = jnp.where(hit, 1.0, 0.0)
            part = slice(SLOTS * p, SLOTS * p + SLOTS)
            gate_ref[j, part, :] = jnp.sum(s * gate, axis=1, keepdims=True)
            s_ref[p, SLOTS * j : SLOTS * j + SLOTS, :] = s.astype(bf16)
        rows = dot(s_ref[p], b).astype(bf16)
        for j in range(2):
            x_ref[j, part, :] = rows[SLOTS * j : SLOTS * j + SLOTS]
    ys = []
    for j in range(2):
        x = x_ref[j]
        g = dot(x, (w0_ref, w1_ref)[j][0, :, 0:512])
        u = dot(x, (w0_ref, w1_ref)[j][0, :, 512:1024])
        gu_ref[j, :, 0:512] = g.astype(bf16)
        gu_ref[j, :, 512:1024] = u.astype(bf16)
        inner = g * jax.nn.sigmoid(g) * u
        ys.append(dot_t((inner * gate_ref[j]).astype(bf16), (w0_ref, w1_ref)[j][0, :, 1024:1536]).astype(bf16))
    for p in range(ROWS // 256):
        part = slice(SLOTS * p, SLOTS * p + SLOTS)
        both = jnp.concatenate([ys[0][part], ys[1][part]], axis=0)
        y_ref[256 * p : 256 * p + 256, :] = t_dot(s_ref[p], both).astype(bf16)


HALF = SLOTS * ROWS // 256
FULL = 2 * HALF


def compact(cols):
    return spec((2, HALF, cols), lambda i: (0, i, 0))


def tokens(cols):
    return spec((ROWS, cols), lambda i: (i, 0))


choice = spec((ROWS // 256, 2 * SLOTS, 256), lambda i: (i, 0, 0))


def experts(b_all, mask_all, wr, pick, w):
    rows = b_all.shape[0]
    return local_call(
        experts_kernel,
        [
            ((rows, 1024), bf16), ((2, FULL, 1024), bf16), ((2, FULL, 1024), bf16),
            ((rows // 256, 2 * SLOTS, 256), bf16), ((2, FULL, 1), f32),
        ],
        "experts",
        grid=(rows // ROWS,),
        in_specs=[
            tokens(1024),
            spec((32, ROWS), lambda i: (0, i)),
            fixed((32, 1024)),
            fixed((32, 8)),
            fixed((1, 1024, 1536)),
            fixed((1, 1024, 1536)),
        ],
        out_specs=[tokens(1024), compact(1024), compact(1024), choice, compact(1)],
        flops=8 * 2 * 1280 * 1024 * 512,
        moved=20 << 20,
    )(b_all, mask_all, wr, pick, *w)


def experts_back_kernel(
    dout_ref, s_ref, gu_ref, gate_ref, wcol_ref, w0_ref, w1_ref, db_ref, d_ref, dgu_ref, in_ref, coef_ref
):
    for p in range(ROWS // 256):
        rows = dot(s_ref[p], dout_ref[256 * p : 256 * p + 256, :]).astype(bf16)
        for j in range(2):
            d_ref[j, SLOTS * p : SLOTS * p + SLOTS, :] = rows[SLOTS * j : SLOTS * j + SLOTS]
    dbs = []
    for j in range(2):
        gate = gate_ref[j]
        g = gu_ref[j, :, 0:512].astype(f32)
        u = gu_ref[j, :, 512:1024].astype(f32)
        back = dot(d_ref[j], (w0_ref, w1_ref)[j][0, :, 1024:1536])
        sig = jax.nn.sigmoid(g)
        silu = g * sig
        inner = silu * u
        coef = gate * jnp.sum(inner * back, axis=1, keepdims=True)
        coef_ref[j] = coef
        in_ref[j] = (inner * gate).astype(bf16)
        dinner = back * gate
        dg = (dinner * u * sig * (1.0 + g * (1.0 - sig))).astype(bf16)
        du = (dinner * silu).astype(bf16)
        dgu_ref[j, :, 0:512] = dg
        dgu_ref[j, :, 512:1024] = du
        db = dot_t(dg, (w0_ref, w1_ref)[j][0, :, 0:512]) + dot_t(du, (w0_ref, w1_ref)[j][0, :, 512:1024])
        dbs.append((db + coef * wcol_ref[j : j + 1, :]).astype(bf16))
    for p in range(ROWS // 256):
        part = slice(SLOTS * p, SLOTS * p + SLOTS)
        both = jnp.concatenate([dbs[0][part], dbs[1][part]], axis=0)
        db_ref[256 * p : 256 * p + 256, :] = t_dot(s_ref[p], both).astype(bf16)


def experts_back(dout_all, choices, gu, gate, wcol, w):
    rows = dout_all.shape[0]
    return local_call(
        experts_back_kernel,
        [
            ((rows, 1024), bf16), ((2, FULL, 1024), bf16), ((2, FULL, 1024), bf16),
            ((2, FULL, 512), bf16), ((2, FULL, 1), f32),
        ],
        "experts_back",
        grid=(rows // ROWS,),
        in_specs=[
            tokens(1024), choice, compact(1024), compact(1), fixed((8, 1024)), fixed((1, 1024, 1536)),
            fixed((1, 1024, 1536)),
        ],
        out_specs=[tokens(1024), compact(1024), compact(1024), compact(512), compact(1)],
        flops=8 * 2 * 1280 * 1024 * 512,
        moved=24 << 20,
    )(dout_all, choices, gu, gate, wcol, *w)


def expert_grads_kernel(x_ref, d_ref, dgu_ref, in_ref, out_ref):
    out_ref[0, :, 0:1024] = t_dot(x_ref[0], dgu_ref[0]).astype(bf16)
    out_ref[0, :, 1024:1536] = t_dot(d_ref[0], in_ref[0]).astype(bf16)


def expert_grads(x, d, dgu, inner):
    def one(cols):
        return spec((1, FULL, cols), lambda j: (j, 0, 0))

    return local_call(
        expert_grads_kernel,
        [((2, 1024, 1536), bf16)],
        "expert_grads",
        grid=(2,),
        in_specs=[one(1024), one(1024), one(1024), one(512)],
        out_specs=[spec((1, 1024, 1536), lambda j: (j, 0, 0))],
        flops=3 * 2 * 1280 * 1024 * 512,
        moved=16 << 20,
    )(x, d, dgu, inner)[0]


def mid_back_kernel(
    sum_ref, dout_ref, mix_ref, h_ref, b_ref, gain_ref, wr_ref, mask_ref, wo_ref,
    dh_ref, dattn_ref, do_ref, router_ref, gain_grad_ref,
):
    dout = dout_ref[...].astype(f32)
    b = b_ref[...]
    wr = wr_ref[...]
    h = h_ref[...]
    r = rms(h)
    n = h * r
    gates = chosen_gates(b, wr, mask_ref[...])
    level = jnp.sum(dout * mix_ref[...], axis=-1, keepdims=True)
    taken = (gates * -level).astype(bf16)
    router_ref[...] = t_dot(taken, b)
    db = sum_ref[...] + dot_t(taken, wr)
    gain_grad_ref[...] = jnp.broadcast_to(jnp.sum(db * n, axis=0, keepdims=True), gain_grad_ref.shape)
    ng = db * gain_ref[...]
    dh = dout + r * (ng - n * jnp.mean(ng * n, axis=-1, keepdims=True))
    dh_ref[...] = dh
    dattn = dh.astype(bf16)
    dattn_ref[...] = dattn
    w0, w1 = halves(wo_ref, 0)
    do_ref[...] = (dot_t(dattn[:, :512], w0) + dot_t(dattn[:, 512:], w1)).astype(bf16)


def end_back_kernel(
    dq_ref, dkv_ref, cos_ref, sin_ref, w_ref, x_ref, gain_ref, dh_ref,
    dq_lin_ref, dkv_lin_ref, dx_ref, gain_grad_ref,
):
    cosine, sine = cos_ref[...], -sin_ref[...]
    dq = turned(dq_ref[...], cosine, sine).astype(bf16)
    dkv = dkv_ref[...]
    dk = jnp.concatenate([dkv[:, 256 * i : 256 * i + 128] for i in range(4)], axis=1)
    dv = jnp.concatenate([dkv[:, 256 * i + 128 : 256 * i + 256] for i in range(4)], axis=1)
    dk = turned(dk, cosine, sine).astype(bf16)
    dv = dv.astype(bf16)
    dq_lin_ref[...] = dq
    dkv_lin_ref[:, :512] = dk
    dkv_lin_ref[:, 512:] = dv
    (q0, q1), (wk, wv) = halves(w_ref, 0), halves(w_ref, 64)
    da = dot_t(dq[:, :512], q0) + dot_t(dq[:, 512:], q1) + dot_t(dk, wk) + dot_t(dv, wv)
    x = x_ref[...].astype(f32)
    r = rms(x)
    n = x * r
    gain_grad_ref[...] = jnp.broadcast_to(jnp.sum(da * n, axis=0, keepdims=True), gain_grad_ref.shape)
    ng = da * gain_ref[...]
    dx = dh_ref[...] + r * (ng - n * jnp.mean(ng * n, axis=-1, keepdims=True))
    dx_ref[...] = dx.astype(bf16)


def dense_grads_kernel(*refs):
    small_ref, out_ref = refs[10:]
    for layer in range(2):
        a_ref, o_ref, dq_ref, dkv_ref, dattn_ref = refs[5 * layer : 5 * layer + 5]
        a = a_ref[...]
        gq = t_dot(a, dq_ref[...]).astype(bf16)
        gkv = t_dot(a, dkv_ref[...]).astype(bf16)
        go = t_dot(o_ref[...], dattn_ref[...]).astype(bf16)
        cols = slice(512 * layer, 512 * layer + 512)
        for t in range(2):
            part = slice(64 * t, 64 * t + 64)
            for h in range(2):
                side = slice(512 * h, 512 * h + 512)
                out_ref[h, t, 0:64, cols] = gq[part, side]
                out_ref[h, t, 64:128, cols] = gkv[part, side]
                out_ref[h, t, 128:192, cols] = go[part, side]
    for h in range(2):
        out_ref[h, 0, 0:64, 1024:1152] = small_ref[h]
        out_ref[h, 0, 64:192, 1024:1152] = jnp.zeros((128, 128), bf16)
        out_ref[h, 1, :, 1024:1152] = jnp.zeros((192, 128), bf16)


def dense_grads(layer0, layer1, small):
    narrow = spec((128, 128), lambda i: (0, i))
    out = local_call(
        dense_grads_kernel,
        [((2, 16, 192, 1152), bf16)],
        "dense_grads",
        grid=(8,),
        in_specs=([narrow, narrow] + [fixed((128, 1024))] * 3) * 2 + [spec((2, 64, 128), lambda i: (0, 0, i))],
        out_specs=[spec((2, 2, 192, 1152), lambda i: (0, i, 0, 0))],
        flops=6 * 2 * 128 * 1024 * 1024,
        moved=18 << 20,
    )(*layer0, *layer1, small)[0]
    return out.reshape(2, 3072, 1152)


def cross_kernel(own_ref, other_ref, out_ref, land, mine, send, recv):
    section, dp = lax.axis_index("section"), lax.axis_index("dp")
    partners = (
        {"section": 1 - section},
        {"dp": lax.rem(dp + 2, 4)},
    )
    barrier = pltpu.get_barrier_semaphore()
    for to in partners:
        pl.semaphore_signal(barrier, inc=1, device_id=to, device_id_type=MESH)
    pl.semaphore_wait(barrier, 2)
    copies = []
    for i, to in enumerate(partners):
        src = other_ref if i == 0 else mine
        c = pltpu.make_async_remote_copy(
            src_ref=src, dst_ref=land.at[i], send_sem=send.at[i], recv_sem=recv.at[i],
            device_id=to, device_id_type=MESH)
        c.start()
        copies.append(c)
        c.wait_recv()
        before = own_ref[...] if i == 0 else mine[...].astype(f32)
        after = (before + land[i].astype(f32)).astype(bf16)
        if i == 0:
            mine[...] = after
        else:
            out_ref[...] = after
    for c in copies:
        c.wait_send()


def cross_sum(own, other, ident):
    rows, cols = own.shape
    return pl.pallas_call(
        cross_kernel,
        out_shape=jax.ShapeDtypeStruct((rows, cols), bf16),
        in_specs=[whole(), whole()],
        out_specs=whole(),
        scratch_shapes=[
            pltpu.VMEM((2, rows, cols), bf16),
            pltpu.VMEM((rows, cols), bf16),
            pltpu.SemaphoreType.DMA((2,)),
            pltpu.SemaphoreType.DMA((2,)),
        ],
        compiler_params=pltpu.CompilerParams(
            collective_id=ident, has_side_effects=True, vmem_limit_bytes=24 << 20),
        name="cross_sum",
    )(own, other)


def qkv_block(layer):
    return spec((1, 2, 16, 128, 640), lambda i: (layer, 0, 0, 0, 0))


def out_block(layer):
    return spec((1, 2, 16, 64, 640), lambda i: (layer, 0, 0, 2, 0))


def forward(x, layer, place, weights, dense, w, masks):
    cosine, sine, lo, hi, pick, _ = place
    gain_attn, gain_moe, wr = dense
    a, q, kv = local_call(
        pre_kernel, [((128, 1024), bf16)] * 3, "pre", in_specs={4: qkv_block(layer)},
        flops=2 * 128 * 1024 * 2048, moved=6 << 20,
    )(x, gain_attn, cosine, sine, weights)
    if callable(w):
        kv_all, w = w(kv)
    else:
        kv_all = gather_rows(kv, 1)
    o, probs = attend(q, kv_all, lo, hi)
    h, b = local_call(
        post_kernel, [((128, 1024), f32), ((128, 1024), bf16)], "post", in_specs={2: out_block(layer)},
        flops=2 * 128 * 1024 * 1024, moved=4 << 20,
    )(x, o, weights, gain_moe)
    b_all = gather_rows(b, 1)
    y, rows, gu, choices, gate = experts(b_all, masks[1], wr.T, pick, w)
    mix = scatter_sum(y, 2)
    out = (h + mix).astype(bf16)
    return out, w, (x, a, q, kv_all, o, probs, h, b, rows, gu, choices, gate, mix)


def backward(dout, dout_all, saved, layer, place, weights, dense, w, masks):
    cosine, sine, lo, hi, pick, pick_rows = place
    gain_attn, gain_moe, wr = dense
    x, a, q, kv_all, o, probs, h, b, rows, gu, choices, gate, mix = saved
    if dout_all is None:
        dout_all = gather_rows(dout, 1)
    wcol = dot_t(pick_rows.astype(bf16), wr)
    db_part, drows, dgu, inner, coef = experts_back(dout_all, choices, gu, gate, wcol, w)
    db_sum = scatter_sum(db_part, 2)
    expert_grad = lax.psum_scatter(
        expert_grads(rows, drows, dgu, inner), "dp", scatter_dimension=1, tiled=True)
    router_cols = jnp.einsum("jrd,jr->jd", rows, coef[:, :, 0].astype(bf16), preferred_element_type=f32)
    router_part = jnp.einsum(
        "je,jd->ed", pick_rows[:2], router_cols, preferred_element_type=f32, precision=lax.Precision.HIGHEST)
    dh, dattn, do, router_own, gain_moe_grad = local_call(
        mid_back_kernel,
        [((128, 1024), f32), ((128, 1024), bf16), ((128, 1024), bf16), ((32, 1024), f32), ((8, 1024), f32)],
        "mid_back", in_specs={8: out_block(layer)}, flops=2 * 128 * 1024 * 1024, moved=5 << 20,
    )(db_sum, dout, mix, h, b, gain_moe, wr, masks[0], weights)
    dq, dkv = attend_back(q, o, do, kv_all, probs)
    dkv_sum = scatter_sum(dkv, 2)
    dq_lin, dkv_lin, dx, gain_attn_grad = local_call(
        end_back_kernel,
        [((128, 1024), bf16), ((128, 1024), bf16), ((128, 1024), bf16), ((8, 1024), f32)],
        "end_back", in_specs={4: qkv_block(layer)}, flops=2 * 128 * 1024 * 2048, moved=8 << 20,
    )(dq, dkv_sum, cosine, sine, weights, x, gain_attn, dh)
    small = jnp.concatenate(
        [router_part + router_own, gain_attn_grad[0:1], gain_moe_grad[0:1], jnp.zeros((30, 1024), f32)], axis=0
    ).astype(bf16)
    return dx, expert_grad, (a, o, dq_lin, dkv_lin, dattn), small


def results_kernel(s_ref, query_ref, key_ref, value_ref, out_ref):
    for h in range(2):
        side = slice(512 * h, 512 * h + 512)
        query_ref[:, side] = s_ref[h, :, 0:64, 0:512].reshape(256, 512).astype(f32)
        out_ref[:, side] = s_ref[h, :, 128:192, 0:512].reshape(256, 512).astype(f32)
    key_ref[...] = s_ref[0, :, 64:128, 0:512].reshape(256, 512).astype(f32)
    value_ref[...] = s_ref[1, :, 64:128, 0:512].reshape(256, 512).astype(f32)


def results(summed):
    return local_call(
        results_kernel,
        [((1024, 1024), f32), ((1024, 512), f32), ((1024, 512), f32), ((1024, 1024), f32)],
        "results",
        grid=(4,),
        in_specs=[spec((2, 4, 192, 640), lambda i: (0, i, 0, 0))],
        out_specs=[spec((256, n), lambda i: (i, 0)) for n in (1024, 512, 512, 1024)],
        moved=20 << 20,
    )(summed)


def swapped(x):
    return lax.ppermute(x, "section", [(0, 1), (1, 0)])


def on_device(
    inputs, cotangent, offsets, routes, w_query, w_key, w_value, w_out,
    norm_attn, norm_moe, w_router, w_gate, w_up, w_down,
):
    section = lax.axis_index("section")
    expert = lax.axis_index("expert")
    first = section == 0

    def by_layer(own, other):
        return jnp.where(first, own, other), jnp.where(first, other, own)

    def mine(pair):
        return jnp.where(first, pair[0], pair[1])

    ids = lax.broadcasted_iota(jnp.int32, (1, 1, 1, 32), 3)
    mask_both = jnp.any(routes[0][:, :, :, None] == ids, axis=2).astype(bf16)
    mask_own = mine(mask_both)
    mask_away = jnp.where(first, mask_both[1], mask_both[0])
    start = expert * 64
    left = lax.rem(lax.axis_index("dp"), 2) == 0

    def part(w, there=True):
        if not there:
            return lax.dynamic_slice_in_dim(w, start, 64, axis=0)
        return lax.dynamic_slice(w, (start, jnp.where(left, 0, 512)), (64, 512))

    rows = jnp.concatenate(
        [part(w_query[0]), jnp.where(left, part(w_key[0], False), part(w_value[0], False)), part(w_out[0])],
        axis=0,
    )
    small = jnp.concatenate(
        [part(w_router[0], False), part(norm_attn[0][:, None], False), part(norm_moe[0][:, None], False),
         jnp.zeros((64, 30), bf16)], axis=1)
    extra = jnp.concatenate([mask_away, jnp.zeros((128, 32), bf16)], axis=1)
    extra = jnp.concatenate([extra, small], axis=0)
    extra = jnp.concatenate([extra, jnp.zeros((192, 64), bf16)], axis=1)
    payload = swapped(jnp.concatenate([rows, extra], axis=1))
    mask_other = payload[0:128, 512:544]
    own_rows = jnp.concatenate([mask_own, jnp.zeros((64, 32), bf16)], axis=0)
    payload = jnp.concatenate([payload[:, :576], own_rows, payload[:, 608:]], axis=1)
    shards = jnp.concatenate([w_gate[0], w_up[0], w_down[0]], axis=2)
    weights, away0 = gather_weights(payload, shards[0:1], w_query[0], w_key[0], w_value[0], w_out[0], 3)
    got = jnp.where(
        first,
        jnp.where(left, weights[1, 0, :, :, 512:], weights[1, 1, :, :, 512:]),
        jnp.where(left, weights[0, 0, :, :, 512:], weights[0, 1, :, :, 512:]),
    )
    other_small = got[:, 128:192, 0:64].reshape(1024, 64)
    all_other = got[:, 0:128, 0:32].reshape(2048, 32).T
    all_own = got[:, 0:128, 64:96].reshape(2048, 32).T
    pairs = [
        by_layer(norm_attn.astype(f32), other_small[:, 32][None].astype(f32)),
        by_layer(norm_moe.astype(f32), other_small[:, 33][None].astype(f32)),
        by_layer(w_router[0], other_small[:, :32]),
    ]
    dense = [tuple(p[l] for p in pairs) for l in range(2)]
    masks_own = by_layer(mask_own, mask_other)
    masks_all = by_layer(all_own, all_other)
    masks = [(masks_own[l], masks_all[l]) for l in range(2)]

    def over_dp(w):
        return lax.all_gather(w, "dp", axis=1, tiled=True)

    def first_kv(kv):
        kv, expert_w[0][0], expert_w[1][0] = lax.optimization_barrier((kv, expert_w[0][0], expert_w[1][0]))
        expert_w[0][0] = over_dp(expert_w[0][0])
        expert_w[1][0] = over_dp(expert_w[1][0])
        kv_all, away1 = gather_swap(kv, shards[1:2], 8)
        second = by_layer(shards[1:2], away1)
        for l in range(2):
            expert_w[l].append(over_dp(second[l]))
        return kv_all, expert_w[0]

    expert_w = [[w] for w in by_layer(shards[0:1], away0)]

    seq = mine(offsets)
    local = expert * 128 + jnp.arange(128, dtype=jnp.int32)
    steps = jnp.arange(HEAD // 2, dtype=f32) * 2.0 / HEAD
    angles = (local - seq).astype(f32)[:, None] * (rope_base ** (-steps))[None, :]
    cosine = jnp.tile(jnp.cos(angles), (1, 4))
    sine = jnp.tile(jnp.sin(angles), (1, 4))
    pick_rows = (
        lax.broadcasted_iota(jnp.int32, (8, 32), 1)
        == 2 * expert + lax.broadcasted_iota(jnp.int32, (8, 32), 0)
    ).astype(f32)
    place = (cosine, sine, seq[:, None], local[:, None], pick_rows.T, pick_rows)

    x0 = mine(inputs)
    out0, _, saved0 = forward(x0, 0, place, weights, dense[0], first_kv, masks[0])
    out1, _, saved1 = forward(out0, 1, place, weights, dense[1], expert_w[1], masks[1])
    cot = mine(cotangent)
    later, _ = lax.optimization_barrier((cot, saved0[4]))
    cot_all = gather_rows(later, 1)
    dx1, eg1, dg1, small1 = backward(cot, cot_all, saved1, 1, place, weights, dense[1], expert_w[1], masks[1])
    dx0, eg0, dg0, small0 = backward(dx1, None, saved0, 0, place, weights, dense[0], expert_w[0], masks[0])
    eg_sent = jnp.where(first, eg1, eg0)
    both_small = jnp.stack([small0, small1])
    dense_sum, eg_away = scatter_sum(dense_grads(dg0, dg1, both_small), 4, eg_sent)

    def in_place(l0, l1):
        got = swapped(jnp.where(first, l1, l0))
        own = jnp.where(first, l0, l1)
        return jnp.stack([jnp.where(first, own, got), jnp.where(first, got, own)])[None]

    acts = in_place(out0, out1)
    in_grads = in_place(dx0, dx1)

    tail = dense_sum[:, 1024:]
    full0 = jnp.concatenate([dense_sum[:, :512], tail], axis=1)
    full1 = dense_sum[:, 512:]
    own = jnp.where(first, full0, full1)
    other = jnp.where(first, full1, full0).astype(bf16)
    summed = gather_split(cross_sum(own, other, 6), 7)
    grad_query, grad_key, grad_value, grad_out = results(summed)
    grad_small = mine(summed[:, ::2, 0:64, 512:640]).transpose(1, 0, 2).reshape(64, 1024).astype(f32)
    eg = jnp.where(first, eg0, eg1).astype(f32) + eg_away.astype(f32)
    return (
        acts,
        in_grads,
        grad_query[None],
        grad_key[None],
        grad_value[None],
        grad_out[None],
        grad_small[32:33],
        grad_small[33:34],
        grad_small[:32].T[None],
        eg[None, :, :, 0:512],
        eg[None, :, :, 512:1024],
        eg[None, :, :, 1024:1536],
    )


def solution(mesh):
    token = P(None, ("dp", "expert"), None)
    layer_token = P("section", None, ("dp", "expert"), None)
    matrix = P("section", None, None)
    gain = P("section", None)
    expert = P("section", "expert", "dp", None)
    return jax.shard_map(
        on_device,
        mesh=mesh,
        in_specs=(
            token, token, P(None, ("dp", "expert")), layer_token,
            matrix, matrix, matrix, matrix, gain, gain, matrix, expert, expert, expert,
        ),
        out_specs=(
            layer_token, layer_token, matrix, matrix, matrix, matrix, gain, gain, matrix,
            expert, expert, expert,
        ),
        check_vma=False,
    )
```

```python
import functools

import jax
import jax.numpy as jnp
from jax import lax
from jax.experimental import pallas as pl
from jax.experimental.pallas import tpu as pltpu

from jax.sharding import PartitionSpec as P

HEAD = 64
MESH = pl.DeviceIdType.MESH
bf16 = jnp.bfloat16
f32 = jnp.float32
norm_eps = 1e-06
masked_score = -1e30
rope_base = 10000.0


def ring_places():
    me = lax.axis_index("expert")
    z, x = lax.div(me, 4), lax.rem(me, 4)
    xr, xl = lax.rem(x + 1, 4), lax.rem(x + 3, 4)
    zr, zl = lax.rem(z + 1, 4), lax.rem(z + 3, 4)
    near = (z * 4 + xr, z * 4 + xl, zr * 4 + x, zl * 4 + x)
    return z, x, xr, xl, zr, zl, near


def gather_kernel(kind, x_ref, *refs):
    split = kind in ("split", "weights")
    sided = kind in ("swap", "weights")
    if kind == "weights":
        side_ref, wq_ref, wk_ref, wv_ref, wo_ref, out_all, side_out = refs[:7]
    elif sided:
        side_ref, out_all, side_out = refs[:3]
    else:
        out_all = refs[0]
    send, recv, own_sem = refs[-3:]
    z, x, xr, xl, zr, zl, (dxr, dxl, dzr, dzl) = ring_places()
    x2, z2 = lax.rem(x + 2, 4), lax.rem(z + 2, 4)
    section, dp = lax.axis_index("section"), lax.axis_index("dp")
    core = lax.rem(dp, 2)
    rows, cols = x_ref.shape
    half, quarter = rows // 2, rows // 4
    locals_ = []
    if kind == "weights":
        out_ref = out_all.at[1 - section, core]
        moves = (
            (wq_ref.at[:, :, :, pl.ds(0, 512)], 0, 0),
            (wq_ref.at[:, :, :, pl.ds(512, 512)], 1, 0),
            (wk_ref, 0, 64),
            (wv_ref, 1, 64),
            (wo_ref.at[:, :, :, pl.ds(0, 512)], 0, 128),
            (wo_ref.at[:, :, :, pl.ds(512, 512)], 1, 128),
        )
        for i, (src, side, row) in enumerate(moves):
            dst = out_all.at[section, side, :, :, pl.ds(row, 64), pl.ds(0, 512)]
            c = pltpu.make_async_copy(src, dst, own_sem.at[1 + i])
            c.start()
            locals_.append(c)
    elif split:
        out_ref = out_all.at[core]
    else:
        out_ref = out_all
    own = pltpu.make_async_copy(x_ref, out_ref.at[z, x], own_sem.at[0])
    own.start()
    other_core, other_section = {"dp": dp + 1 - 2 * core}, {"section": 1 - section}
    barrier = pltpu.get_barrier_semaphore()
    greeted = [{"expert": d} for d in (dxr, dxl, dzr, dzl)]
    if split:
        greeted.append(other_core)
    if sided:
        greeted.append(other_section)
    for to in greeted:
        pl.semaphore_signal(barrier, inc=1, device_id=to, device_id_type=MESH)
    pl.semaphore_wait(barrier, len(greeted))

    def send_to(i, src, dst, to):
        c = pltpu.make_async_remote_copy(
            src_ref=src, dst_ref=dst, send_sem=send.at[i], recv_sem=recv.at[i],
            device_id=to, device_id_type=MESH)
        c.start()
        return c

    def copy(i, src, dst, to):
        return send_to(i, src, dst, {"expert": to})

    forwards = []

    def forward(*piece):
        if split:
            there = out_ref.at[piece]
            forwards.append(send_to(45 + len(forwards), there, there, other_core))

    A, B = pl.ds(0, half), pl.ds(half, half)
    A0, A1 = pl.ds(0, quarter), pl.ds(quarter, quarter)
    B0, B1 = pl.ds(half, quarter), pl.ds(half + quarter, quarter)
    every = slice(None)
    began = []

    def pair(piece, to_r, to_l, src=None):
        out = []
        for to in (to_r, to_l):
            there = out_ref.at[piece]
            out.append(copy(len(began), there if src is None else src, there, to))
            began.append(out[-1])
        return out

    def single(piece, to):
        there = out_ref.at[piece]
        began.append(copy(len(began), there, there, to))
        return began[-1]

    a_r, a_l = pair((z, x, A), dxr, dxl, x_ref.at[A])
    b_r, b_l = pair((z, x, B), dzr, dzl, x_ref.at[B])
    c_r, c_l = pair((z, x, A), dzr, dzl, x_ref.at[A])
    d_r, d_l = pair((z, x, B), dxr, dxl, x_ref.at[B])
    if sided:
        swap = send_to(44, side_ref, side_out, other_section)
    a_r.wait_recv()
    a2_r = single((z, xl, A0), dxr)
    c1_r, c1_l = pair((z, xl, A), dzr, dzl)
    a_l.wait_recv()
    a2_l = single((z, xr, A1), dxl)
    c2_r, c2_l = pair((z, xr, A), dzr, dzl)
    b_r.wait_recv()
    b2_r = single((zl, x, B0), dzr)
    d1_r, d1_l = pair((zl, x, B), dxr, dxl)
    b_l.wait_recv()
    b2_l = single((zr, x, B1), dzl)
    d2_r, d2_l = pair((zr, x, B), dxr, dxl)
    last = []
    c_r.wait_recv()
    last.append(single((zl, x, A0), dzr))
    c_l.wait_recv()
    last.append(single((zr, x, A1), dzl))
    d_r.wait_recv()
    last.append(single((z, xl, B0), dxr))
    d_l.wait_recv()
    last.append(single((z, xr, B1), dxl))
    a2_r.wait_recv()
    c3_r, c3_l = pair((z, x2, A0), dzr, dzl)
    a2_l.wait_recv()
    c4_r, c4_l = pair((z, x2, A1), dzr, dzl)
    b2_r.wait_recv()
    d3_r, d3_l = pair((z2, x, B0), dxr, dxl)
    b2_l.wait_recv()
    d4_r, d4_l = pair((z2, x, B1), dxr, dxl)
    c1_r.wait_recv()
    last.append(single((zl, xl, A0), dzr))
    c1_l.wait_recv()
    last.append(single((zr, xl, A1), dzl))
    d1_r.wait_recv()
    last.append(single((zl, xl, B0), dxr))
    d1_l.wait_recv()
    last.append(single((zl, xr, B1), dxl))
    own.wait()
    forward(z, every, A)
    forward(every, x, B)
    c2_r.wait_recv()
    last.append(single((zl, xr, A0), dzr))
    c2_l.wait_recv()
    last.append(single((zr, xr, A1), dzl))
    d2_r.wait_recv()
    last.append(single((zr, xl, B0), dxr))
    d2_l.wait_recv()
    last.append(single((zr, xr, B1), dxl))
    c3_r.wait_recv()
    last.append(single((zl, x2, A0), dzr))
    c4_l.wait_recv()
    last.append(single((zr, x2, A1), dzl))
    d3_r.wait_recv()
    last.append(single((z2, xl, B0), dxr))
    d4_l.wait_recv()
    last.append(single((z2, xr, B1), dxl))
    c3_l.wait_recv()
    c4_r.wait_recv()
    forward(zl, every, A)
    forward(zr, every, A)
    d3_l.wait_recv()
    d4_r.wait_recv()
    forward(every, xl, B)
    forward(every, xr, B)
    for c in last:
        c.wait_recv()
    forward(z2, every, A)
    forward(every, x2, B)
    for c in began:
        c.wait_send()
    for c in forwards + ([swap] if sided else []):
        c.wait_recv()
        c.wait_send()
    for c in locals_:
        c.wait()


def gather_call(ident, kind, outs, in_memory, *args):
    anywhere, memory = pl.BlockSpec(memory_space=pl.ANY), pl.BlockSpec(memory_space=pltpu.VMEM)
    return pl.pallas_call(
        functools.partial(gather_kernel, kind),
        out_shape=outs,
        in_specs=[memory if held else anywhere for held in in_memory],
        out_specs=[anywhere] * len(outs),
        scratch_shapes=[
            pltpu.SemaphoreType.DMA((53,)),
            pltpu.SemaphoreType.DMA((53,)),
            pltpu.SemaphoreType.DMA((7,)),
        ],
        compiler_params=pltpu.CompilerParams(
            collective_id=ident, has_side_effects=True, vmem_limit_bytes=56 << 20),
        name="gather_" + kind,
    )(*args)


def gather_rows(x, ident):
    rows, cols = x.shape
    out = gather_call(ident, "plain", [jax.ShapeDtypeStruct((4, 4, rows, cols), x.dtype)], (True,), x)[0]
    return out.reshape(16 * rows, cols)


def gather_swap(x, side, ident):
    rows, cols = x.shape
    out, side_out = gather_call(
        ident, "swap",
        [jax.ShapeDtypeStruct((4, 4, rows, cols), x.dtype), jax.ShapeDtypeStruct(side.shape, side.dtype)],
        (True, False), x, side)
    return out.reshape(16 * rows, cols), side_out


def gather_split(x, ident):
    rows, cols = x.shape
    out = gather_call(ident, "split", [jax.ShapeDtypeStruct((2, 4, 4, rows, cols), x.dtype)], (True,), x)[0]
    return out.reshape(2, 16, rows, cols)


def gather_weights(x, side, wq, wk, wv, wo, ident):
    rows, cols = x.shape
    parts = [w.reshape(4, 4, 64, w.shape[1]) for w in (wq, wk, wv, wo)]
    out, side_out = gather_call(
        ident, "weights",
        [jax.ShapeDtypeStruct((2, 2, 4, 4, rows, cols), x.dtype), jax.ShapeDtypeStruct(side.shape, side.dtype)],
        (True, False) + (True,) * 4, x, side, *parts)
    return out.reshape(2, 2, 16, rows, cols), side_out


def scatter_kernel(split, x_ref, *refs):
    if split:
        side_ref, out_ref, side_out, loc, land = refs[:5]
        core_send, core_recv = refs[-2:]
        refs = refs[5:-2]
    else:
        out_ref, loc = refs[:2]
        refs = refs[2:]
    s1, l1, l2, t0, m1, n1, m2, send, recv, loc_sem = refs
    z, x, xr, xl, zr, zl, (dxr, dxl, dzr, dzl) = ring_places()
    x2, z2 = lax.rem(x + 2, 4), lax.rem(z + 2, 4)
    dp = lax.axis_index("dp")
    core = lax.rem(dp, 2)
    rows = x_ref.shape[-2]
    half, quarter = rows // 2, rows // 4
    A0, A1 = pl.ds(0, quarter), pl.ds(quarter, quarter)
    B0, B1 = pl.ds(half, quarter), pl.ds(half + quarter, quarter)
    every = slice(None)
    pieces = (
        (z2, every, A0), (z2, every, A1), (every, x2, B0), (every, x2, B1),
        (zr, every, A1), (zl, every, A0), (every, xr, B1), (every, xl, B0),
        (zr, every, A0), (zl, every, A1), (every, xr, B0), (every, xl, B1),
        (z, every, A0), (z, every, A1), (every, x, B0), (every, x, B1),
    )
    part = x_ref.at[core] if split else x_ref
    skip = 0 if split else 8
    held = []
    for i, piece in enumerate(pieces[skip:]):
        c = pltpu.make_async_copy(part.at[piece], loc.at[i], loc_sem.at[i])
        c.start()
        held.append(c)
    other_core, other_section = {"dp": dp + 1 - 2 * core}, {"section": 1 - lax.axis_index("section")}
    barrier = pltpu.get_barrier_semaphore()
    greeted = [{"expert": d} for d in (dxr, dxl, dzr, dzl)] + ([other_core, other_section] if split else [])
    for to in greeted:
        pl.semaphore_signal(barrier, inc=1, device_id=to, device_id_type=MESH)
    pl.semaphore_wait(barrier, len(greeted))
    away = []
    if split:
        for i, piece in enumerate(pieces):
            c = pltpu.make_async_remote_copy(
                src_ref=x_ref.at[(1 - core,) + piece], dst_ref=land.at[i], send_sem=core_send.at[i],
                recv_sem=core_recv.at[i], device_id=other_core, device_id_type=MESH)
            c.start()
            away.append(c)
        swap = pltpu.make_async_remote_copy(
            src_ref=side_ref, dst_ref=side_out, send_sem=core_send.at[16], recv_sem=core_recv.at[16],
            device_id=other_section, device_id_type=MESH)
        swap.start()

    def copy(i, src, dst, to):
        c = pltpu.make_async_remote_copy(
            src_ref=src, dst_ref=dst, send_sem=send.at[i], recv_sem=recv.at[i],
            device_id={"expert": to}, device_id_type=MESH)
        c.start()
        return c

    def total(*parts):
        acc = parts[0].astype(f32)
        for p in parts[1:]:
            acc = acc + p.astype(f32)
        return acc

    def ready(i):
        if i < skip:
            return x_ref.at[pieces[i]]
        held[i - skip].wait()
        if split:
            away[i].wait_recv()
            loc[i] = total(loc[i], land[i]).astype(bf16)
        return loc.at[i - skip]

    c0 = copy(0, ready(0), l1.at[0], dzr)
    c1 = copy(1, ready(1), l1.at[1], dzl)
    c2 = copy(2, ready(2), l1.at[2], dxr)
    c3 = copy(3, ready(3), l1.at[3], dxl)
    c4 = copy(4, ready(4), l2.at[0, 1], dzr)
    c5 = copy(5, ready(5), l2.at[1, 0], dzl)
    c6 = copy(6, ready(6), l2.at[2, 1], dxr)
    c7 = copy(7, ready(7), l2.at[3, 0], dxl)
    mine = ready(8)
    c0.wait_recv()
    s1[0] = total(mine[...], l1[0]).astype(bf16)
    c8 = copy(8, s1.at[0], l2.at[0, 0], dzr)
    mine = ready(9)
    c1.wait_recv()
    s1[1] = total(mine[...], l1[1]).astype(bf16)
    c9 = copy(9, s1.at[1], l2.at[1, 1], dzl)
    mine = ready(10)
    c2.wait_recv()
    s1[2] = total(mine[...], l1[2]).astype(bf16)
    c10 = copy(10, s1.at[2], l2.at[2, 0], dxr)
    mine = ready(11)
    c3.wait_recv()
    s1[3] = total(mine[...], l1[3]).astype(bf16)
    c11 = copy(11, s1.at[3], l2.at[3, 1], dxl)
    mine = ready(13)
    c4.wait_recv()
    c9.wait_recv()
    t0[0, 1] = total(mine[...], l2[0, 1], l2[1, 1]).astype(bf16)
    mine = ready(12)
    c5.wait_recv()
    c8.wait_recv()
    t0[0, 0] = total(mine[...], l2[0, 0], l2[1, 0]).astype(bf16)
    e0 = copy(12, t0.at[0, 0, x2], m1.at[0], dxr)
    e1 = copy(13, t0.at[0, 1, x2], m1.at[1], dxl)
    e4 = copy(14, t0.at[0, 1, xr], m2.at[0, 1], dxr)
    e5 = copy(15, t0.at[0, 0, xl], m2.at[1, 0], dxl)
    mine = ready(15)
    c6.wait_recv()
    c11.wait_recv()
    t0[1, 1] = total(mine[...], l2[2, 1], l2[3, 1]).astype(bf16)
    mine = ready(14)
    c7.wait_recv()
    c10.wait_recv()
    t0[1, 0] = total(mine[...], l2[2, 0], l2[3, 0]).astype(bf16)
    e2 = copy(16, t0.at[1, 0, z2], m1.at[2], dzr)
    e3 = copy(17, t0.at[1, 1, z2], m1.at[3], dzl)
    e6 = copy(18, t0.at[1, 1, zr], m2.at[2, 1], dzr)
    e7 = copy(19, t0.at[1, 0, zl], m2.at[3, 0], dzl)
    e0.wait_recv()
    n1[0] = total(t0[0, 0, xr], m1[0]).astype(bf16)
    e8 = copy(20, n1.at[0], m2.at[0, 0], dxr)
    e1.wait_recv()
    n1[1] = total(t0[0, 1, xl], m1[1]).astype(bf16)
    e9 = copy(21, n1.at[1], m2.at[1, 1], dxl)
    e2.wait_recv()
    n1[2] = total(t0[1, 0, zr], m1[2]).astype(bf16)
    e10 = copy(22, n1.at[2], m2.at[2, 0], dzr)
    e3.wait_recv()
    n1[3] = total(t0[1, 1, zl], m1[3]).astype(bf16)
    e11 = copy(23, n1.at[3], m2.at[3, 1], dzl)
    e4.wait_recv()
    e9.wait_recv()
    out_ref[A1] = total(t0[0, 1, x], m2[0, 1], m2[1, 1])
    e5.wait_recv()
    e8.wait_recv()
    out_ref[A0] = total(t0[0, 0, x], m2[0, 0], m2[1, 0])
    e6.wait_recv()
    e11.wait_recv()
    out_ref[B1] = total(t0[1, 1, z], m2[2, 1], m2[3, 1])
    e7.wait_recv()
    e10.wait_recv()
    out_ref[B0] = total(t0[1, 0, z], m2[2, 0], m2[3, 0])
    for c in (c0, c1, c2, c3, c4, c5, c6, c7, c8, c9, c10, c11,
              e0, e1, e2, e3, e4, e5, e6, e7, e8, e9, e10, e11):
        c.wait_send()
    for c in away:
        c.wait_send()
    if split:
        swap.wait_recv()
        swap.wait_send()


def scatter_sum(x, ident, side=None):
    split = side is not None
    anywhere = pl.BlockSpec(memory_space=pl.ANY)
    summed, held = jax.ShapeDtypeStruct((x.shape[-2] // 16, x.shape[-1]), f32), whole()
    rows, cols = x.shape[-2] // 16, x.shape[-1]
    q = rows // 4
    piece = (4, q, cols)
    count = 16 if split else 8
    scratch = [pltpu.VMEM((count,) + piece, bf16)]
    if split:
        scratch.append(pltpu.VMEM((16,) + piece, bf16))
    scratch += [
        pltpu.VMEM((4,) + piece, bf16),
        pltpu.VMEM((4,) + piece, bf16),
        pltpu.VMEM((4, 2) + piece, bf16),
        pltpu.VMEM((2, 2) + piece, bf16),
        pltpu.VMEM(piece, bf16),
        pltpu.VMEM(piece, bf16),
        pltpu.VMEM((4, 2, q, cols), bf16),
        pltpu.SemaphoreType.DMA((24,)),
        pltpu.SemaphoreType.DMA((24,)),
        pltpu.SemaphoreType.DMA((count,)),
    ]
    if split:
        scratch += [pltpu.SemaphoreType.DMA((17,)), pltpu.SemaphoreType.DMA((17,))]
    return pl.pallas_call(
        functools.partial(scatter_kernel, split),
        out_shape=[summed, jax.ShapeDtypeStruct(side.shape, side.dtype)] if split else summed,
        in_specs=[anywhere] * (2 if split else 1),
        out_specs=[held, anywhere] if split else held,
        scratch_shapes=scratch,
        compiler_params=pltpu.CompilerParams(
            collective_id=ident, has_side_effects=True, vmem_limit_bytes=56 << 20),
        name="scatter_split" if split else "scatter_sum",
    )(x.reshape(x.shape[:-2] + (4, 4, rows, cols)), *([side] if split else []))


def spec(shape, index):
    return pl.BlockSpec(shape, index)


def fixed(shape):
    return pl.BlockSpec(shape, lambda *_: (0,) * len(shape), pipeline_mode=pl.Buffered(1))


def whole():
    return pl.BlockSpec(memory_space=pltpu.VMEM)


def local_call(kernel, outs, name, grid=None, in_specs=None, out_specs=None, flops=0, moved=0):
    params = pltpu.CompilerParams(vmem_limit_bytes=60 << 20)
    kinds = dict(
        out_shape=[jax.ShapeDtypeStruct(s, d) for s, d in outs],
        compiler_params=params,
        name=name,
        cost_estimate=pl.CostEstimate(flops=flops, bytes_accessed=moved, transcendentals=0),
    )
    if grid is None:
        kinds["out_specs"] = [spec(s, lambda i, n=len(s): (0,) * n) for s, _ in outs]
        blocks = in_specs or {}

        def call(*args):
            ins = [blocks.get(i) or spec(a.shape, lambda i, n=a.ndim: (0,) * n) for i, a in enumerate(args)]
            return pl.pallas_call(kernel, grid=(1,), in_specs=ins, **kinds)(*args)

        return call
    return pl.pallas_call(kernel, grid=grid, in_specs=in_specs, out_specs=out_specs, **kinds)


def dot(a, b):
    return jnp.dot(a, b, preferred_element_type=f32)


def dot_t(a, b):
    return lax.dot_general(a, b, (((1,), (1,)), ((), ())), preferred_element_type=f32)


def t_dot(a, b):
    return lax.dot_general(a, b, (((0,), (0,)), ((), ())), preferred_element_type=f32)


def lanes(shape):
    return lax.broadcasted_iota(jnp.int32, shape, len(shape) - 1)


def turned(u, cosine, sine):
    chunks = []
    for c in range(u.shape[1] // 128):
        part = u[:, 128 * c : 128 * c + 128]
        low = lax.rem(lanes(part.shape), 64) < 32
        rot = jnp.where(low, -pltpu.roll(part, 96, 1), pltpu.roll(part, 32, 1))
        chunks.append(part * cosine + rot * sine)
    return jnp.concatenate(chunks, axis=1)


def rms(x):
    return lax.rsqrt(jnp.mean(x * x, axis=-1, keepdims=True) + norm_eps)


def halves(w_ref, row):
    return tuple(w_ref[0, h, :, row : row + 64, 0:512].reshape(1024, 512) for h in range(2))


def pre_kernel(x_ref, gain_ref, cos_ref, sin_ref, w_ref, a_ref, q_ref, kv_ref):
    x = x_ref[...].astype(f32)
    a = (x * rms(x) * gain_ref[...]).astype(bf16)
    a_ref[...] = a
    cosine, sine = cos_ref[...], sin_ref[...]
    for h, w in enumerate(halves(w_ref, 0)):
        q_ref[:, 512 * h : 512 * h + 512] = turned(dot(a, w), cosine, sine).astype(bf16)
    wk, wv = halves(w_ref, 64)
    kv_ref[:, :512] = turned(dot(a, wk), cosine, sine).astype(bf16)
    kv_ref[:, 512:] = dot(a, wv).astype(bf16)


def head_rows(q):
    q = q.astype(f32)
    left, right = q[:, :128], q[:, 128:]
    low = lanes(left.shape) < 64
    parts = [
        jnp.where(low, left, 0.0),
        jnp.where(low, pltpu.roll(left, 64, 1), 0.0),
        jnp.where(low, 0.0, pltpu.roll(right, 64, 1)),
        jnp.where(low, 0.0, right),
    ]
    return parts


def head_lanes(p0, p1, p2, p3):
    low = lanes(p0.shape) < 64
    left = jnp.where(low, p0, pltpu.roll(p1, 64, 1))
    right = jnp.where(low, pltpu.roll(p2, 64, 1), p3)
    return jnp.concatenate([left, right], axis=1)


def attend_kernel(q_ref, k_ref, v_ref, lo_ref, hi_ref, o_ref, p_ref):
    key = lax.broadcasted_iota(jnp.int32, (128, 2048), 1)
    seen = (key >= lo_ref[...]) & (key <= hi_ref[...])
    k, v = k_ref[...], v_ref[...]
    outs = []
    for h, q in enumerate(head_rows(q_ref[...])):
        s = dot_t((q * 0.125).astype(bf16), k)
        s = jnp.where(seen, s, masked_score)
        e = jnp.exp(s - jnp.max(s, axis=-1, keepdims=True))
        p = (e * (1.0 / jnp.sum(e, axis=-1, keepdims=True))).astype(bf16)
        p_ref[0, 128 * h : 128 * h + 128, :] = p
        outs.append(dot(p, v))
    o_ref[...] = head_lanes(*outs).astype(bf16)


def attend(q, kv, lo, hi):
    return local_call(
        attend_kernel,
        [((128, 1024), bf16), ((4, 512, 2048), bf16)],
        "attend",
        grid=(4,),
        in_specs=[
            spec((128, 256), lambda i: (0, i)),
            spec((2048, 128), lambda i: (0, i)),
            spec((2048, 128), lambda i: (0, i + 4)),
            fixed((128, 1)),
            fixed((128, 1)),
        ],
        out_specs=[
            spec((128, 256), lambda i: (0, i)),
            spec((1, 512, 2048), lambda i: (i, 0, 0)),
        ],
        flops=2 * 2 * 2048 * 2048 * 128,
        moved=13 << 20,
    )(q, kv, kv, lo, hi)


def attend_back_kernel(q_ref, o_ref, do_ref, k_ref, v_ref, p_ref, dq_ref, dkv_ref):
    k, v = k_ref[...], v_ref[...]
    do = do_ref[...]
    prod = do.astype(f32) * o_ref[...].astype(f32)
    low = lanes((128, 128)) < 64
    left, right = prod[:, :128], prod[:, 128:]
    deltas = [
        jnp.sum(jnp.where(low, left, 0.0), axis=1, keepdims=True),
        jnp.sum(jnp.where(low, 0.0, left), axis=1, keepdims=True),
        jnp.sum(jnp.where(low, right, 0.0), axis=1, keepdims=True),
        jnp.sum(jnp.where(low, 0.0, right), axis=1, keepdims=True),
    ]
    do_rows = [r.astype(bf16) for r in head_rows(do)]
    q_rows = [(r * 0.125).astype(bf16) for r in head_rows(q_ref[...])]
    dqs, dss = [], []
    for h in range(4):
        dp = dot_t(do_rows[h], v)
        p = p_ref[0, 128 * h : 128 * h + 128, :].astype(f32)
        ds = (p * (dp - deltas[h])).astype(bf16)
        dss.append(ds)
        dqs.append(dot(ds, k) * 0.125)
    dq_ref[...] = head_lanes(*dqs)
    dkv_ref[:, :128] = t_dot(jnp.concatenate(dss, axis=0), jnp.concatenate(q_rows, axis=0)).astype(bf16)
    dkv_ref[:, 128:] = t_dot(p_ref[0], jnp.concatenate(do_rows, axis=0)).astype(bf16)


def attend_back(q, o, do, kv, probs):
    side = spec((128, 256), lambda i: (0, i))
    return local_call(
        attend_back_kernel,
        [((128, 1024), f32), ((2048, 1024), bf16)],
        "attend_back",
        grid=(4,),
        in_specs=[
            side,
            side,
            side,
            spec((2048, 128), lambda i: (0, i)),
            spec((2048, 128), lambda i: (0, i + 4)),
            spec((1, 512, 2048), lambda i: (i, 0, 0)),
        ],
        out_specs=[side, spec((2048, 256), lambda i: (0, i))],
        flops=4 * 2 * 2048 * 2048 * 128,
        moved=17 << 20,
    )(q, o, do, kv, kv, probs)


def post_kernel(x_ref, o_ref, wo_ref, gain_ref, h_ref, b_ref):
    o = o_ref[...]
    h = x_ref[...].astype(f32) + jnp.concatenate([dot(o, w) for w in halves(wo_ref, 0)], axis=1)
    h_ref[...] = h
    b_ref[...] = (h * rms(h) * gain_ref[...]).astype(bf16)


def chosen_gates(b, wr, mask):
    logits = dot(b, wr)
    chosen = mask.astype(f32) > 0.5
    top = jnp.max(jnp.where(chosen, logits, masked_score), axis=-1, keepdims=True)
    e = jnp.where(chosen, jnp.exp(jnp.where(chosen, logits - top, 0.0)), 0.0)
    return e / jnp.sum(e, axis=-1, keepdims=True)


SLOTS = 80
ROWS = 1024


def experts_kernel(b_ref, mask_ref, wr_ref, pick_ref, w0_ref, w1_ref, y_ref, x_ref, gu_ref, s_ref, gate_ref):
    row, col = lax.broadcasted_iota(jnp.int32, (256, 256), 0), lanes((256, 256))
    before = ((row < col) & ((row < 128) == (col < 128))).astype(bf16)
    slot_ids = lax.broadcasted_iota(jnp.int32, (SLOTS, 256), 0)
    second = jnp.where(lanes((1, 256)) < 128, 0.0, SLOTS // 2)
    for p in range(ROWS // 256):
        b = b_ref[256 * p : 256 * p + 256, :]
        mask = mask_ref[:, 256 * p : 256 * p + 256]
        chosen = mask.astype(f32) > 0.5
        logits = dot_t(wr_ref[...], b)
        top = jnp.max(jnp.where(chosen, logits, masked_score), axis=0, keepdims=True)
        e = jnp.where(chosen, jnp.exp(jnp.where(chosen, logits - top, 0.0)), 0.0)
        gates = e / jnp.sum(e, axis=0, keepdims=True)
        rank = dot(mask, before)
        for j in range(2):
            one = pick_ref[:, j : j + 1]
            gate = jnp.sum(gates * one, axis=0, keepdims=True)
            used = jnp.sum(mask.astype(f32) * one, axis=0, keepdims=True)
            place = jnp.sum(rank * one, axis=0, keepdims=True) + second
            hit = (slot_ids == place.astype(jnp.int32)) & (used > 0.5)
            s = jnp.where(hit, 1.0, 0.0)
            part = slice(SLOTS * p, SLOTS * p + SLOTS)
            gate_ref[j, part, :] = jnp.sum(s * gate, axis=1, keepdims=True)
            s_ref[p, SLOTS * j : SLOTS * j + SLOTS, :] = s.astype(bf16)
        rows = dot(s_ref[p], b).astype(bf16)
        for j in range(2):
            x_ref[j, part, :] = rows[SLOTS * j : SLOTS * j + SLOTS]
    ys = []
    for j in range(2):
        x = x_ref[j]
        g = dot(x, (w0_ref, w1_ref)[j][0, :, 0:512])
        u = dot(x, (w0_ref, w1_ref)[j][0, :, 512:1024])
        gu_ref[j, :, 0:512] = g.astype(bf16)
        gu_ref[j, :, 512:1024] = u.astype(bf16)
        inner = g * jax.nn.sigmoid(g) * u
        ys.append(dot_t((inner * gate_ref[j]).astype(bf16), (w0_ref, w1_ref)[j][0, :, 1024:1536]).astype(bf16))
    for p in range(ROWS // 256):
        part = slice(SLOTS * p, SLOTS * p + SLOTS)
        both = jnp.concatenate([ys[0][part], ys[1][part]], axis=0)
        y_ref[256 * p : 256 * p + 256, :] = t_dot(s_ref[p], both).astype(bf16)


HALF = SLOTS * ROWS // 256
FULL = 2 * HALF


def compact(cols):
    return spec((2, HALF, cols), lambda i: (0, i, 0))


def tokens(cols):
    return spec((ROWS, cols), lambda i: (i, 0))


choice = spec((ROWS // 256, 2 * SLOTS, 256), lambda i: (i, 0, 0))


def experts(b_all, mask_all, wr, pick, w):
    rows = b_all.shape[0]
    return local_call(
        experts_kernel,
        [
            ((rows, 1024), bf16), ((2, FULL, 1024), bf16), ((2, FULL, 1024), bf16),
            ((rows // 256, 2 * SLOTS, 256), bf16), ((2, FULL, 1), f32),
        ],
        "experts",
        grid=(rows // ROWS,),
        in_specs=[
            tokens(1024),
            spec((32, ROWS), lambda i: (0, i)),
            fixed((32, 1024)),
            fixed((32, 8)),
            fixed((1, 1024, 1536)),
            fixed((1, 1024, 1536)),
        ],
        out_specs=[tokens(1024), compact(1024), compact(1024), choice, compact(1)],
        flops=8 * 2 * 1280 * 1024 * 512,
        moved=20 << 20,
    )(b_all, mask_all, wr, pick, *w)


def experts_back_kernel(
    dout_ref, s_ref, gu_ref, gate_ref, wcol_ref, w0_ref, w1_ref, db_ref, d_ref, dgu_ref, in_ref, coef_ref
):
    for p in range(ROWS // 256):
        rows = dot(s_ref[p], dout_ref[256 * p : 256 * p + 256, :]).astype(bf16)
        for j in range(2):
            d_ref[j, SLOTS * p : SLOTS * p + SLOTS, :] = rows[SLOTS * j : SLOTS * j + SLOTS]
    dbs = []
    for j in range(2):
        gate = gate_ref[j]
        g = gu_ref[j, :, 0:512].astype(f32)
        u = gu_ref[j, :, 512:1024].astype(f32)
        back = dot(d_ref[j], (w0_ref, w1_ref)[j][0, :, 1024:1536])
        sig = jax.nn.sigmoid(g)
        silu = g * sig
        inner = silu * u
        coef = gate * jnp.sum(inner * back, axis=1, keepdims=True)
        coef_ref[j] = coef
        in_ref[j] = (inner * gate).astype(bf16)
        dinner = back * gate
        dg = (dinner * u * sig * (1.0 + g * (1.0 - sig))).astype(bf16)
        du = (dinner * silu).astype(bf16)
        dgu_ref[j, :, 0:512] = dg
        dgu_ref[j, :, 512:1024] = du
        db = dot_t(dg, (w0_ref, w1_ref)[j][0, :, 0:512]) + dot_t(du, (w0_ref, w1_ref)[j][0, :, 512:1024])
        dbs.append((db + coef * wcol_ref[j : j + 1, :]).astype(bf16))
    for p in range(ROWS // 256):
        part = slice(SLOTS * p, SLOTS * p + SLOTS)
        both = jnp.concatenate([dbs[0][part], dbs[1][part]], axis=0)
        db_ref[256 * p : 256 * p + 256, :] = t_dot(s_ref[p], both).astype(bf16)


def experts_back(dout_all, choices, gu, gate, wcol, w):
    rows = dout_all.shape[0]
    return local_call(
        experts_back_kernel,
        [
            ((rows, 1024), bf16), ((2, FULL, 1024), bf16), ((2, FULL, 1024), bf16),
            ((2, FULL, 512), bf16), ((2, FULL, 1), f32),
        ],
        "experts_back",
        grid=(rows // ROWS,),
        in_specs=[
            tokens(1024), choice, compact(1024), compact(1), fixed((8, 1024)), fixed((1, 1024, 1536)),
            fixed((1, 1024, 1536)),
        ],
        out_specs=[tokens(1024), compact(1024), compact(1024), compact(512), compact(1)],
        flops=8 * 2 * 1280 * 1024 * 512,
        moved=24 << 20,
    )(dout_all, choices, gu, gate, wcol, *w)


def expert_grads_kernel(x_ref, d_ref, dgu_ref, in_ref, out_ref):
    out_ref[0, :, 0:1024] = t_dot(x_ref[0], dgu_ref[0]).astype(bf16)
    out_ref[0, :, 1024:1536] = t_dot(d_ref[0], in_ref[0]).astype(bf16)


def expert_grads(x, d, dgu, inner):
    def one(cols):
        return spec((1, FULL, cols), lambda j: (j, 0, 0))

    return local_call(
        expert_grads_kernel,
        [((2, 1024, 1536), bf16)],
        "expert_grads",
        grid=(2,),
        in_specs=[one(1024), one(1024), one(1024), one(512)],
        out_specs=[spec((1, 1024, 1536), lambda j: (j, 0, 0))],
        flops=3 * 2 * 1280 * 1024 * 512,
        moved=16 << 20,
    )(x, d, dgu, inner)[0]


def mid_back_kernel(
    sum_ref, dout_ref, mix_ref, h_ref, b_ref, gain_ref, wr_ref, mask_ref, wo_ref,
    dh_ref, dattn_ref, do_ref, router_ref, gain_grad_ref,
):
    dout = dout_ref[...].astype(f32)
    b = b_ref[...]
    wr = wr_ref[...]
    h = h_ref[...]
    r = rms(h)
    n = h * r
    gates = chosen_gates(b, wr, mask_ref[...])
    level = jnp.sum(dout * mix_ref[...], axis=-1, keepdims=True)
    taken = (gates * -level).astype(bf16)
    router_ref[...] = t_dot(taken, b)
    db = sum_ref[...] + dot_t(taken, wr)
    gain_grad_ref[...] = jnp.broadcast_to(jnp.sum(db * n, axis=0, keepdims=True), gain_grad_ref.shape)
    ng = db * gain_ref[...]
    dh = dout + r * (ng - n * jnp.mean(ng * n, axis=-1, keepdims=True))
    dh_ref[...] = dh
    dattn = dh.astype(bf16)
    dattn_ref[...] = dattn
    w0, w1 = halves(wo_ref, 0)
    do_ref[...] = (dot_t(dattn[:, :512], w0) + dot_t(dattn[:, 512:], w1)).astype(bf16)


def end_back_kernel(
    dq_ref, dkv_ref, cos_ref, sin_ref, w_ref, x_ref, gain_ref, dh_ref,
    dq_lin_ref, dkv_lin_ref, dx_ref, gain_grad_ref,
):
    cosine, sine = cos_ref[...], -sin_ref[...]
    dq = turned(dq_ref[...], cosine, sine).astype(bf16)
    dkv = dkv_ref[...]
    dk = jnp.concatenate([dkv[:, 256 * i : 256 * i + 128] for i in range(4)], axis=1)
    dv = jnp.concatenate([dkv[:, 256 * i + 128 : 256 * i + 256] for i in range(4)], axis=1)
    dk = turned(dk, cosine, sine).astype(bf16)
    dv = dv.astype(bf16)
    dq_lin_ref[...] = dq
    dkv_lin_ref[:, :512] = dk
    dkv_lin_ref[:, 512:] = dv
    (q0, q1), (wk, wv) = halves(w_ref, 0), halves(w_ref, 64)
    da = dot_t(dq[:, :512], q0) + dot_t(dq[:, 512:], q1) + dot_t(dk, wk) + dot_t(dv, wv)
    x = x_ref[...].astype(f32)
    r = rms(x)
    n = x * r
    gain_grad_ref[...] = jnp.broadcast_to(jnp.sum(da * n, axis=0, keepdims=True), gain_grad_ref.shape)
    ng = da * gain_ref[...]
    dx = dh_ref[...] + r * (ng - n * jnp.mean(ng * n, axis=-1, keepdims=True))
    dx_ref[...] = dx.astype(bf16)


def dense_grads_kernel(*refs):
    small_ref, out_ref = refs[10:]
    for layer in range(2):
        a_ref, o_ref, dq_ref, dkv_ref, dattn_ref = refs[5 * layer : 5 * layer + 5]
        a = a_ref[...]
        gq = t_dot(a, dq_ref[...]).astype(bf16)
        gkv = t_dot(a, dkv_ref[...]).astype(bf16)
        go = t_dot(o_ref[...], dattn_ref[...]).astype(bf16)
        cols = slice(512 * layer, 512 * layer + 512)
        for t in range(4):
            part = slice(64 * t, 64 * t + 64)
            for h in range(2):
                side = slice(512 * h, 512 * h + 512)
                out_ref[h, t, 0:64, cols] = gq[part, side]
                out_ref[h, t, 64:128, cols] = gkv[part, side]
                out_ref[h, t, 128:192, cols] = go[part, side]
    for h in range(2):
        for t in (0, 2):
            out_ref[h, t, 0:64, 1024:1152] = small_ref[h, :, 64 * t : 64 * t + 128]
            out_ref[h, t, 64:192, 1024:1152] = jnp.zeros((128, 128), bf16)
            out_ref[h, t + 1, :, 1024:1152] = jnp.zeros((192, 128), bf16)


def dense_grads(layer0, layer1, small):
    narrow = spec((128, 256), lambda i: (0, i))
    out = local_call(
        dense_grads_kernel,
        [((2, 16, 192, 1152), bf16)],
        "dense_grads",
        grid=(4,),
        in_specs=([narrow, narrow] + [fixed((128, 1024))] * 3) * 2 + [spec((2, 64, 256), lambda i: (0, 0, i))],
        out_specs=[spec((2, 4, 192, 1152), lambda i: (0, i, 0, 0))],
        flops=6 * 2 * 128 * 1024 * 1024,
        moved=18 << 20,
    )(*layer0, *layer1, small)[0]
    return out.reshape(2, 3072, 1152)


def cross_kernel(own_ref, other_ref, out_ref, land, mine, send, recv):
    section, dp = lax.axis_index("section"), lax.axis_index("dp")
    partners = (
        {"section": 1 - section},
        {"dp": lax.rem(dp + 2, 4)},
    )
    barrier = pltpu.get_barrier_semaphore()
    for to in partners:
        pl.semaphore_signal(barrier, inc=1, device_id=to, device_id_type=MESH)
    pl.semaphore_wait(barrier, 2)
    copies = []
    for i, to in enumerate(partners):
        src = other_ref if i == 0 else mine
        c = pltpu.make_async_remote_copy(
            src_ref=src, dst_ref=land.at[i], send_sem=send.at[i], recv_sem=recv.at[i],
            device_id=to, device_id_type=MESH)
        c.start()
        copies.append(c)
        c.wait_recv()
        before = own_ref[...] if i == 0 else mine[...].astype(f32)
        after = (before + land[i].astype(f32)).astype(bf16)
        if i == 0:
            mine[...] = after
        else:
            out_ref[...] = after
    for c in copies:
        c.wait_send()


def cross_sum(own, other, ident):
    rows, cols = own.shape
    return pl.pallas_call(
        cross_kernel,
        out_shape=jax.ShapeDtypeStruct((rows, cols), bf16),
        in_specs=[whole(), whole()],
        out_specs=whole(),
        scratch_shapes=[
            pltpu.VMEM((2, rows, cols), bf16),
            pltpu.VMEM((rows, cols), bf16),
            pltpu.SemaphoreType.DMA((2,)),
            pltpu.SemaphoreType.DMA((2,)),
        ],
        compiler_params=pltpu.CompilerParams(
            collective_id=ident, has_side_effects=True, vmem_limit_bytes=24 << 20),
        name="cross_sum",
    )(own, other)


def qkv_block(layer):
    return spec((1, 2, 16, 128, 640), lambda i: (layer, 0, 0, 0, 0))


def out_block(layer):
    return spec((1, 2, 16, 64, 640), lambda i: (layer, 0, 0, 2, 0))


def forward(x, layer, place, weights, dense, w, masks):
    cosine, sine, lo, hi, pick, _ = place
    gain_attn, gain_moe, wr = dense
    a, q, kv = local_call(
        pre_kernel, [((128, 1024), bf16)] * 3, "pre", in_specs={4: qkv_block(layer)},
        flops=2 * 128 * 1024 * 2048, moved=6 << 20,
    )(x, gain_attn, cosine, sine, weights)
    if callable(w):
        kv_all, w = w(kv)
    else:
        kv_all = gather_rows(kv, 1)
    o, probs = attend(q, kv_all, lo, hi)
    h, b = local_call(
        post_kernel, [((128, 1024), f32), ((128, 1024), bf16)], "post", in_specs={2: out_block(layer)},
        flops=2 * 128 * 1024 * 1024, moved=4 << 20,
    )(x, o, weights, gain_moe)
    b_all = gather_rows(b, 1)
    y, rows, gu, choices, gate = experts(b_all, masks[1], wr.T, pick, w)
    mix = scatter_sum(y, 2)
    out = (h + mix).astype(bf16)
    return out, w, (x, a, q, kv_all, o, probs, h, b, rows, gu, choices, gate, mix)


def backward(dout, dout_all, saved, layer, place, weights, dense, w, masks):
    cosine, sine, lo, hi, pick, pick_rows = place
    gain_attn, gain_moe, wr = dense
    x, a, q, kv_all, o, probs, h, b, rows, gu, choices, gate, mix = saved
    dout_all, mix = lax.optimization_barrier((dout_all, mix))
    wcol = dot_t(pick_rows.astype(bf16), wr)
    db_part, drows, dgu, inner, coef = experts_back(dout_all, choices, gu, gate, wcol, w)
    expert_grad = expert_grads(rows, drows, dgu, inner)
    db_part, expert_grad = lax.optimization_barrier((db_part, expert_grad))
    db_sum = scatter_sum(db_part, 2)
    expert_grad = lax.psum_scatter(expert_grad, "dp", scatter_dimension=1, tiled=True)
    router_cols = jnp.einsum("jrd,jr->jd", rows, coef[:, :, 0].astype(bf16), preferred_element_type=f32)
    router_part = jnp.einsum(
        "je,jd->ed", pick_rows[:2], router_cols, preferred_element_type=f32, precision=lax.Precision.HIGHEST)
    dh, dattn, do, router_own, gain_moe_grad = local_call(
        mid_back_kernel,
        [((128, 1024), f32), ((128, 1024), bf16), ((128, 1024), bf16), ((32, 1024), f32), ((8, 1024), f32)],
        "mid_back", in_specs={8: out_block(layer)}, flops=2 * 128 * 1024 * 1024, moved=5 << 20,
    )(db_sum, dout, mix, h, b, gain_moe, wr, masks[0], weights)
    dq, dkv = attend_back(q, o, do, kv_all, probs)
    dkv_sum = scatter_sum(dkv, 2)
    dq_lin, dkv_lin, dx, gain_attn_grad = local_call(
        end_back_kernel,
        [((128, 1024), bf16), ((128, 1024), bf16), ((128, 1024), bf16), ((8, 1024), f32)],
        "end_back", in_specs={4: qkv_block(layer)}, flops=2 * 128 * 1024 * 2048, moved=8 << 20,
    )(dq, dkv_sum, cosine, sine, weights, x, gain_attn, dh)
    small = jnp.concatenate(
        [router_part + router_own, gain_attn_grad[0:1], gain_moe_grad[0:1], jnp.zeros((30, 1024), f32)], axis=0
    ).astype(bf16)
    return dx, expert_grad, (a, o, dq_lin, dkv_lin, dattn), small


def results_kernel(s_ref, query_ref, key_ref, value_ref, out_ref):
    for h in range(2):
        side = slice(512 * h, 512 * h + 512)
        query_ref[:, side] = s_ref[h, :, 0:64, 0:512].reshape(256, 512).astype(f32)
        out_ref[:, side] = s_ref[h, :, 128:192, 0:512].reshape(256, 512).astype(f32)
    key_ref[...] = s_ref[0, :, 64:128, 0:512].reshape(256, 512).astype(f32)
    value_ref[...] = s_ref[1, :, 64:128, 0:512].reshape(256, 512).astype(f32)


def results(summed):
    return local_call(
        results_kernel,
        [((1024, 1024), f32), ((1024, 512), f32), ((1024, 512), f32), ((1024, 1024), f32)],
        "results",
        grid=(4,),
        in_specs=[spec((2, 4, 192, 640), lambda i: (0, i, 0, 0))],
        out_specs=[spec((256, n), lambda i: (i, 0)) for n in (1024, 512, 512, 1024)],
        moved=20 << 20,
    )(summed)


def swapped(x):
    return lax.ppermute(x, "section", [(0, 1), (1, 0)])


def on_device(
    inputs, cotangent, offsets, routes, w_query, w_key, w_value, w_out,
    norm_attn, norm_moe, w_router, w_gate, w_up, w_down,
):
    section = lax.axis_index("section")
    expert = lax.axis_index("expert")
    first = section == 0

    def by_layer(own, other):
        return jnp.where(first, own, other), jnp.where(first, other, own)

    def mine(pair):
        return jnp.where(first, pair[0], pair[1])

    ids = lax.broadcasted_iota(jnp.int32, (1, 1, 1, 32), 3)
    mask_both = jnp.any(routes[0][:, :, :, None] == ids, axis=2).astype(bf16)
    mask_own = mine(mask_both)
    mask_away = jnp.where(first, mask_both[1], mask_both[0])
    start = expert * 64
    left = lax.rem(lax.axis_index("dp"), 2) == 0

    def part(w, there=True):
        if not there:
            return lax.dynamic_slice_in_dim(w, start, 64, axis=0)
        return lax.dynamic_slice(w, (start, jnp.where(left, 0, 512)), (64, 512))

    rows = jnp.concatenate(
        [part(w_query[0]), jnp.where(left, part(w_key[0], False), part(w_value[0], False)), part(w_out[0])],
        axis=0,
    )
    small = jnp.concatenate(
        [part(w_router[0], False), part(norm_attn[0][:, None], False), part(norm_moe[0][:, None], False),
         jnp.zeros((64, 30), bf16)], axis=1)
    extra = jnp.concatenate([mask_away, jnp.zeros((128, 32), bf16)], axis=1)
    extra = jnp.concatenate([extra, small], axis=0)
    extra = jnp.concatenate([extra, jnp.zeros((192, 64), bf16)], axis=1)
    payload = swapped(jnp.concatenate([rows, extra], axis=1))
    mask_other = payload[0:128, 512:544]
    own_rows = jnp.concatenate([mask_own, jnp.zeros((64, 32), bf16)], axis=0)
    payload = jnp.concatenate([payload[:, :576], own_rows, payload[:, 608:]], axis=1)
    shards = jnp.concatenate([w_gate[0], w_up[0], w_down[0]], axis=2)
    weights, away0 = gather_weights(payload, shards[0:1], w_query[0], w_key[0], w_value[0], w_out[0], 3)
    got = jnp.where(
        first,
        jnp.where(left, weights[1, 0, :, :, 512:], weights[1, 1, :, :, 512:]),
        jnp.where(left, weights[0, 0, :, :, 512:], weights[0, 1, :, :, 512:]),
    )
    other_small = got[:, 128:192, 0:64].reshape(1024, 64)
    all_other = got[:, 0:128, 0:32].reshape(2048, 32).T
    all_own = got[:, 0:128, 64:96].reshape(2048, 32).T
    pairs = [
        by_layer(norm_attn.astype(f32), other_small[:, 32][None].astype(f32)),
        by_layer(norm_moe.astype(f32), other_small[:, 33][None].astype(f32)),
        by_layer(w_router[0], other_small[:, :32]),
    ]
    dense = [tuple(p[l] for p in pairs) for l in range(2)]
    masks_own = by_layer(mask_own, mask_other)
    masks_all = by_layer(all_own, all_other)
    masks = [(masks_own[l], masks_all[l]) for l in range(2)]

    def over_dp(w):
        return lax.all_gather(w, "dp", axis=1, tiled=True)

    def first_kv(kv):
        kv, expert_w[0][0], expert_w[1][0] = lax.optimization_barrier((kv, expert_w[0][0], expert_w[1][0]))
        expert_w[0][0] = over_dp(expert_w[0][0])
        expert_w[1][0] = over_dp(expert_w[1][0])
        kv_all, away1 = gather_swap(kv, shards[1:2], 8)
        second = by_layer(shards[1:2], away1)
        for l in range(2):
            expert_w[l].append(over_dp(second[l]))
        return kv_all, expert_w[0]

    expert_w = [[w] for w in by_layer(shards[0:1], away0)]

    seq = mine(offsets)
    local = expert * 128 + jnp.arange(128, dtype=jnp.int32)
    steps = jnp.arange(HEAD // 2, dtype=f32) * 2.0 / HEAD
    angles = (local - seq).astype(f32)[:, None] * (rope_base ** (-steps))[None, :]
    cosine = jnp.tile(jnp.cos(angles), (1, 4))
    sine = jnp.tile(jnp.sin(angles), (1, 4))
    pick_rows = (
        lax.broadcasted_iota(jnp.int32, (8, 32), 1)
        == 2 * expert + lax.broadcasted_iota(jnp.int32, (8, 32), 0)
    ).astype(f32)
    place = (cosine, sine, seq[:, None], local[:, None], pick_rows.T, pick_rows)

    x0 = mine(inputs)
    out0, _, saved0 = forward(x0, 0, place, weights, dense[0], first_kv, masks[0])
    out1, _, saved1 = forward(out0, 1, place, weights, dense[1], expert_w[1], masks[1])
    cot = mine(cotangent)
    later, _ = lax.optimization_barrier((cot, saved0[4]))
    cot_all = gather_rows(later, 1)
    dx1, eg1, dg1, small1 = backward(cot, cot_all, saved1, 1, place, weights, dense[1], expert_w[1], masks[1])
    dx1_all, eg1 = lax.optimization_barrier((gather_rows(dx1, 1), eg1))
    dx0, eg0, dg0, small0 = backward(dx1, dx1_all, saved0, 0, place, weights, dense[0], expert_w[0], masks[0])
    eg_sent = jnp.where(first, eg1, eg0)
    both_small = jnp.stack([small0, small1])
    dense_sum, eg_away = scatter_sum(dense_grads(dg0, dg1, both_small), 4, eg_sent)

    def in_place(l0, l1):
        got = swapped(jnp.where(first, l1, l0))
        own = jnp.where(first, l0, l1)
        return jnp.stack([jnp.where(first, own, got), jnp.where(first, got, own)])[None]

    acts = in_place(out0, out1)
    in_grads = in_place(dx0, dx1)

    tail = dense_sum[:, 1024:]
    full0 = jnp.concatenate([dense_sum[:, :512], tail], axis=1)
    full1 = dense_sum[:, 512:]
    own = jnp.where(first, full0, full1)
    other = jnp.where(first, full1, full0).astype(bf16)
    summed = gather_split(cross_sum(own, other, 6), 7)
    grad_query, grad_key, grad_value, grad_out = results(summed)
    grad_small = mine(summed[:, ::2, 0:64, 512:640]).transpose(1, 0, 2).reshape(64, 1024).astype(f32)
    eg = jnp.where(first, eg0, eg1).astype(f32) + eg_away.astype(f32)
    return (
        acts,
        in_grads,
        grad_query[None],
        grad_key[None],
        grad_value[None],
        grad_out[None],
        grad_small[32:33],
        grad_small[33:34],
        grad_small[:32].T[None],
        eg[None, :, :, 0:512],
        eg[None, :, :, 512:1024],
        eg[None, :, :, 1024:1536],
    )


def solution(mesh):
    token = P(None, ("dp", "expert"), None)
    layer_token = P("section", None, ("dp", "expert"), None)
    matrix = P("section", None, None)
    gain = P("section", None)
    expert = P("section", "expert", "dp", None)
    return jax.shard_map(
        on_device,
        mesh=mesh,
        in_specs=(
            token, token, P(None, ("dp", "expert")), layer_token,
            matrix, matrix, matrix, matrix, gain, gain, matrix, expert, expert, expert,
        ),
        out_specs=(
            layer_token, layer_token, matrix, matrix, matrix, matrix, gain, gain, matrix,
            expert, expert, expert,
        ),
        check_vma=False,
    )
```
